32 devices in a mesh: expert: 8 (over z, x), tensor: 4 (over y, core).
Axes of the slice: x: 2, y: 2, z: 4, core: 2. Of those that a mesh axis runs over, the one named last changes fastest.
Arguments:
- activations: bfloat16 [8192, 1536], P('expert'), may hold values from -6 to 6
- cotangent: bfloat16 [8192, 1536], P('expert'), may hold values from -6 to 6
- block_ids: int32 [8, 1024], P('expert'), may hold values from 0 to 7, never falling along the last dimension, each value on 1 to 256 neighbouring positions
- expert_ids: int32 [8192, 8], P('expert'), may hold values from 0 to 15, as said below
- route_ranks: int32 [8192, 8], P('expert'), may hold values from 0 to 1023, as said below
- attention_gain: bfloat16 [1536], replicated, may hold values from 0.25 to 1.75
- query_weight: bfloat16 [1536, 1536], P(None, 'tensor'), may hold values from -0.15625 to 0.15625
- key_matrix: bfloat16 [1536, 512], P(None, 'tensor'), may hold values from -0.15625 to 0.15625
- value_matrix: bfloat16 [1536, 512], P(None, 'tensor'), may hold values from -0.15625 to 0.15625
- output_weight: bfloat16 [1536, 1536], P('tensor'), may hold values from -1.25 to 1.25
- mixture_gain: bfloat16 [1536], replicated, may hold values from 0.25 to 1.75
- router_weight: bfloat16 [1536, 16], replicated, may hold values from -0.078125 to 0.078125
- expert_gate: bfloat16 [16, 1536, 512], P('expert', None, 'tensor'), may hold values from -0.15625 to 0.15625
- expert_up: bfloat16 [16, 1536, 512], P('expert', None, 'tensor'), may hold values from -0.15625 to 0.15625
- expert_down: bfloat16 [16, 512, 1536], P('expert', 'tensor'), may hold values from -1.5 to 1.5
Outputs:
- output: bfloat16 [8192, 1536], P('expert')
- input_gradient: float32 [8192, 1536], P('expert')
- attention_gain_gradient: float32 [1536], replicated
- query_weight_gradient: float32 [1536, 1536], P(None, 'tensor')
- key_weight_gradient: float32 [1536, 512], P(None, 'tensor')
- value_weight_gradient: float32 [1536, 512], P(None, 'tensor')
- output_weight_gradient: float32 [1536, 1536], P('tensor')
- mixture_gain_gradient: float32 [1536], replicated
- router_weight_gradient: float32 [1536, 16], replicated
- expert_gate_gradient: float32 [16, 1536, 512], P('expert', None, 'tensor')
- expert_up_gradient: float32 [16, 1536, 512], P('expert', None, 'tensor')
- expert_down_gradient: float32 [16, 512, 1536], P('expert', 'tensor')
The draws below stay inside these ranges and needn't reach their ends.
Inputs may be any that keep to these rules, and one draw needn't show every extreme that they name: `expert_ids`: each row names 8 different experts. route_ranks[t, k] is the place of pair (t, k) among the pairs of the same 1024 tokens of one index of the expert axis that name the same expert, in a route order drawn from the seed: for each such index and expert the places are 0, 1, 2, ... without gaps. `block_ids`: each row numbers the blocks of one sequence from 0 upward, never falling; every number occurs, on at most 256 positions.
All inputs are finite; a program needn't handle non-finite values.
Results may differ from the reference program's by a relative error of at most 0.024.
Values may be sent and summed in bfloat16 or wider, within the bound.
No kernel may reach another device: no remote copies, remote signals or barrier semaphores. Data moves between devices by JAX's collectives and lax.ppermute only.
A program may use at most 192 MiB of HBM per device.

```python
import math
import jax
import jax.numpy as jnp
import numpy as np
from jax import lax

MODEL_WIDTH = 1536
QUERY_HEAD_COUNT = 24
KEY_VALUE_HEADS = 8
HEAD_WIDTH = 64
FF = 512
TOP = 8
TOK_DEV = 1024
BLOCK = 256
SEQS = 8
TOKENS = 8192
EXPERTS = 16
N_EXPERT = 8


def route_tables(key):
    base_key = jax.random.fold_in(key, 4242)
    key_popular, key_noise, key_order, key_favored = jax.random.split(base_key, 4)
    popular = jax.random.randint(key_popular, (EXPERTS,), 0, 4) * 12
    favored = jax.random.randint(key_favored, (), 0, EXPERTS)
    popular = popular + jnp.where(jnp.arange(EXPERTS, dtype=jnp.int32) == favored, 1000, 0).astype(jnp.int32)
    noise = jax.random.randint(key_noise, (TOKENS, EXPERTS), 0, 64)
    scores = (noise + popular[None, :]) * EXPERTS + jnp.arange(EXPERTS, dtype=jnp.int32)[None, :]
    top_scores, chosen = lax.top_k(scores, TOP)
    chosen = chosen.astype(jnp.int32)
    pair_total = TOK_DEV * TOP
    chosen_blocks = chosen.reshape(SEQS, pair_total)
    order_keys = jax.random.split(key_order, SEQS)

    def ranks_of(order_key, experts_row):
        priority = jax.random.permutation(order_key, pair_total).astype(jnp.int32)
        sort_key = experts_row * pair_total + priority
        ordering = jnp.argsort(sort_key, stable=True)
        placing = jnp.argsort(ordering, stable=True).astype(jnp.int32)
        counts = jnp.sum((experts_row[:, None] == jnp.arange(EXPERTS, dtype=jnp.int32)[None, :]).astype(jnp.int32), axis=0)
        starts = jnp.cumsum(counts) - counts
        return (placing - starts[experts_row]).astype(jnp.int32)
    ranks = jax.vmap(ranks_of)(order_keys, chosen_blocks)
    return (chosen, ranks.reshape(TOKENS, TOP))


def draw_expert_ids(key, part):
    return route_tables(key)[0]


def draw_route_ranks(key, part):
    return route_tables(key)[1]


def block_scale(own_key, extent, cuts, least, top_value):
    factor_of = 1.0
    for axis_at, shards_of in cuts:
        draws = jax.random.uniform(jax.random.fold_in(jax.random.fold_in(own_key, 6), axis_at), (shards_of,), jnp.float32, least / len(cuts), top_value / len(cuts))
        factor_of = factor_of * jnp.repeat(jnp.exp(draws), extent[axis_at] // shards_of).reshape((-1,) + (1,) * (len(extent) - 1 - axis_at))
    return factor_of


def profile(count, total, reach, lean):
    portions = [(1 << 20) // math.isqrt(rank ** lean) + 1 for rank in range(2, count + 1)]
    rest, given = total - reach - (count - 1), [1] * (count - 1)
    while rest > 0:
        candidates = [i for i in range(count - 1) if given[i] < reach]
        pool, budget = sum([portions[i] for i in candidates]), rest
        for i in candidates:
            more = min(reach - given[i], max(1, budget * portions[i] // pool), rest)
            given[i] = given[i] + more
            rest = rest - more
    return np.array([reach] + given)


def ragged_sizes(key, amount, total, bound, slope):
    if amount == 2:
        one = jax.random.randint(key, (), max(1, total - bound), min(bound, total - 1) + 1)
        return jnp.stack([one, total - one])
    sizes = jnp.asarray(profile(amount, total, bound, slope), jnp.int32)
    twos = (amount - 1) // 2
    donor, receiver = sizes[1:1 + 2 * twos:2], sizes[2:2 + 2 * twos:2]
    room = jnp.minimum(donor - 1, bound - receiver)
    shifted = jax.random.randint(jax.random.fold_in(key, 1), (twos,), 0, 1 << 20) % (room + 1)
    sizes = sizes.at[1:1 + 2 * twos:2].set(donor - shifted).at[2:2 + 2 * twos:2].set(receiver + shifted)
    return sizes[jax.random.permutation(jax.random.fold_in(key, 2), amount)]


def normal_values(own_key, shape, width, reach, shards=(), held_as=jnp.bfloat16):
    loudness = block_scale(own_key, shape, shards, -0.22, 0.18) if shards else 1.0
    values = jax.random.normal(own_key, shape, jnp.float32) * width * loudness
    return jnp.minimum(jnp.maximum(values, -reach), reach).astype(held_as)


def setup_inputs(seed: int = 0) -> dict:
    splits = jax.random.split(jax.random.key(seed), 16)
    return {
        "activations": normal_values(splits[0], (TOKENS, MODEL_WIDTH), 1.0, 6.0, ((0, 8),)),
        "cotangent": normal_values(splits[1], (TOKENS, MODEL_WIDTH), 1.0, 6.0, ((0, 8),)),
        "block_ids": jax.vmap(lambda own: jnp.searchsorted(jnp.cumsum(ragged_sizes(own, 2 * TOK_DEV // BLOCK, TOK_DEV, BLOCK, 1)), jnp.arange(TOK_DEV), side="right"))(jax.random.split(splits[2], SEQS)).reshape((SEQS, TOK_DEV)).astype(jnp.int32),
        "expert_ids": draw_expert_ids(jax.random.fold_in(splits[15], 71), 0),
        "route_ranks": draw_route_ranks(jax.random.fold_in(splits[15], 71), 0),
        "attention_gain": jnp.clip(1.0 + 0.15 * jax.random.normal(splits[5], (MODEL_WIDTH,), jnp.float32), 0.25, 1.75).astype(jnp.bfloat16),
        "query_weight": normal_values(splits[6], (MODEL_WIDTH, QUERY_HEAD_COUNT * HEAD_WIDTH), MODEL_WIDTH ** -0.5, 0.15625, ((1, 4),)),
        "key_matrix": normal_values(splits[7], (MODEL_WIDTH, KEY_VALUE_HEADS * HEAD_WIDTH), MODEL_WIDTH ** -0.5, 0.15625, ((1, 4),)),
        "value_matrix": normal_values(splits[8], (MODEL_WIDTH, KEY_VALUE_HEADS * HEAD_WIDTH), MODEL_WIDTH ** -0.5, 0.15625, ((1, 4),)),
        "output_weight": normal_values(splits[9], (QUERY_HEAD_COUNT * HEAD_WIDTH, MODEL_WIDTH), (QUERY_HEAD_COUNT * HEAD_WIDTH // 64) ** -0.5, 1.25, ((0, 4),)),
        "mixture_gain": jnp.clip(1.0 + 0.15 * jax.random.normal(splits[10], (MODEL_WIDTH,), jnp.float32), 0.25, 1.75).astype(jnp.bfloat16),
        "router_weight": normal_values(splits[11], (MODEL_WIDTH, EXPERTS), (4 * MODEL_WIDTH) ** -0.5, 0.078125),
        "expert_gate": normal_values(splits[12], (EXPERTS, MODEL_WIDTH, FF), MODEL_WIDTH ** -0.5, 0.15625, ((0, 8), (2, 4))),
        "expert_up": normal_values(splits[13], (EXPERTS, MODEL_WIDTH, FF), MODEL_WIDTH ** -0.5, 0.15625, ((0, 8), (2, 4))),
        "expert_down": normal_values(splits[14], (EXPERTS, FF, MODEL_WIDTH), (FF // 32) ** -0.5, 1.5, ((0, 8), (1, 4))),
    }


EPSILON = 1e-05
NEGATIVE = -1e+30
HIGHEST = lax.Precision.HIGHEST

@jax.custom_vjp
def lower_precision(v):
    return lax.optimization_barrier(v.astype(jnp.bfloat16)).astype(jnp.float32)

@jax.custom_vjp
def lower_precision_backward(v):
    return v

def low_keep(v):
    return (lower_precision(v), None)

def low_pass(kept, grad):
    return (grad,)

def back_keep(v):
    return (v, None)

def back_low(kept, grad):
    return (lower_precision(grad),)
lower_precision.defvjp(low_keep, low_pass)
lower_precision_backward.defvjp(back_keep, back_low)

def matrix_multiply(left, right):
    return jnp.dot(left, right, precision=HIGHEST, preferred_element_type=jnp.float32)

def normalize(values, gain_vector):
    return values * lax.rsqrt(lax.optimization_barrier(jnp.mean(values * values, axis=-1, keepdims=True)) + EPSILON) * gain_vector

def rope_tables(sequence_length, head_size):
    half_width = head_size // 2
    frequency = jnp.exp(jnp.arange(half_width, dtype=jnp.float32) * (-2.0 * math.log(10000.0) / head_size))
    angles = jnp.arange(sequence_length, dtype=jnp.float32)[:, None] * frequency[None, :]
    return (jnp.cos(angles), jnp.sin(angles))

def apply_rotation(values, cosine_table, sine_lookup):
    half_width = values.shape[-1] // 2
    first_half = values[..., :half_width]
    second_half = values[..., half_width:]
    cosine_rows = cosine_table[:, None, :]
    sine_rows = sine_lookup[:, None, :]
    return jnp.concatenate([first_half * cosine_rows - second_half * sine_rows, second_half * cosine_rows + first_half * sine_rows], axis=-1)

def sequence_attention(hidden_state_rows, block_row, query_weight, key_matrix, value_matrix):
    sequence_length = hidden_state_rows.shape[0]
    cosine_table, sine_lookup = rope_tables(sequence_length, HEAD_WIDTH)
    query_rows = lower_precision_backward(matrix_multiply(hidden_state_rows, query_weight)).reshape(sequence_length, QUERY_HEAD_COUNT, HEAD_WIDTH)
    keys_unrotated = lower_precision_backward(matrix_multiply(hidden_state_rows, key_matrix)).reshape(sequence_length, KEY_VALUE_HEADS, HEAD_WIDTH)
    values_unprojected = lower_precision_backward(matrix_multiply(hidden_state_rows, value_matrix)).reshape(sequence_length, KEY_VALUE_HEADS, HEAD_WIDTH)
    query_rows = lower_precision(apply_rotation(query_rows, cosine_table, sine_lookup)).reshape(sequence_length, KEY_VALUE_HEADS, QUERY_HEAD_COUNT // KEY_VALUE_HEADS, HEAD_WIDTH)
    keys_rot = lower_precision(apply_rotation(keys_unrotated, cosine_table, sine_lookup))
    values_low = lower_precision(values_unprojected)
    scores = jnp.einsum('qkgd,skd->kgqs', query_rows, keys_rot, precision=HIGHEST) * HEAD_WIDTH ** (-0.5)
    scores = lower_precision_backward(scores)
    visible = block_row[None, :] <= block_row[:, None]
    scores = jnp.where(visible[None, None], scores, NEGATIVE)
    weights = lower_precision(jax.nn.softmax(scores, axis=-1))
    mixture = jnp.einsum('kgqs,skd->qkgd', weights, values_low, precision=HIGHEST)
    return lower_precision_backward(lower_precision(mixture.reshape(sequence_length, QUERY_HEAD_COUNT * HEAD_WIDTH)))

def reference(activations, cotangent, block_ids, expert_ids, route_ranks, attention_gain, query_weight, key_matrix, value_matrix, output_weight, mixture_gain, router_weight, expert_gate, expert_up, expert_down):
    capacity = TOK_DEV * TOP // EXPERTS
    slot_total = EXPERTS * N_EXPERT * capacity
    per_expert = N_EXPERT * capacity
    source = (jnp.arange(TOKENS, dtype=jnp.int32) // TOK_DEV)[:, None]
    kept = route_ranks < capacity
    flat_slots = jnp.where(kept, (expert_ids * N_EXPERT + source) * capacity + route_ranks, slot_total).astype(jnp.int32)
    pair_index = jnp.arange(TOKENS * TOP, dtype=jnp.int32)
    pair_of_slot = jnp.zeros((slot_total + 1,), jnp.int32).at[flat_slots.reshape(-1)].set(pair_index)[:slot_total]
    slot_filled = jnp.zeros((slot_total + 1,), jnp.float32).at[flat_slots.reshape(-1)].set(1.0)[:slot_total]
    token_of_slot = (pair_of_slot // TOP).astype(jnp.int32)

    def forward(inputs_x, gain_first, weight_query, weight_key, weight_value, weight_output, gain_second, weight_router, weight_gate, weight_up, weight_down):
        hidden_first = lower_precision(normalize(inputs_x, gain_first))

        def one_sequence(pieces):
            return sequence_attention(pieces[0], pieces[1], weight_query, weight_key, weight_value)
        mixture = lax.map(jax.checkpoint(one_sequence), (hidden_first.reshape(SEQS, TOK_DEV, MODEL_WIDTH), block_ids))
        attention_out = lower_precision_backward(matrix_multiply(mixture.reshape(TOKENS, QUERY_HEAD_COUNT * HEAD_WIDTH), weight_output))
        residual_mid = inputs_x + attention_out
        hidden_second = lower_precision(normalize(residual_mid, gain_second))
        logits = lower_precision_backward(matrix_multiply(hidden_second, weight_router))
        chosen = jnp.take_along_axis(logits, expert_ids, axis=1)
        gates_low = lower_precision(jax.nn.softmax(chosen, axis=-1))
        gate_of_slot = gates_low.reshape(-1)[pair_of_slot] * slot_filled

        def expert_step(running, pieces):
            tokens_here, gates_here, filled_here, gate_matrix, up_matrix, down_matrix = pieces
            slot_rows = lower_precision_backward(hidden_second[tokens_here] * filled_here[:, None])
            gate_pre = lower_precision_backward(matrix_multiply(slot_rows, gate_matrix))
            up_pre = lower_precision_backward(matrix_multiply(slot_rows, up_matrix))
            activated = lower_precision(jax.nn.silu(gate_pre) * up_pre)
            expert_out = lower_precision_backward(lower_precision(matrix_multiply(activated, down_matrix)))
            return (running.at[tokens_here].add(gates_here[:, None] * expert_out), None)
        pieces_all = (token_of_slot.reshape(EXPERTS, per_expert), gate_of_slot.reshape(EXPERTS, per_expert), slot_filled.reshape(EXPERTS, per_expert), weight_gate, weight_up, weight_down)
        mixed_out, unused = lax.scan(jax.checkpoint(expert_step), jnp.zeros((TOKENS, MODEL_WIDTH), jnp.float32), pieces_all)
        return residual_mid + mixed_out
    floats = (activations.astype(jnp.float32), attention_gain.astype(jnp.float32), query_weight.astype(jnp.float32), key_matrix.astype(jnp.float32), value_matrix.astype(jnp.float32), output_weight.astype(jnp.float32), mixture_gain.astype(jnp.float32), router_weight.astype(jnp.float32), expert_gate.astype(jnp.float32), expert_up.astype(jnp.float32), expert_down.astype(jnp.float32))
    result, pullback = jax.vjp(forward, *floats)
    grads = pullback(cotangent.astype(jnp.float32))
    return (result.astype(jnp.bfloat16), grads[0], grads[1], grads[2], grads[3], grads[4], grads[5], grads[6], grads[7], grads[8], grads[9], grads[10])
```

```python
import functools
import math

import jax
import jax.numpy as jnp
from jax import lax
from jax.experimental import pallas as pl
from jax.experimental.pallas import tpu as pltpu
from jax.sharding import PartitionSpec as P

HEAD_WIDTH = 64
EPSILON = 1e-05
NEGATIVE = -1e30
LANES = 128
LOW = jnp.bfloat16
FULL = jnp.float32
NN = (((1,), (0,)), ((), ()))
NT = (((1,), (1,)), ((), ()))
TN = (((0,), (0,)), ((), ()))


def mul(left, right, dims=NN):
    return lax.dot_general(left, right, dims, preferred_element_type=FULL)


def rope_tables(sequence_length, head_size):
    half_width = head_size // 2
    frequency = jnp.exp(
        jnp.arange(half_width, dtype=FULL) * (-2.0 * math.log(10000.0) / head_size)
    )
    angles = jnp.arange(sequence_length, dtype=FULL)[:, None] * frequency[None, :]
    return (jnp.cos(angles), jnp.sin(angles))


def apply_rotation(values, cosine_table, sine_lookup, sign=1.0):
    half_width = values.shape[-1] // 2
    first_half = values[..., :half_width]
    second_half = values[..., half_width:]
    cosine_rows = cosine_table[:, None, :]
    sine_rows = sine_lookup[:, None, :] * sign
    return jnp.concatenate(
        [
            first_half * cosine_rows - second_half * sine_rows,
            second_half * cosine_rows + first_half * sine_rows,
        ],
        axis=-1,
    )


def block_scores(part_queries, keys_rot, blocks, part_blocks, scale):
    scores = (
        jnp.einsum("qkgd,skd->kgqs", part_queries, keys_rot, preferred_element_type=FULL) * scale
    )
    visible = blocks[None, :] <= part_blocks[:, None]
    return jnp.where(visible, scores, NEGATIVE)


def attention_forward(queries_rot, keys_rot, values_low, blocks, block_rows, scale):
    block_count = queries_rot.shape[0] // block_rows

    def one_block(block_index):
        offset = block_index * block_rows
        part_queries = lax.dynamic_slice_in_dim(queries_rot, offset, block_rows, 0)
        part_blocks = lax.dynamic_slice_in_dim(blocks, offset, block_rows, 0)
        scores = block_scores(part_queries, keys_rot, blocks, part_blocks, scale)
        row_peak = jnp.max(scores, axis=-1, keepdims=True)
        exponent = jnp.exp(scores - row_peak)
        summed = jnp.sum(exponent, axis=-1, keepdims=True)
        weights = (exponent / summed).astype(LOW)
        mixture = jnp.einsum("kgqs,skd->qkgd", weights, values_low, preferred_element_type=FULL)
        return (mixture.astype(LOW), row_peak + jnp.log(summed))

    mixture, log_sums = lax.map(one_block, jnp.arange(block_count, dtype=jnp.int32))
    return (mixture.reshape(queries_rot.shape), log_sums)


def attention_backward(
    queries_rot, keys_rot, values_low, blocks, log_sums, d_mixture, block_rows, scale
):
    block_count = queries_rot.shape[0] // block_rows

    def one_block(running, pieces):
        d_keys, d_values = running
        block_index, log_sum = pieces
        offset = block_index * block_rows
        part_queries = lax.dynamic_slice_in_dim(queries_rot, offset, block_rows, 0)
        part_blocks = lax.dynamic_slice_in_dim(blocks, offset, block_rows, 0)
        part_grads = lax.dynamic_slice_in_dim(d_mixture, offset, block_rows, 0)
        scores = block_scores(part_queries, keys_rot, blocks, part_blocks, scale)
        weights = jnp.exp(scores - log_sum)
        weights_low = weights.astype(LOW)
        d_weights = jnp.einsum("qkgd,skd->kgqs", part_grads, values_low, preferred_element_type=FULL)
        row_delta = jnp.sum(weights * d_weights, axis=-1, keepdims=True)
        d_scores = (weights * (d_weights - row_delta)).astype(LOW)
        d_queries = (
            jnp.einsum("kgqs,skd->qkgd", d_scores, keys_rot, preferred_element_type=FULL) * scale
        )
        d_keys = (
            d_keys
            + jnp.einsum("kgqs,qkgd->skd", d_scores, part_queries, preferred_element_type=FULL)
            * scale
        )
        d_values = d_values + jnp.einsum(
            "kgqs,qkgd->skd", weights_low, part_grads, preferred_element_type=FULL
        )
        return ((d_keys, d_values), d_queries)

    zeros_kv = jnp.zeros(keys_rot.shape, FULL)
    (d_keys, d_values), d_queries = lax.scan(
        one_block, (zeros_kv, zeros_kv), (jnp.arange(block_count, dtype=jnp.int32), log_sums)
    )
    return (d_queries.reshape(queries_rot.shape), d_keys, d_values)


def expert_body(shard_count, local, hidden, row_tile, column_tile, columns_ref, h_ref, g_ref,
                code_ref, router_ref, *rest):
    w_refs = rest[:shard_count]
    y_ref, dh_ref, hid_ref, dgb_ref, first_buffer, second_buffer, arrived, kept_ref = rest[shard_count:]
    wide = local * hidden
    first = 2 * wide
    copies = []
    for s in range(shard_count):
        a = pltpu.make_async_copy(
            w_refs[s].at[pl.ds(0, first)], first_buffer.at[pl.ds(s * first, first)], arrived.at[s, 0]
        )
        b = pltpu.make_async_copy(
            w_refs[s].at[pl.ds(first, wide)], second_buffer.at[pl.ds(s * wide, wide)], arrived.at[s, 1]
        )
        a.start()
        b.start()
        copies.append((a, b))
    rows, width = h_ref.shape
    logits = mul(h_ref[...], router_ref[...])
    code = code_ref[...].astype(FULL)
    picked = code > 0.5
    peak = jnp.max(jnp.where(picked, logits, NEGATIVE), axis=1, keepdims=True)
    exponent = jnp.where(picked, jnp.exp(logits - peak), 0.0)
    gates = exponent / jnp.sum(exponent, axis=1, keepdims=True)
    kept_ref[...] = jnp.where(code > 1.5, gates, 0.0).astype(LOW).astype(FULL)
    dgb_ref[...] = jnp.zeros(dgb_ref.shape, FULL)
    lane = lax.broadcasted_iota(jnp.int32, (row_tile, LANES), 1)
    owner = lax.broadcasted_iota(jnp.int32, (row_tile, wide), 1) // hidden
    for s in range(shard_count):
        copies[s][0].wait()
        copies[s][1].wait()
        place = local * (s // (shard_count // 2))

        @pl.loop(0, rows // row_tile)
        def _(i, s=s, place=place):
            at = pl.ds(pl.multiple_of(i * row_tile, row_tile), row_tile)
            z = mul(h_ref[at, :], first_buffer[s * first : (s + 1) * first, :], NT)
            q = mul(g_ref[at, :], second_buffer[s * wide : (s + 1) * wide, :], NT)
            kept = kept_ref[at, :]
            hits = [lane == columns_ref[place + e] for e in range(local)]
            gate_of = jnp.zeros((row_tile, wide), FULL)
            for e in range(local):
                own = jnp.sum(jnp.where(hits[e], kept, 0.0), axis=1, keepdims=True)
                gate_of = jnp.where(owner == e, own, gate_of)
            gate, up = z[:, :wide], z[:, wide:]
            sigmoid = jax.nn.sigmoid(gate)
            silu = gate * sigmoid
            act = silu * up
            d_act = q * gate_of
            base = s * first
            hid_ref[at, base : base + wide] = (
                d_act * up * sigmoid * (1.0 + gate * (1.0 - sigmoid))
            ).astype(LOW)
            hid_ref[at, base + wide : base + first] = (d_act * silu).astype(LOW)
            base = shard_count * first + s * wide
            hid_ref[at, base : base + wide] = (act * gate_of).astype(LOW)
            product = act * q
            dgb = dgb_ref[at, :]
            for e in range(local):
                part = jnp.sum(jnp.where(owner == e, product, 0.0), axis=1, keepdims=True)
                dgb = dgb + jnp.where(hits[e], part, 0.0)
            dgb_ref[at, :] = dgb

    @pl.loop(0, rows // row_tile)
    def _(i):
        at = pl.ds(pl.multiple_of(i * row_tile, row_tile), row_tile)

        @pl.loop(0, width // column_tile)
        def _(j):
            cut = pl.ds(pl.multiple_of(j * column_tile, column_tile), column_tile)
            middle = shard_count * first
            dh_ref[at, cut] = mul(hid_ref[at, 0:middle], first_buffer[:, cut]).astype(LOW)
            y_ref[at, cut] = mul(hid_ref[at, middle:], second_buffer[:, cut]).astype(LOW)


def run_experts(columns, h, g, code, router, shards_of, local, hidden):
    count = len(shards_of)
    rows, width = h.shape
    depth = shards_of[0].shape[0]
    wide = local * hidden
    whole = pl.BlockSpec(memory_space=pltpu.VMEM)
    row_tile = min(512, rows)
    return pl.pallas_call(
        functools.partial(expert_body, count, local, hidden, row_tile, 256),
        out_shape=(
            jax.ShapeDtypeStruct((rows, width), LOW),
            jax.ShapeDtypeStruct((rows, width), LOW),
            jax.ShapeDtypeStruct((rows, count * depth), LOW),
            jax.ShapeDtypeStruct((rows, LANES), FULL),
        ),
        in_specs=[pl.BlockSpec(memory_space=pltpu.SMEM)]
        + [whole] * 4
        + [pl.BlockSpec(memory_space=pl.ANY)] * count,
        out_specs=(whole,) * 4,
        scratch_shapes=[
            pltpu.VMEM((count * 2 * wide, width), LOW),
            pltpu.VMEM((count * wide, width), LOW),
            pltpu.SemaphoreType.DMA((count, 2)),
            pltpu.VMEM((rows, LANES), FULL),
        ],
        compiler_params=pltpu.CompilerParams(vmem_limit_bytes=50 * 1024 * 1024),
        cost_estimate=pl.CostEstimate(
            flops=rows * width * depth * 4 * count,
            bytes_accessed=count * depth * width * 2 + rows * width * 8 + count * rows * depth * 2,
            transcendentals=0,
        ),
        name="experts",
    )(columns, h, g, code, router, *shards_of)


def swap(values, axis, bit):
    count = lax.axis_size(axis)
    return lax.ppermute(values, axis, [(i, i ^ bit) for i in range(count)])


def pair(values):
    return swap(values, "expert", 1)


def ring(values):
    count = lax.axis_size("expert")
    return lax.ppermute(values, "expert", [(i, (i + 2) % count) for i in range(count)])


def pick(values, index):
    return lax.dynamic_index_in_dim(values, index, 0, keepdims=False)


def ring_gather(block):
    blocks = [block]
    for _ in range(lax.axis_size("expert") // 2 - 1):
        blocks.append(ring(blocks[-1]))
    return blocks


def ring_sum(blocks):
    running = blocks[1 % len(blocks)].astype(FULL)
    for k in range(2, len(blocks) + 1):
        running = ring(running.astype(LOW)).astype(FULL) + blocks[k % len(blocks)].astype(FULL)
    return running


def bits_of(count):
    return [1 << i for i in range(count.bit_length() - 1)]


def tensor_sum(values):
    count = lax.axis_size("tensor")
    here = lax.axis_index("tensor")
    own = values
    for bit in bits_of(count):
        split = own.reshape((own.shape[0] // 2, 2) + own.shape[1:])
        mine = (here // bit) % 2
        send = lax.dynamic_index_in_dim(split, 1 - mine, 1, keepdims=False).astype(LOW)
        keep = lax.dynamic_index_in_dim(split, mine, 1, keepdims=False)
        own = keep.astype(FULL) + swap(send, "tensor", bit).astype(FULL)
    return own[0]


def tensor_gather(values):
    count = lax.axis_size("tensor")
    here = lax.axis_index("tensor")
    own = values[None]
    for bit in reversed(bits_of(count)):
        other = swap(own, "tensor", bit)
        low = (here // bit) % 2 == 0
        own = jnp.stack([jnp.where(low, own, other), jnp.where(low, other, own)], axis=1)
        own = own.reshape((-1,) + values.shape)
    return own.reshape((-1,) + values.shape[1:])


def expert_sum(values):
    size = lax.axis_size("expert") // 2
    here = lax.axis_index("expert")
    place, side = here // 2, here % 2
    n, m = values.shape
    halves = values.reshape(2, n // 2, m)
    half = pick(halves, side) + pair(pick(halves, 1 - side).astype(LOW)).astype(FULL)
    cuts = half.reshape(size, n // 2 // size, m)
    own = ring_sum([pick(cuts, (place - k) % size) for k in range(size)]).astype(LOW)
    gathered = ring_gather(own)
    half = jnp.zeros((size,) + own.shape, LOW)
    for k in range(size):
        half = lax.dynamic_update_index_in_dim(half, gathered[k], (place - k) % size, 0)
    half = half.reshape(n // 2, m)
    other = pair(half)
    low = side == 0
    return jnp.concatenate([jnp.where(low, half, other), jnp.where(low, other, half)]).astype(FULL)


def gather_weights(own):
    cut = own.shape[0] // 2
    near, far = [own], [pair(own)]
    for bit in bits_of(lax.axis_size("tensor"))[1:]:
        for i in range(len(near)):
            near.append(swap(near[i], "tensor", bit))
            far.append(
                jnp.concatenate([pair(near[-1][:cut]), swap(far[i][cut:], "tensor", bit)])
            )
    shards_of = []
    for chip in near + far:
        shards_of += [chip, swap(chip, "tensor", 1)]
    return shards_of


def scatter_weights(parts):
    cut = parts[0].shape[0] // 2
    full = lambda v: v.astype(FULL)
    sums = [
        full(parts[i]) + full(swap(parts[i + 1], "tensor", 1)) for i in range(0, len(parts), 2)
    ]
    near, far = sums[: len(sums) // 2], sums[len(sums) // 2 :]
    for bit in reversed(bits_of(lax.axis_size("tensor"))[1:]):
        count = len(near) // 2
        for i in range(count):
            last_near, last_far = near[count + i], far[count + i]
            moved = full(pair(last_far[:cut].astype(LOW)))
            last_near = jnp.concatenate([last_near[:cut] + moved, last_near[cut:]])
            moved = full(swap(last_far[cut:].astype(LOW), "tensor", bit))
            far[i] = jnp.concatenate([far[i][:cut], far[i][cut:] + moved])
            near[i] = near[i] + full(swap(last_near.astype(LOW), "tensor", bit))
        near, far = near[:count], far[:count]
    return near[0] + full(pair(far[0].astype(LOW)))


def shards(
    activations,
    cotangent,
    block_ids,
    expert_ids,
    route_ranks,
    attention_gain,
    query_weight,
    key_matrix,
    value_matrix,
    output_weight,
    mixture_gain,
    router_weight,
    expert_gate,
    expert_up,
    expert_down,
):
    sequence_length, width = activations.shape
    query_heads = query_weight.shape[1] // HEAD_WIDTH
    group_heads = key_matrix.shape[1] // HEAD_WIDTH
    group_size = query_heads // group_heads
    tensor_count = lax.axis_size("tensor")
    expert_count = lax.axis_size("expert")
    tensor_index = lax.axis_index("tensor")
    expert_index = lax.axis_index("expert")
    num_experts = router_weight.shape[1]
    local, _, hidden = expert_gate.shape
    picks = expert_ids.shape[1]
    capacity = sequence_length * picks // num_experts
    rows = sequence_length // tensor_count
    ring_size = expert_count // 2
    place, side = expert_index // 2, expert_index % 2
    row_offset = tensor_index * rows
    own_rows = lambda v: lax.dynamic_slice_in_dim(v, row_offset, rows, 0)
    block_rows = min(512, sequence_length)
    scale = HEAD_WIDTH ** (-0.5)
    blocks = block_ids[0]
    wide = local * hidden

    packed = jnp.concatenate(
        [
            expert_gate.transpose(0, 2, 1).reshape(wide, width),
            expert_up.transpose(0, 2, 1).reshape(wide, width),
            expert_down.reshape(wide, width),
        ]
    )
    weight_shards = gather_weights(packed)
    cotangent_own = own_rows(cotangent)
    cotangent_blocks = ring_gather(cotangent_own)
    ids_own, ranks_own = own_rows(expert_ids), own_rows(route_ranks)
    expert_range = jnp.arange(LANES, dtype=jnp.int32)
    pair_code = jnp.where(ranks_own < capacity, 2.0, 1.0)
    code = jnp.zeros((rows, LANES), FULL)
    for j in range(picks):
        code = code + jnp.where(
            ids_own[:, j, None] == expert_range[None, :], pair_code[:, j, None], 0.0
        )
    code_blocks = ring_gather(code.astype(LOW))

    cosine_table, sine_lookup = rope_tables(sequence_length, HEAD_WIDTH)
    residual_in = activations.astype(FULL)
    gain_first = attention_gain.astype(FULL)
    inverse_first = lax.rsqrt(jnp.mean(residual_in * residual_in, axis=-1, keepdims=True) + EPSILON)
    hidden_first = (residual_in * inverse_first * gain_first).astype(LOW)
    weight_all = jnp.concatenate([query_weight, key_matrix, value_matrix], axis=1)
    cut_keys = query_heads * HEAD_WIDTH
    cut_values = cut_keys + group_heads * HEAD_WIDTH
    projected = mul(hidden_first, weight_all)
    values_low = (
        projected[:, cut_values:].astype(LOW).reshape(sequence_length, group_heads, HEAD_WIDTH)
    )
    queries_rot = (
        apply_rotation(
            projected[:, :cut_keys].reshape(sequence_length, query_heads, HEAD_WIDTH),
            cosine_table,
            sine_lookup,
        )
        .astype(LOW)
        .reshape(sequence_length, group_heads, group_size, HEAD_WIDTH)
    )
    keys_rot = apply_rotation(
        projected[:, cut_keys:cut_values].reshape(sequence_length, group_heads, HEAD_WIDTH),
        cosine_table,
        sine_lookup,
    ).astype(LOW)
    mixture, log_sums = attention_forward(
        queries_rot, keys_rot, values_low, blocks, block_rows, scale
    )
    mixture_flat = mixture.reshape(sequence_length, query_heads * HEAD_WIDTH)
    partial_out = mul(mixture_flat, output_weight)
    attention_out = tensor_sum(partial_out.reshape(tensor_count, rows, width))

    gain_second = mixture_gain.astype(FULL)
    residual_mid = own_rows(activations).astype(FULL) + attention_out
    inverse_second = lax.rsqrt(
        jnp.mean(residual_mid * residual_mid, axis=-1, keepdims=True) + EPSILON
    )
    normed_second = residual_mid * inverse_second
    hidden_second = (normed_second * gain_second).astype(LOW)
    hidden_blocks = ring_gather(hidden_second)

    router_wide = jnp.pad(router_weight, ((0, 0), (0, LANES - num_experts)))
    columns = jnp.concatenate(
        [
            expert_index * local + jnp.arange(local, dtype=jnp.int32),
            (expert_index ^ 1) * local + jnp.arange(local, dtype=jnp.int32),
        ]
    ).astype(jnp.int32)
    step = max(1, min(512, rows * ring_size) // rows)
    y_parts, dh_parts, dgb_parts, hids = [], [], [], []
    for k in range(0, ring_size, step):
        join = lambda v: v[k] if step == 1 else jnp.concatenate(v[k : k + step])
        y, dh, hid, dgb = run_experts(
            columns,
            join(hidden_blocks),
            join(cotangent_blocks),
            join(code_blocks),
            router_wide,
            weight_shards,
            local,
            hidden,
        )
        hids.append(hid)
        for i in range(step):
            cut = slice(i * rows, (i + 1) * rows)
            y_parts.append(y[cut])
            dh_parts.append(dh[cut])
            dgb_parts.append(dgb[cut, :num_experts])
    dgb_sends = jnp.zeros((ring_size, 2, rows, num_experts), FULL)
    for k in range(ring_size):
        dgb_sends = lax.dynamic_update_slice(
            dgb_sends, dgb_parts[k][None, None], ((place - k) % ring_size, side, 0, 0)
        )
    d_gates = jnp.sum(
        lax.all_to_all(
            dgb_sends.reshape(expert_count, rows, num_experts), "expert", 0, 0, tiled=True
        ),
        axis=0,
    )

    hid = jnp.concatenate(hids)
    h_all = jnp.concatenate(hidden_blocks)
    g_all = jnp.concatenate(cotangent_blocks)
    middle = len(weight_shards) * 2 * wide
    d_first_weights = mul(hid[:, :middle], h_all, TN).astype(LOW)
    d_second_weights = mul(hid[:, middle:], g_all, TN).astype(LOW)

    d_hidden_moe = ring_sum(dh_parts)
    logits = mul(hidden_second, router_weight)
    picked = code[:, :num_experts] > 0.5
    kept = code[:, :num_experts] > 1.5
    gates = jax.nn.softmax(jnp.where(picked, logits, NEGATIVE), axis=-1)
    d_gates = jnp.where(kept, d_gates, 0.0)
    d_logits = (
        gates * (d_gates - jnp.sum(gates * d_gates, axis=-1, keepdims=True))
    ).astype(LOW)
    d_hidden_second = d_hidden_moe + mul(d_logits, router_weight, NT)
    grad_router = mul(hidden_second, d_logits, TN)
    grad_gain_second = jnp.sum(d_hidden_second * normed_second, axis=0)
    scaled = d_hidden_second * gain_second
    d_mid = cotangent_own.astype(FULL) + inverse_second * (
        scaled - normed_second * jnp.mean(scaled * normed_second, axis=-1, keepdims=True)
    )
    d_attention = tensor_gather(d_mid.astype(LOW))
    d_mixture = (
        mul(d_attention, output_weight, NT)
        .astype(LOW)
        .reshape(sequence_length, group_heads, group_size, HEAD_WIDTH)
    )
    d_queries, d_keys, d_values = attention_backward(
        queries_rot, keys_rot, values_low, blocks, log_sums, d_mixture, block_rows, scale
    )
    d_queries_low = (
        apply_rotation(
            d_queries.reshape(sequence_length, query_heads, HEAD_WIDTH),
            cosine_table,
            sine_lookup,
            -1.0,
        )
        .astype(LOW)
        .reshape(sequence_length, query_heads * HEAD_WIDTH)
    )
    d_keys_low = (
        apply_rotation(d_keys, cosine_table, sine_lookup, -1.0)
        .astype(LOW)
        .reshape(sequence_length, group_heads * HEAD_WIDTH)
    )
    d_values_low = d_values.astype(LOW).reshape(sequence_length, group_heads * HEAD_WIDTH)
    d_projected = jnp.concatenate([d_queries_low, d_keys_low, d_values_low], axis=1)
    d_first_part = mul(d_projected, weight_all, NT)
    grad_gain_first = jnp.sum(d_first_part * (residual_in * inverse_first), axis=0)
    d_first = tensor_sum(d_first_part.reshape(tensor_count, rows, width))
    inverse_own = own_rows(inverse_first)
    normed_own = own_rows(activations).astype(FULL) * inverse_own
    scaled = d_first * gain_first
    d_in = d_mid + inverse_own * (
        scaled - normed_own * jnp.mean(scaled * normed_own, axis=-1, keepdims=True)
    )
    input_gradient = tensor_gather(d_in.astype(LOW)).astype(FULL)
    grad_projected = expert_sum(mul(hidden_first, d_projected, TN))
    grad_output = expert_sum(mul(mixture_flat, d_attention, TN))

    output = tensor_gather((residual_mid + ring_sum(y_parts)).astype(LOW))

    shard_count = len(weight_shards)
    grads = scatter_weights(
        [
            jnp.concatenate(
                [
                    d_first_weights[s * 2 * wide : (s + 1) * 2 * wide],
                    d_second_weights[s * wide : (s + 1) * wide],
                ]
            )
            for s in range(shard_count)
        ]
    )
    grad_gate = grads[:wide].reshape(local, hidden, width).transpose(0, 2, 1)
    grad_up = grads[wide : 2 * wide].reshape(local, hidden, width).transpose(0, 2, 1)
    grad_down = grads[2 * wide :].reshape(local, hidden, width)

    small = lax.psum(
        jnp.concatenate(
            [grad_gain_first[None], grad_gain_second[None], grad_router.T], axis=0
        ),
        ("expert", "tensor"),
    )
    return (
        output,
        input_gradient,
        small[0],
        grad_projected[:, :cut_keys],
        grad_projected[:, cut_keys:cut_values],
        grad_projected[:, cut_values:],
        grad_output,
        small[1],
        small[2:].T,
        grad_gate,
        grad_up,
        grad_down,
    )


def solution(mesh):
    in_specs = (
        P("expert", None),
        P("expert", None),
        P("expert", None),
        P("expert", None),
        P("expert", None),
        P(),
        P(None, "tensor"),
        P(None, "tensor"),
        P(None, "tensor"),
        P("tensor", None),
        P(),
        P(),
        P("expert", None, "tensor"),
        P("expert", None, "tensor"),
        P("expert", "tensor", None),
    )
    out_specs = (
        P("expert", None),
        P("expert", None),
        P(),
        P(None, "tensor"),
        P(None, "tensor"),
        P(None, "tensor"),
        P("tensor", None),
        P(),
        P(),
        P("expert", None, "tensor"),
        P("expert", None, "tensor"),
        P("expert", "tensor", None),
    )
    return jax.shard_map(shards, mesh=mesh, in_specs=in_specs, out_specs=out_specs, check_vma=False)
```

```python
import functools
import math

import jax
import jax.numpy as jnp
import numpy as np
from jax import lax
from jax.experimental import pallas as pl
from jax.experimental.pallas import tpu as pltpu
from jax.sharding import PartitionSpec as P

HEAD_WIDTH = 64
EPSILON = 1e-05
NEGATIVE = -1e30
LANES = 128
LOW = jnp.bfloat16
FULL = jnp.float32
NN = (((1,), (0,)), ((), ()))
NT = (((1,), (1,)), ((), ()))
TN = (((0,), (0,)), ((), ()))
BLOCK = 256
EXTRA = 32


def cost_of(flops, size):
    return pl.CostEstimate(flops=flops // 64, bytes_accessed=size // 64, transcendentals=0)


def tie(*values):
    return lax.optimization_barrier(values)


def mul(left, right, dims=NN):
    return lax.dot_general(left, right, dims, preferred_element_type=FULL)


def rope_tables(sequence_length):
    half_width = HEAD_WIDTH // 2
    frequency = np.exp(
        np.arange(half_width, dtype=np.float32) * np.float32(-2.0 * math.log(10000.0) / HEAD_WIDTH)
    )
    angles = np.arange(sequence_length, dtype=np.float32)[:, None] * frequency[None, :]
    cosine, sine = np.cos(angles), np.sin(angles)
    return (
        jnp.asarray(np.concatenate([cosine, cosine], axis=1)),
        jnp.asarray(np.concatenate([-sine, sine], axis=1)),
    )


def normalized(values):
    inverse = lax.rsqrt(jnp.mean(values * values, axis=-1, keepdims=True) + EPSILON)
    return inverse


def swapped(values):
    half = values.shape[1] // 2
    return jnp.concatenate([values[:, half:], values[:, :half]], axis=1)


def tiles_of(length, tile):
    return [(start, min(length, start + tile + BLOCK)) for start in range(0, length, tile)]


def front_body(heads, groups, x_ref, gain_ref, wq_ref, wk_ref, wv_ref, cos_ref, sin_ref,
               h_ref, q_ref, k_ref, v_ref):
    scale = HEAD_WIDTH ** (-0.5)
    x = x_ref[...].astype(FULL)
    h = (x * normalized(x) * gain_ref[...]).astype(LOW)
    h_ref[...] = h
    zq, zk, zv = mul(h, wq_ref[...]), mul(h, wk_ref[...]), mul(h, wv_ref[...])
    cosine, sine = cos_ref[...], sin_ref[...]
    for j in range(heads + groups):
        z, n = (zq, j) if j < heads else (zk, j - heads)
        part = z[:, n * HEAD_WIDTH : (n + 1) * HEAD_WIDTH]
        part = part * cosine + swapped(part) * sine
        if j < heads:
            q_ref[j] = (part.astype(LOW).astype(FULL) * scale).astype(LOW)
        else:
            k_ref[j - heads] = part.astype(LOW)
    for j in range(groups):
        v_ref[j] = zv[:, j * HEAD_WIDTH : (j + 1) * HEAD_WIDTH].astype(LOW)


def run_front(x, gain, weights, cosine, sine, heads, groups):
    length, width = x.shape
    tile = min(256, length)
    shape = jax.ShapeDtypeStruct
    fixed = lambda v: pl.BlockSpec(v.shape, lambda i: (0,) * v.ndim)
    strip = lambda columns: pl.BlockSpec((tile, columns), lambda i: (i, 0))
    of_heads = lambda n: pl.BlockSpec((n, tile, HEAD_WIDTH), lambda i: (0, i, 0))
    return pl.pallas_call(
        functools.partial(front_body, heads, groups),
        grid=(length // tile,),
        out_shape=[
            shape((length, width), LOW),
            shape((heads, length, HEAD_WIDTH), LOW),
            shape((groups, length, HEAD_WIDTH), LOW),
            shape((groups, length, HEAD_WIDTH), LOW),
        ],
        in_specs=[strip(width), fixed(gain)]
        + [fixed(w) for w in weights]
        + [strip(HEAD_WIDTH), strip(HEAD_WIDTH)],
        out_specs=[strip(width), of_heads(heads), of_heads(groups), of_heads(groups)],
        compiler_params=pltpu.CompilerParams(vmem_limit_bytes=32 * 1024 * 1024),
        cost_estimate=cost_of(8 * length * width * width, 12 * length * width),
        name="front",
    )(x, gain, *weights, cosine, sine)


def add_body(count, *refs):
    for i in range(count):
        total = refs[2 * i][...].astype(FULL) + refs[2 * i + 1][...].astype(FULL)
        refs[2 * count + i][...] = total.astype(LOW)


def run_adds(pairs):
    rows, width = pairs[0][0].shape
    tile = rows // 2
    count = len(pairs)
    block = pl.BlockSpec((tile, width), lambda i: (i, 0))
    specs, values = [], []
    for one in pairs:
        offset = one[2] // tile if len(one) > 2 else 0
        specs += [block, pl.BlockSpec((tile, width), lambda i, offset=offset: (i + offset, 0))]
        values += one[:2]
    return list(
        pl.pallas_call(
            functools.partial(add_body, count),
            grid=(rows // tile,),
            out_shape=[jax.ShapeDtypeStruct((rows, width), LOW)] * count,
            in_specs=specs,
            out_specs=[block] * count,
            compiler_params=pltpu.CompilerParams(vmem_limit_bytes=40 * 1024 * 1024),
            cost_estimate=cost_of(1000, 6 * count * rows * width),
            name="adds",
        )(*values)
    )


def attention_body(heads, groups, rows, tile, mine_ref, q_ref, k_ref, v_ref, wo_ref, column_ref,
                   row_ref, mix_ref, lse_ref, *rest):
    part_refs, (turned_ref, out_ref) = rest[:-2], rest[-2:]
    length = row_ref.shape[1]
    size = heads // groups
    for j in range(groups):
        turned_ref[j] = v_ref[j].astype(FULL).T.astype(LOW)

    for group in range(groups):
        for start, keys in tiles_of(length, tile):
            visible = column_ref[0:keys, :] <= row_ref[:, start : start + tile]

            @pl.loop(group * size, (group + 1) * size)
            def _(head, group=group, start=start, keys=keys, visible=visible):
                s = mul(k_ref[group, 0:keys, :], q_ref[head, start : start + tile, :], NT)
                s = jnp.where(visible, s, NEGATIVE)
                peak = jnp.max(s, axis=0, keepdims=True)
                p = jnp.exp(s - peak)
                total = jnp.sum(p, axis=0, keepdims=True)
                lse_ref[head, :, start : start + tile] = peak + jnp.log(total)
                o = mul(turned_ref[group, :, 0:keys], p.astype(LOW)) / total
                out_ref[head, start : start + tile, :] = o.T.astype(LOW)

    for head in range(heads):
        mix_ref[:, head * HEAD_WIDTH : (head + 1) * HEAD_WIDTH] = out_ref[head]
    for r, part_ref in enumerate(part_refs):
        at = pl.ds(pl.multiple_of((mine_ref[0] ^ r) * rows, rows), rows)
        part_ref[...] = mul(mix_ref[at, :], wo_ref[...]).astype(part_ref.dtype)


def run_attention(mine, q, k, v, output_weight, column, row, count):
    heads, length, _ = q.shape
    groups = k.shape[0]
    width = output_weight.shape[1]
    rows = length // count
    whole = pl.BlockSpec(memory_space=pltpu.VMEM)
    shape = jax.ShapeDtypeStruct
    results = pl.pallas_call(
        functools.partial(attention_body, heads, groups, rows, min(256, length)),
        out_shape=[
            shape((length, heads * HEAD_WIDTH), LOW),
            shape((heads, 1, length), FULL),
        ]
        + [shape((rows, width), LOW if r % 2 else FULL) for r in range(count)],
        in_specs=[pl.BlockSpec(memory_space=pltpu.SMEM)] + [whole] * 6,
        out_specs=[whole] * (2 + count),
        scratch_shapes=[
            pltpu.VMEM((groups, HEAD_WIDTH, length), LOW),
            pltpu.VMEM((heads, length, HEAD_WIDTH), LOW),
        ],
        compiler_params=pltpu.CompilerParams(vmem_limit_bytes=40 * 1024 * 1024),
        cost_estimate=cost_of(12 * length * width * width, 12 * length * width),
        name="attention",
    )(mine, q, k, v, output_weight, column, row)
    return results[0], results[1], list(results[2:])


def back_body(count, group, size, rows, tile, mine_ref, *rest):
    da_refs = rest[:count]
    (h_in, wo_ref, mix_ref, q_ref, k_ref, v_ref, lse_ref, column_ref, row_ref, cos_ref, sin_ref,
     d_ref, keep_ref, send_ref, da_ref, h_ref, do_ref, turned_ref, dk_ref, dv_ref, dq_ref,
     square_ref, landed) = rest[count:]
    length = row_ref.shape[1]
    scale = HEAD_WIDTH ** (-0.5)
    first = group * size
    loads = []
    for r in range(count):
        at = pl.ds(pl.multiple_of((mine_ref[0] ^ r) * rows, rows), rows)
        load = pltpu.make_async_copy(da_refs[r], da_ref.at[at], landed.at[r])
        load.start()
        loads.append(load)
    late = pltpu.make_async_copy(h_in, h_ref, landed.at[count])
    late.start()
    for load in loads:
        load.wait()
    turned_ref[...] = k_ref[group].astype(FULL).T.astype(LOW)
    dk_ref[...] = jnp.zeros(dk_ref.shape, FULL)
    dv_ref[...] = jnp.zeros(dv_ref.shape, FULL)
    span = slice(first * HEAD_WIDTH, (first + size) * HEAD_WIDTH)

    @pl.loop(0, length // tile)
    def _(i):
        at = pl.ds(pl.multiple_of(i * tile, tile), tile)
        z = mul(da_ref[at, :], wo_ref[span, :], NT).astype(LOW)
        for j in range(size):
            do_ref[j, at, :] = z[:, j * HEAD_WIDTH : (j + 1) * HEAD_WIDTH]

    for start, keys in tiles_of(length, tile):
        visible = column_ref[0:keys, :] <= row_ref[:, start : start + tile]
        cosine, sine = cos_ref[start : start + tile, :], sin_ref[start : start + tile, :]

        @pl.loop(0, size)
        def _(head, start=start, keys=keys, visible=visible, cosine=cosine, sine=sine):
            q = q_ref[first + head, start : start + tile, :]
            do = do_ref[head, start : start + tile, :]
            s = mul(k_ref[group, 0:keys, :], q, NT)
            p = jnp.where(visible, jnp.exp(s - lse_ref[first + head, :, start : start + tile]), 0.0)
            dp = mul(v_ref[group, 0:keys, :], do, NT)
            delta = jnp.sum(p * dp, axis=0, keepdims=True)
            ds = (p * (dp - delta)).astype(LOW)
            dv_ref[0:keys, :] += mul(p.astype(LOW), do)
            dk_ref[0:keys, :] += mul(ds, q)
            dq = mul(turned_ref[:, 0:keys], ds).T * scale
            dq = dq * cosine - swapped(dq) * sine
            dq_ref[head, start : start + tile, :] = dq.astype(LOW)

    for head in range(size):
        d_ref[:, head * HEAD_WIDTH : (head + 1) * HEAD_WIDTH] = dq_ref[head]
    dk = dk_ref[...]
    dk = dk * cos_ref[...] - swapped(dk) * sin_ref[...]
    d_ref[:, size * HEAD_WIDTH : (size + 1) * HEAD_WIDTH] = dk.astype(LOW)
    d_ref[:, (size + 1) * HEAD_WIDTH :] = dv_ref[...].astype(LOW)
    late.wait()
    depth = (size + 2) * HEAD_WIDTH
    square_ref[0:depth, :] = mul(d_ref[...], h_ref[...], TN)
    square_ref[depth:, :] = mul(mix_ref[:, span], da_ref[...], TN)
    half = keep_ref.shape[0]
    for side in range(2):

        @pl.when(mine_ref[1] == side)
        def _(side=side):
            keep_ref[...] = square_ref[side * half : (side + 1) * half, :]
            send_ref[...] = square_ref[(1 - side) * half : (2 - side) * half, :].astype(LOW)


def run_back(group, mine, da, hidden, output_weight, mixture, q, k, v, lse, column, row, cosine, sine):
    heads, length, _ = q.shape
    groups = k.shape[0]
    size = heads // groups
    rows, width = da[0].shape
    count = len(da)
    half = (size + 1) * HEAD_WIDTH
    whole = pl.BlockSpec(memory_space=pltpu.VMEM)
    shape = jax.ShapeDtypeStruct
    return pl.pallas_call(
        functools.partial(back_body, count, group, size, rows, min(256, length)),
        out_shape=(
            shape((length, (size + 2) * HEAD_WIDTH), LOW),
            shape((half, width), FULL),
            shape((half, width), LOW),
        ),
        in_specs=[pl.BlockSpec(memory_space=pltpu.SMEM)]
        + [pl.BlockSpec(memory_space=pltpu.HBM)] * (count + 1)
        + [whole] * 10,
        out_specs=(whole, whole, whole),
        scratch_shapes=[
            pltpu.VMEM((length, width), LOW),
            pltpu.VMEM((length, width), LOW),
            pltpu.VMEM((size, length, HEAD_WIDTH), LOW),
            pltpu.VMEM((HEAD_WIDTH, length), LOW),
            pltpu.VMEM((length, HEAD_WIDTH), FULL),
            pltpu.VMEM((length, HEAD_WIDTH), FULL),
            pltpu.VMEM((size, length, HEAD_WIDTH), LOW),
            pltpu.VMEM((2 * half, width), FULL),
            pltpu.SemaphoreType.DMA((count + 1,)),
        ],
        compiler_params=pltpu.CompilerParams(vmem_limit_bytes=44 * 1024 * 1024),
        cost_estimate=cost_of(8 * length * width * width, 12 * length * width),
        name="back",
    )(mine, *da, hidden, output_weight, mixture, q, k, v, lse, column, row, cosine, sine)


def place_body(rows, mine_ref, *refs):
    for r, ref in enumerate(refs[:-1]):
        at = pl.ds(pl.multiple_of((mine_ref[0] ^ r) * rows, rows), rows)
        refs[-1][at, :] = ref[...].astype(refs[-1].dtype)


def run_place(mine, blocks, kind):
    rows, width = blocks[0].shape
    whole = pl.BlockSpec(memory_space=pltpu.VMEM)
    return pl.pallas_call(
        functools.partial(place_body, rows),
        out_shape=jax.ShapeDtypeStruct((len(blocks) * rows, width), kind),
        in_specs=[pl.BlockSpec(memory_space=pltpu.SMEM)] + [whole] * len(blocks),
        out_specs=whole,
        compiler_params=pltpu.CompilerParams(vmem_limit_bytes=24 * 1024 * 1024),
        cost_estimate=cost_of(1000, 10 * len(blocks) * rows * width),
        name="place",
    )(mine, *blocks)


def gate_columns(num_experts):
    return -(-3 * num_experts // LANES) * LANES


def expert_body(places, block_count, local, hidden, row_tile, column_tile, num_experts, more,
                columns_ref, router_ref, *rest):
    rest = list(rest)
    take = lambda n: [rest.pop(0) for _ in range(n)]
    shard_count = len(places)
    h_refs, g_refs = take(block_count), take(block_count)
    w_refs = [take(3) for _ in range(shard_count)]
    before = take(3 * block_count) if more else None
    y_outs, dh_outs, sum_outs = take(block_count), take(block_count), take(block_count)
    (hid_out,) = take(1)
    (h_ref, g_ref, hid_ref, first_buffer, second_buffer, code_ref, kept_ref, y_ref, dh_ref,
     sum_ref) = take(10)
    arrived, landed, left = rest
    wide = local * hidden
    first = 2 * wide
    rows = h_refs[0].shape[0]
    total, width = h_ref.shape
    span = [pl.ds(i * rows, rows) for i in range(block_count)]

    def begin(source, target, flag):
        copy = pltpu.make_async_copy(source, target, flag)
        copy.start()
        return copy

    loads, olds = [], []
    for i in range(block_count):
        loads += [
            begin(h_refs[i], h_ref.at[span[i]], landed.at[i, 0]),
            begin(g_refs[i].at[:, pl.ds(0, width)], g_ref.at[span[i]], landed.at[i, 1]),
            begin(g_refs[i].at[:, pl.ds(width, LANES)], code_ref.at[span[i]], landed.at[i, 2]),
        ]
        if more:
            for j, target in enumerate((y_ref, dh_ref, sum_ref)):
                olds.append(
                    begin(before[j * block_count + i], target.at[span[i]], landed.at[i, 3 + j])
                )
    copies = []
    for s in range(shard_count):
        targets = (
            first_buffer.at[pl.ds(s * first, wide)],
            first_buffer.at[pl.ds(s * first + wide, wide)],
            second_buffer.at[pl.ds(s * wide, wide)],
        )
        copies.append([begin(w_refs[s][j], targets[j], arrived.at[s, j]) for j in range(3)])
    for load in loads:
        load.wait()
    code = code_ref[...].astype(FULL)
    logits = mul(h_ref[...], router_ref[...])
    picked = code > 0.5
    peak = jnp.max(jnp.where(picked, logits, NEGATIVE), axis=1, keepdims=True)
    exponent = jnp.where(picked, jnp.exp(logits - peak), 0.0)
    gates = exponent / jnp.sum(exponent, axis=1, keepdims=True)
    kept_ref[...] = jnp.where(code > 1.5, gates, 0.0).astype(LOW).astype(FULL)
    if more:
        for old in olds:
            old.wait()
    else:
        sum_ref[...] = jnp.zeros(sum_ref.shape, FULL)
    lane = lax.broadcasted_iota(jnp.int32, (row_tile, LANES), 1)
    owner = lax.broadcasted_iota(jnp.int32, (row_tile, wide), 1) // hidden
    for s in range(shard_count):
        for copy in copies[s]:
            copy.wait()
        place = local * places[s]

        @pl.loop(0, total // row_tile)
        def _(i, s=s, place=place):
            at = pl.ds(pl.multiple_of(i * row_tile, row_tile), row_tile)
            z = mul(h_ref[at, :], first_buffer[s * first : (s + 1) * first, :], NT)
            q = mul(g_ref[at, :], second_buffer[s * wide : (s + 1) * wide, :], NT)
            kept = kept_ref[at, :]
            hits = [lane == columns_ref[place + e] for e in range(local)]
            gate_of = jnp.zeros((row_tile, wide), FULL)
            for e in range(local):
                own = jnp.sum(jnp.where(hits[e], kept, 0.0), axis=1, keepdims=True)
                gate_of = jnp.where(owner == e, own, gate_of)
            gate, up = z[:, :wide], z[:, wide:]
            sigmoid = jax.nn.sigmoid(gate)
            silu = gate * sigmoid
            act = silu * up
            d_act = q * gate_of
            base = s * first
            hid_ref[at, base : base + wide] = (
                d_act * up * sigmoid * (1.0 + gate * (1.0 - sigmoid))
            ).astype(LOW)
            hid_ref[at, base + wide : base + first] = (d_act * silu).astype(LOW)
            base = shard_count * first + s * wide
            hid_ref[at, base : base + wide] = (act * gate_of).astype(LOW)
            product = act * q
            dgb = sum_ref[at, :]
            for e in range(local):
                part = jnp.sum(jnp.where(owner == e, product, 0.0), axis=1, keepdims=True)
                dgb = dgb + jnp.where(hits[e], part, 0.0)
            sum_ref[at, :] = dgb

    leaves = [begin(hid_ref, hid_out, left.at[0, 0])]
    rest_of = sum_ref[...]
    tiles = [jnp.zeros((total, LANES), FULL)] * (gate_columns(num_experts) // LANES)
    for n in range(3):
        piece = rest_of.astype(LOW).astype(FULL)
        rest_of = rest_of - piece
        tile, turn = divmod(n * num_experts, LANES)
        tiles[tile] = tiles[tile] + (pltpu.roll(piece, turn, 1) if turn else piece)
    for n, tile in enumerate(tiles):
        dh_ref[:, width + n * LANES : width + (n + 1) * LANES] = tile.astype(LOW)
    middle = shard_count * first
    for i in range(block_count):
        at = slice(i * rows, (i + 1) * rows)

        @pl.loop(0, width // column_tile)
        def _(j, i=i, at=at):
            cut = pl.ds(pl.multiple_of(j * column_tile, column_tile), column_tile)
            dh = mul(hid_ref[at, 0:middle], first_buffer[:, cut])
            y = mul(hid_ref[at, middle:], second_buffer[:, cut])
            if more:
                y = y + y_ref[at, cut].astype(FULL)
                dh = dh + dh_ref[at, cut].astype(FULL)
            dh_ref[at, cut] = dh.astype(LOW)
            y_ref[at, cut] = y.astype(LOW)

        leaves += [
            begin(y_ref.at[span[i]], y_outs[i], left.at[1 + i, 0]),
            begin(dh_ref.at[span[i]], dh_outs[i], left.at[1 + i, 1]),
            begin(sum_ref.at[span[i]], sum_outs[i], left.at[1 + i, 2]),
        ]
    for leave in leaves:
        leave.wait()


def run_experts(columns, router, h, g, weights, places, local, hidden, num_experts, before=None):
    count, blocks = len(weights), len(h)
    rows, width = h[0].shape
    wide = local * hidden
    depth = 3 * wide
    total = blocks * rows
    wider = width + gate_columns(num_experts)
    whole = pl.BlockSpec(memory_space=pltpu.VMEM)
    away = pl.BlockSpec(memory_space=pltpu.HBM)
    shape = jax.ShapeDtypeStruct
    extra = [] if before is None else before[0] + before[1] + before[2]
    results = pl.pallas_call(
        functools.partial(
            expert_body, tuple(places), blocks, local, hidden, total // -(-total // 512), 512,
            num_experts, bool(extra),
        ),
        out_shape=[shape((rows, width), LOW)] * blocks
        + [shape((rows, wider), LOW)] * blocks
        + [shape((rows, LANES), FULL)] * blocks
        + [shape((total, count * depth), LOW)],
        in_specs=[pl.BlockSpec(memory_space=pltpu.SMEM), whole]
        + [away] * (2 * blocks + 3 * count + len(extra)),
        out_specs=[away] * (3 * blocks + 1),
        scratch_shapes=[
            pltpu.VMEM((total, width), LOW),
            pltpu.VMEM((total, width), LOW),
            pltpu.VMEM((total, count * depth), LOW),
            pltpu.VMEM((count * 2 * wide, width), LOW),
            pltpu.VMEM((count * wide, width), LOW),
            pltpu.VMEM((total, LANES), LOW),
            pltpu.VMEM((total, LANES), FULL),
            pltpu.VMEM((total, width), LOW),
            pltpu.VMEM((total, wider), LOW),
            pltpu.VMEM((total, LANES), FULL),
            pltpu.SemaphoreType.DMA((count, 3)),
            pltpu.SemaphoreType.DMA((blocks, 6)),
            pltpu.SemaphoreType.DMA((blocks + 1, 3)),
        ],
        compiler_params=pltpu.CompilerParams(
            vmem_limit_bytes=min(56, 16 + total * count * 3 // 500 + count * 3) * 1024 * 1024
        ),
        cost_estimate=cost_of(4 * total * width * depth * count, depth * width * count * 2),
        name="experts",
    )(columns, router, *h, *g, *[piece for shard in weights for piece in shard], *extra)
    return (
        list(results[:blocks]),
        list(results[blocks : 2 * blocks]),
        list(results[2 * blocks : 3 * blocks]),
        results[-1],
    )


def weight_body(plan, rows, wide, *rest):
    rest = list(rest)
    take = lambda n: [rest.pop(0) for _ in range(n)]
    blocks = plan[0][1]
    shards_plan = plan[1]
    h_refs, g_refs = take(blocks), take(blocks)
    hid_refs = take(plan[0][0])
    stay = len(shards_plan) // 2
    out_refs = [take(3) for _ in range(stay)]
    (away_ref,) = take(1)
    h_ref, g_ref, first_ref, second_ref, landed, arrived = rest
    loads = []
    for i in range(blocks):
        at = pl.ds(i * rows, rows)
        sources = (h_refs[i], g_refs[i].at[:, pl.ds(0, h_ref.shape[1])])
        for j, (source, target) in enumerate(zip(sources, (h_ref, g_ref))):
            load = pltpu.make_async_copy(source, target.at[at], landed.at[i, j])
            load.start()
            loads.append(load)

    def fetch(s):
        slot = s % 2
        group = []
        for n, (hid, first, second, start, count) in enumerate(shards_plan[s]):
            at = pl.ds(start, count)
            group.append(
                pltpu.make_async_copy(
                    hid_refs[hid].at[:, pl.ds(first, 2 * wide)],
                    first_ref.at[slot, at],
                    arrived.at[slot, n, 0],
                )
            )
            group.append(
                pltpu.make_async_copy(
                    hid_refs[hid].at[:, pl.ds(second, wide)],
                    second_ref.at[slot, at],
                    arrived.at[slot, n, 1],
                )
            )
        for copy in group:
            copy.start()
        return group

    waiting = fetch(0)
    for load in loads:
        load.wait()
    for s in range(len(shards_plan)):
        following = fetch(s + 1) if s + 1 < len(shards_plan) else None
        for copy in waiting:
            copy.wait()
        slot = s % 2
        sums = (
            lambda: mul(first_ref[slot, :, 0:wide], h_ref[...], TN),
            lambda: mul(first_ref[slot, :, wide:], h_ref[...], TN),
            lambda: mul(second_ref[slot], g_ref[...], TN),
        )
        for j in range(3):
            if s < stay:
                out_refs[s][j][...] = sums[j]().astype(LOW)
            else:
                start = (3 * (s - stay) + j) * wide
                away_ref[start : start + wide, :] = sums[j]().astype(LOW)
        waiting = following


def run_weights(h, g, hids, shards_plan, wide):
    blocks = len(h)
    rows, width = h[0].shape
    total = blocks * rows
    stay = len(shards_plan) // 2
    pieces = max(len(p) for p in shards_plan)
    whole = pl.BlockSpec(memory_space=pltpu.VMEM)
    away = pl.BlockSpec(memory_space=pltpu.HBM)
    plan = ((len(hids), blocks), tuple(tuple(p) for p in shards_plan))
    results = pl.pallas_call(
        functools.partial(weight_body, plan, rows, wide),
        out_shape=[jax.ShapeDtypeStruct((wide, width), LOW)] * (3 * stay)
        + [jax.ShapeDtypeStruct((3 * stay * wide, width), LOW)],
        in_specs=[away] * (2 * blocks + len(hids)),
        out_specs=[whole] * (3 * stay + 1),
        scratch_shapes=[
            pltpu.VMEM((total, width), LOW),
            pltpu.VMEM((total, width), LOW),
            pltpu.VMEM((2, total, 2 * wide), LOW),
            pltpu.VMEM((2, total, wide), LOW),
            pltpu.SemaphoreType.DMA((blocks, 2)),
            pltpu.SemaphoreType.DMA((2, pieces, 2)),
        ],
        compiler_params=pltpu.CompilerParams(vmem_limit_bytes=44 * 1024 * 1024),
        cost_estimate=cost_of(12 * total * width * wide * stay, total * 6 * wide * stay * 2),
        name="weight_gradients",
    )(*h, *g, *hids)
    return list(results[:-1]), results[-1]


def swap(values, axis, bit):
    count = lax.axis_size(axis)
    return lax.ppermute(values, axis, [(i, i ^ bit) for i in range(count)])


def pair(values):
    return swap(values, "expert", 1)


def ring(values):
    count = lax.axis_size("expert")
    return lax.ppermute(values, "expert", [(i, (i + 2) % count) for i in range(count)])


def pick(values, index):
    return lax.dynamic_index_in_dim(values, index, 0, keepdims=False)


def ring_gather(block):
    blocks = [block]
    for _ in range(lax.axis_size("expert") // 2 - 1):
        blocks.append(ring(blocks[-1]))
    return blocks


def ring_sum(blocks, sent=LOW):
    running = blocks[1 % len(blocks)].astype(FULL)
    for k in range(2, len(blocks) + 1):
        running = ring(running.astype(sent)).astype(FULL) + blocks[k % len(blocks)].astype(FULL)
    return running


def bits_of(count):
    return [1 << i for i in range(count.bit_length() - 1)]


def parts_sum(parts):
    parts = list(parts)
    for bit in bits_of(len(parts)):
        for r in reversed(range(0, len(parts), 2 * bit)):
            other = swap(parts[r + bit].astype(LOW), "tensor", bit)
            parts[r] = parts[r].astype(FULL) + other.astype(FULL)
    return parts[0]


def tensor_blocks(own):
    count = lax.axis_size("tensor")
    blocks = [own] * count
    for bit in reversed(bits_of(count)):
        for r in range(0, count, 2 * bit):
            blocks[r + bit] = swap(blocks[r], "tensor", bit)
    return blocks


def sends_z(values):
    size = lax.axis_size("expert") // 2
    place = lax.axis_index("expert") // 2
    n, m = values.shape
    cuts = values.reshape(size, n // size, m)
    return [pick(cuts, place)] + [
        shift(pick(cuts, (place + k) % size).astype(LOW), k) for k in range(1, size)
    ]


def total_of(parts):
    return sum(part.astype(FULL) for part in parts)


def laid_z(blocks):
    size = len(blocks)
    place = lax.axis_index("expert") // 2
    whole = jnp.zeros((size,) + blocks[0].shape, blocks[0].dtype)
    for k, block in enumerate(blocks):
        whole = lax.dynamic_update_index_in_dim(whole, block, (place - k) % size, 0)
    return whole.reshape((-1,) + blocks[0].shape[1:])


def joined(half, other):
    low = lax.axis_index("expert") % 2 == 0
    return jnp.concatenate([jnp.where(low, half, other), jnp.where(low, other, half)])


def sum_everywhere(values):
    for axis in ("tensor", "expert"):
        for bit in bits_of(lax.axis_size(axis)):
            values = values + swap(values, axis, bit)
    return values


def shift(block, steps):
    count = lax.axis_size("expert")
    return lax.ppermute(block, "expert", [(i, (i + 2 * steps) % count) for i in range(count)])


def spread(block):
    return [block] + [shift(block, k) for k in range(1, lax.axis_size("expert") // 2)]


def with_cores(chips):
    shards_of = []
    for chip in chips:
        shards_of += [chip, [swap(piece, "tensor", 1) for piece in chip]]
    return shards_of


def gather_weights(own):
    near, far = [own], [[pair(piece) for piece in own]]
    for bit in bits_of(lax.axis_size("tensor"))[1:]:
        for i in range(len(near)):
            near.append([swap(piece, "tensor", bit) for piece in near[i]])
            far.append(
                [
                    pair(near[-1][0]),
                    swap(far[i][1], "tensor", bit),
                    pair(near[-1][2]),
                ]
            )
    return near, far


def scatter_weights(parts):
    full = lambda v: v.astype(FULL)
    sums = [[full(piece) for piece in chip] for chip in parts]
    near, far = sums[: len(sums) // 2], sums[len(sums) // 2 :]
    for bit in reversed(bits_of(lax.axis_size("tensor"))[1:]):
        count = len(near) // 2
        across = lambda v: full(swap(v.astype(LOW), "tensor", bit))
        beside = lambda v: full(pair(v.astype(LOW)))
        for i in range(count):
            last_near, last_far = near[count + i], far[count + i]
            last_near = [
                last_near[0] + beside(last_far[0]),
                last_near[1],
                last_near[2] + beside(last_far[2]),
            ]
            far[i] = [far[i][0], far[i][1] + across(last_far[1]), far[i][2]]
            near[i] = [one + across(two) for one, two in zip(near[i], last_near)]
        near, far = near[:count], far[:count]
    return [own + full(pair(other.astype(LOW))) for own, other in zip(near[0], far[0])]


def shards(
    activations,
    cotangent,
    block_ids,
    expert_ids,
    route_ranks,
    attention_gain,
    query_weight,
    key_matrix,
    value_matrix,
    output_weight,
    mixture_gain,
    router_weight,
    expert_gate,
    expert_up,
    expert_down,
):
    sequence_length, width = activations.shape
    heads = query_weight.shape[1] // HEAD_WIDTH
    groups = key_matrix.shape[1] // HEAD_WIDTH
    tensor_count = lax.axis_size("tensor")
    expert_count = lax.axis_size("expert")
    tensor_index = lax.axis_index("tensor")
    expert_index = lax.axis_index("expert")
    num_experts = router_weight.shape[1]
    local, _, hidden = expert_gate.shape
    picks = expert_ids.shape[1]
    capacity = sequence_length * picks // num_experts
    rows = sequence_length // tensor_count
    ring_size = expert_count // 2
    row_offset = tensor_index * rows
    own_rows = lambda v: lax.dynamic_slice_in_dim(v, row_offset, rows, 0)
    wide = local * hidden

    down = expert_down.reshape(wide, width)
    gate = expert_gate.transpose(0, 2, 1).reshape(wide, width)
    up = expert_up.transpose(0, 2, 1).reshape(wide, width)
    cotangent_own = own_rows(cotangent)
    ids_own, ranks_own = own_rows(expert_ids), own_rows(route_ranks)
    expert_range = jnp.arange(LANES, dtype=jnp.int32)
    pair_code = jnp.where(ranks_own < capacity, 2.0, 1.0)
    code = jnp.zeros((rows, LANES), FULL)
    for j in range(picks):
        code = code + jnp.where(
            ids_own[:, j, None] == expert_range[None, :], pair_code[:, j, None], 0.0
        )
    cosine, sine = rope_tables(sequence_length)
    gain_first = attention_gain.astype(FULL)[None]
    mine = jnp.stack([tensor_index, expert_index % 2]).astype(jnp.int32)
    row = block_ids
    column = block_ids.reshape(sequence_length, 1)
    fine = tensor_count == 4 and ring_size == 4
    x_in = activations
    across = lambda v: swap(v, "tensor", 2)
    sent = jnp.concatenate([cotangent_own, code.astype(LOW)], axis=1)
    x_own = own_rows(activations)
    core = lambda v: swap(v, "tensor", 1)
    if fine:
        x_in, gate, up, sent, x_own, column = tie(activations, gate, up, sent, x_own, column)
        moved = [pair(down), across(down), ring(sent), core(down), core(gate)]
    hidden_first, q, k, v = run_front(
        x_in, gain_first, (query_weight, key_matrix, value_matrix), cosine, sine, heads, groups
    )
    if fine:
        moved, hidden_first, q, k, v, gate, up = tie(moved, hidden_first, q, k, v, gate, up)
        down_x, down_y, g_1, down_c, gate_c = moved
        moved = [pair(gate), across(gate), ring(g_1), core(down_x), core(up)]
    mixture, lse, parts = run_attention(mine, q, k, v, output_weight, column, row, tensor_count)
    if fine:
        moved, mixture, lse, parts, up = tie(moved, mixture, lse, parts, up)
        gate_x, gate_y, g_2, down_xc, up_c = moved
        parts = tie(parts[0], parts[2], core(parts[3]), core(parts[1]))
        to_send = (parts[1] + parts[2].astype(FULL)).astype(LOW)
        attention_out = parts[0] + parts[3].astype(FULL)
        to_send, attention_out, up, g_2, gate_x, down_y = tie(
            to_send, attention_out, up, g_2, gate_x, down_y
        )
        moved = [across(to_send), pair(up), ring(g_2), core(gate_x), core(down_y)]
        moved, gate_y = tie(moved, gate_y)
        attention_out = attention_out + moved[0].astype(FULL)
        up_x, g_3, gate_xc, down_yc = moved[1:]
        g = [sent, g_1, g_2, g_3]
    else:
        attention_out = parts_sum(parts)

    gain_second = mixture_gain.astype(FULL)
    residual_mid = x_own.astype(FULL) + attention_out
    inverse_second = normalized(residual_mid)
    normed_second = residual_mid * inverse_second
    hidden_second = (normed_second * gain_second).astype(LOW)

    router_wide = jnp.pad(router_weight, ((0, 0), (0, LANES - num_experts)))
    columns = jnp.concatenate(
        [
            expert_index * local + jnp.arange(local, dtype=jnp.int32),
            (expert_index ^ 1) * local + jnp.arange(local, dtype=jnp.int32),
        ]
    ).astype(jnp.int32)
    experts = lambda h, g, weights, places, before=None: run_experts(
        columns, router_wide, h, g, weights, places, local, hidden, num_experts, before
    )
    first = 2 * wide
    low = lambda v: v.astype(LOW)
    full = lambda v: v.astype(FULL)

    def token_gradients(summed_rows):
        d_hidden_moe = summed_rows[:, :width]
        d_gates = sum(
            summed_rows[:, width + n * num_experts : width + (n + 1) * num_experts]
            for n in range(3)
        )
        logits = mul(hidden_second, router_weight)
        picked = code[:, :num_experts] > 0.5
        held = code[:, :num_experts] > 1.5
        gates = jax.nn.softmax(jnp.where(picked, logits, NEGATIVE), axis=-1)
        d_gates = jnp.where(held, d_gates, 0.0)
        d_logits = low(gates * (d_gates - jnp.sum(gates * d_gates, axis=-1, keepdims=True)))
        d_hidden_second = d_hidden_moe + mul(d_logits, router_weight, NT)
        grad_router = mul(hidden_second, d_logits, TN)
        grad_gain_second = jnp.sum(d_hidden_second * normed_second, axis=0)
        scaled = d_hidden_second * gain_second
        d_mid = full(cotangent_own) + inverse_second * (
            scaled - normed_second * jnp.mean(scaled * normed_second, axis=-1, keepdims=True)
        )
        return d_mid, jnp.concatenate([grad_gain_second[None], grad_router.T])

    back = lambda group, da: run_back(
        group, mine, da, hidden_first, output_weight, mixture, q, k, v, lse, column, row, cosine, sine
    )
    size = heads // groups
    cut = size * HEAD_WIDTH
    group_weights = [
        jnp.concatenate(
            [
                query_weight[:, i * cut : (i + 1) * cut],
                key_matrix[:, i * HEAD_WIDTH : (i + 1) * HEAD_WIDTH],
                value_matrix[:, i * HEAD_WIDTH : (i + 1) * HEAD_WIDTH],
            ],
            axis=1,
        )
        for i in range(groups)
    ]

    def first_gradients(d_projected):
        d_first = sum(mul(d, w, NT) for d, w in zip(d_projected, group_weights))
        inverse = normalized(full(activations))
        grad_gain = jnp.sum(d_first * (full(activations) * inverse), axis=0)
        parts = [
            lax.dynamic_slice_in_dim(d_first, (tensor_index ^ r) * rows, rows, 0)
            for r in range(tensor_count)
        ]
        return [low(p) if r % 2 else p for r, p in enumerate(parts)], grad_gain

    def input_rows(d_first, d_mid):
        values = full(x_own)
        inverse = normalized(values)
        normed = values * inverse
        scaled = d_first * gain_first
        return low(
            d_mid
            + inverse * (scaled - normed * jnp.mean(scaled * normed, axis=-1, keepdims=True))
        )

    if fine:
        hidden_second, up_xc, gate_yc = tie(hidden_second, core(up_x), core(gate_y))
        side = [
            [gate, up, down], [gate_c, up_c, down_c],
            [gate_x, up_x, down_x], [gate_xc, up_xc, down_xc],
        ]
        side_places = [0, 0, 1, 1]
        h = [hidden_second]
        moved = [ring(h[0]), across(up), pair(down_y)]
        start = experts(h[:1], g[:1], side, side_places)
        moved, start = tie(moved, start)
        y_0, dh_0, dgb_0, hid_0 = start
        h.append(moved[0])
        up_y, down_far = moved[1:]

        moved = [ring(h[1]), across(gate_x), pair(up_y)]
        up_yc, down_farc = core(up_y), core(down_far)
        y_1, dh_1, dgb_1, hid_1 = experts(h[1:2], g[1:2], side, side_places)
        beside = [[gate_y, up_y, down_y], [gate_yc, up_yc, down_yc]]
        second = experts(
            h[:2], g[:2], beside, [0, 0], (y_0 + y_1, dh_0 + dh_1, dgb_0 + dgb_1)
        )
        moved, second, hid_1, down_farc = tie(moved, second, hid_1, down_farc)
        y_1, dh_1, dgb_1, hid_y = second
        h.append(moved[0])
        gate_far, up_far = moved[1:]

        moved = [ring(h[2])]
        gate_farc, up_farc = core(gate_far), core(up_far)
        y_2, dh_2, dgb_2, hid_2 = experts(h[2:3], g[2:3], side + beside, side_places + [0, 0])
        distant = [[gate_far, up_far, down_far], [gate_farc, up_farc, down_farc]]
        third = experts(
            h[:3], g[:3], distant, [1, 1], (y_1 + y_2, dh_1 + dh_2, dgb_1 + dgb_2)
        )
        moved, third, hid_2, distant = tie(moved, third, hid_2, distant)
        y_parts, dh_parts, dgb_parts, hid_far = third
        h.append(moved[0])

        moved = ring(dh_parts[1])
        last = experts(h[3:], g[3:], side + beside + distant, side_places + [0, 0, 1, 1])
        moved, last = tie(moved, last)
        y, dh, _, hid_last = last
        y_parts, dh_parts = y_parts + y, dh_parts + dh

        (running,) = run_adds([(moved, dh_parts[2])])
        hids = [hid_0, hid_1, hid_y, hid_2, hid_far, hid_last]
        plan = []
        for s in range(8):
            place_of = lambda n, i: (i * first, n * first + i * wide)
            if s < 4:
                head = [(b, *place_of(4, s), b * rows, rows) for b in (0, 1)]
                head.append((3, *place_of(6, s), 2 * rows, rows))
            elif s < 6:
                head = [(2, *place_of(2, s - 4), 0, 2 * rows)]
                head.append((3, *place_of(6, s), 2 * rows, rows))
            else:
                head = [(4, *place_of(2, s - 6), 0, 3 * rows)]
            plan.append(head + [(5, *place_of(8, s), 3 * rows, rows)])
        weights_of = lambda which: run_weights(h, g, hids, [plan[s] for s in which], wide)
        running, hids = tie(running, hids)
        moved = ring(running)
        ready = weights_of([6, 4, 7, 5])
        moved, ready = tie(moved, ready)

        (running,) = run_adds([(moved, dh_parts[3])])
        running, h = tie(running, h)
        moved, others = ring(running), core(ready[1])
        later = weights_of([2, 0, 3, 1])
        moved, later, others = tie(moved, later, others)

        take_all = lambda kept, other, start: run_adds(
            [(piece, other, (start + i) * wide) for i, piece in enumerate(kept)]
        )
        far_sum = take_all(ready[0][:3], others, 0)
        d_mid, small = token_gradients(full(moved) + full(dh_parts[0]))
        d_a = low(d_mid)
        d_a, d_mid, far_sum, y_run, others, later = tie(
            d_a, d_mid, far_sum, y_parts[1], others, later
        )

        moved = [across(d_a), pair(far_sum[0]), ring(y_run), core(d_a), core(later[1])]
        y_sum = take_all(ready[0][3:], others, 3)
        moved, y_sum = tie(moved, y_sum)
        da = [d_a, moved[3], moved[0]]
        later_others = moved[4]
        da_3, y_sum[0], y_run = tie(
            core(da[2]), *run_adds([(y_sum[0], moved[1]), (moved[2], y_parts[2])])
        )
        da.append(da_3)

        moved = [across(far_sum[1]), pair(far_sum[2]), ring(y_run)]
        d_one, keep_one, send_one = back(0, da)
        kept, d_one = tie(later[0], d_one)
        sums = take_all(kept, later_others, 0)
        moved, d_one, keep_one, send_one, sums, da = tie(
            moved, d_one, keep_one, send_one, sums, da
        )
        x_sum, own_sum = sums[:3], sums[3:]
        y_sum[2], x_sum[1], y_run = run_adds(
            [(y_sum[2], moved[1]), (x_sum[1], moved[0]), (moved[2], y_parts[3])]
        )
        y_sum, x_sum, y_run = tie(y_sum, x_sum, y_run)

        moved = [across(y_sum[0]), pair(send_one), ring(y_run)]
        d_two, keep_two, send_two = back(1, da)
        moved, d_two, keep_two, send_two = tie(moved, d_two, keep_two, send_two)
        arrived_y, arrived_x = [moved[0]], []
        summed = moved[2]
        d_parts, grad_gain_first = first_gradients([d_one, d_two])
        half_one = keep_one + full(moved[1])
        extra = jnp.pad(
            jnp.concatenate([small, grad_gain_first[None]]),
            ((0, EXTRA - 2 - num_experts), (0, 0)),
        )
        send_two = jnp.concatenate([send_two, low(extra)])
        d_parts, half_one, extra, send_two = tie(d_parts, half_one, extra, send_two)
        d_others = tie(core(d_parts[3]), core(d_parts[1]))
        to_send = low(d_parts[2] + full(d_others[0]))
        d_first = d_parts[0] + full(d_others[1])

        place = expert_index // 2
        bits = [place % 2, place // 2]
        along = lambda v, bit: swap(v, "expert", 2 << bit)

        def halved(v, bit, more=None):
            parts = v.reshape(2, v.shape[0] // 2, v.shape[1])
            goes = low(pick(parts, 1 - bits[bit]))
            if more is not None:
                goes = jnp.concatenate([goes, low(more)])
            return pick(parts, bits[bit]), goes

        def doubled(v, other, bit):
            front = bits[bit] == 0
            return jnp.concatenate([jnp.where(front, v, other), jnp.where(front, other, v)])

        def apart(keep, came, more):
            n = keep.shape[0]
            return keep + full(came[:n]), more + full(came[n:])

        stay_one, go_one = halved(half_one, 0)
        to_send, d_first, stay_one, go_one = tie(to_send, d_first, stay_one, go_one)

        moved = tie(across(to_send), pair(send_two), along(go_one, 0))
        d_in = input_rows(d_first + full(moved[0]), d_mid)
        half_two, extra = apart(keep_two, moved[1], extra)
        stay_one, go_one = halved(stay_one + full(moved[2]), 1)
        stay_two, go_two = halved(half_two, 0, extra)
        d_in, stay_one, go_one, stay_two, go_two, extra = tie(
            d_in, stay_one, go_one, stay_two, go_two, extra
        )
        moved = [
            across(d_in), core(d_in), along(go_one, 1), along(go_two, 0), pair(x_sum[0]),
        ]
        out_own = low(residual_mid + full(summed) + full(y_parts[0]))
        moved, out_own = tie(moved, out_own)
        input_blocks = [d_in, moved[1], moved[0]]
        arrived_x.append(moved[4])
        one = low(stay_one + full(moved[2]))
        stay_two, extra = apart(stay_two, moved[3], extra)
        stay_two, go_two = halved(stay_two, 1, extra)
        one, stay_two, go_two, extra, input_blocks, arrived_x = tie(
            one, stay_two, go_two, extra, input_blocks, arrived_x
        )
        moved = [
            along(one, 1), along(go_two, 1), pair(x_sum[1]), across(y_sum[2]),
            core(input_blocks[2]),
        ]
        moved = tie(*moved)
        arrived_x.append(moved[2])
        arrived_y.append(moved[3])
        input_blocks.append(moved[4])
        one = doubled(one, moved[0], 1)
        two, extra = apart(stay_two, moved[1], extra)
        two = low(two)
        one, two, extra, input_blocks, arrived_x, arrived_y = tie(
            one, two, extra, input_blocks, arrived_x, arrived_y
        )
        input_gradient = run_place(mine, input_blocks, FULL)
        moved = tie(
            along(one, 0), along(two, 1), pair(x_sum[2]), across(y_sum[1]), core(extra),
            input_gradient,
        )
        input_gradient = moved[5]
        arrived_x.append(moved[2])
        arrived_y.append(moved[3])
        one = doubled(one, moved[0], 0)
        two = doubled(two, moved[1], 1)
        extra = extra + moved[4]
        out_more = jnp.concatenate([out_own, low(extra)])
        one, two, extra, out_more, out_own, arrived_x, arrived_y = tie(
            one, two, extra, out_more, out_own, arrived_x, arrived_y
        )
        grads = [
            total_of([own_sum[0], arrived_y[0], arrived_x[0]]),
            total_of([own_sum[1], arrived_y[2], arrived_x[1]]),
            total_of([own_sum[2], arrived_y[1], arrived_x[2]]),
        ]
        unturned = lambda v: v.reshape(local, hidden, width).transpose(0, 2, 1)
        grad_gate, grad_up, grad_down = unturned(grads[0]), unturned(grads[1]), grads[2]
        moved = tie(pair(one), along(two, 0), across(out_more), core(out_own), grad_gate, grad_up)
        grad_gate, grad_up = moved[4:]
        two = doubled(two, moved[1], 0)
        out_2 = moved[2][:rows]
        sums = extra + full(moved[2][rows:])
        sums = sums[: 2 + num_experts]
        two, out_2 = tie(two, out_2)
        whole_one = joined(one, moved[0])
        output_blocks = [out_own, moved[3], out_2, core(out_2)]
        wholes = [whole_one, joined(two, pair(two))]
    else:
        g = spread(sent)
        h = ring_gather(hidden_second)
        near, far = gather_weights([gate, up, down])
        places = [0] * (2 * len(near)) + [1] * (2 * len(far))
        weights = with_cores(near + far)
        step = max(1, min(ring_size, 1024 // rows))
        y_parts, dh_parts, dgb_parts, hids, plan = [], [], [], [], [[] for _ in weights]
        for i in range(0, ring_size, step):
            at = slice(i, i + step)
            y, dh, dgb, hid = experts(h[at], g[at], weights, places)
            y_parts, dh_parts, dgb_parts = y_parts + y, dh_parts + dh, dgb_parts + dgb
            for s in range(len(weights)):
                base = len(weights) * first + s * wide
                plan[s].append((len(hids), s * first, base, i * rows, step * rows))
            hids.append(hid)
        grad_parts = []
        for i in range(0, len(weights), 4):
            kept, other = run_weights(
                h, g, hids, [plan[i], plan[i + 2], plan[i + 1], plan[i + 3]], wide
            )
            other = core(other)
            sums = run_adds([(piece, other, j * wide) for j, piece in enumerate(kept)])
            grad_parts += [sums[:3], sums[3:]]
        grad_gate, grad_up, grad_down = scatter_weights(grad_parts)
        unturned = lambda v: v.reshape(local, hidden, width).transpose(0, 2, 1)
        grad_gate, grad_up = unturned(grad_gate), unturned(grad_up)
        d_mid, small = token_gradients(ring_sum(dh_parts))
        da = tensor_blocks(low(d_mid))
        backs = [back(i, da) for i in range(groups)]
        d_parts, grad_gain_first = first_gradients([d for d, _, _ in backs])
        d_first = parts_sum(d_parts)
        input_blocks = tensor_blocks(input_rows(d_first, d_mid))
        input_gradient = run_place(mine, input_blocks, FULL)
        output_blocks = tensor_blocks(low(residual_mid + ring_sum(y_parts)))
        wholes = []
        for _, keep, send in backs:
            half = keep + full(pair(send))
            half = laid_z(spread(low(total_of(sends_z(half)))))
            wholes.append(joined(half, pair(half)))
        sums = sum_everywhere(jnp.concatenate([small, grad_gain_first[None]]))

    span = cut + 2 * HEAD_WIDTH
    turned = lambda a, b: full(jnp.concatenate([w[a:b] for w in wholes])).T
    return (
        run_place(mine, output_blocks, LOW),
        input_gradient,
        sums[-1],
        turned(0, cut),
        turned(cut, cut + HEAD_WIDTH),
        turned(cut + HEAD_WIDTH, span),
        full(jnp.concatenate([w[span:] for w in wholes])),
        sums[0],
        sums[1:-1].T,
        grad_gate,
        grad_up,
        grad_down.reshape(local, hidden, width),
    )


def solution(mesh):
    in_specs = (
        P("expert", None),
        P("expert", None),
        P("expert", None),
        P("expert", None),
        P("expert", None),
        P(),
        P(None, "tensor"),
        P(None, "tensor"),
        P(None, "tensor"),
        P("tensor", None),
        P(),
        P(),
        P("expert", None, "tensor"),
        P("expert", None, "tensor"),
        P("expert", "tensor", None),
    )
    out_specs = (
        P("expert", None),
        P("expert", None),
        P(),
        P(None, "tensor"),
        P(None, "tensor"),
        P(None, "tensor"),
        P("tensor", None),
        P(),
        P(),
        P("expert", None, "tensor"),
        P("expert", None, "tensor"),
        P("expert", "tensor", None),
    )
    return jax.shard_map(shards, mesh=mesh, in_specs=in_specs, out_specs=out_specs, check_vma=False)
```

```python
import functools
import math

import jax
import jax.numpy as jnp
import numpy as np
from jax import lax
from jax.experimental import pallas as pl
from jax.experimental.pallas import tpu as pltpu
from jax.sharding import PartitionSpec as P

HEAD_WIDTH = 64
EPSILON = 1e-05
NEGATIVE = -1e30
LANES = 128
LOW = jnp.bfloat16
FULL = jnp.float32
NN = (((1,), (0,)), ((), ()))
NT = (((1,), (1,)), ((), ()))
TN = (((0,), (0,)), ((), ()))
BLOCK = 256
EXTRA = 32
AHEAD = 2
TILE = 512
VMEM_GRANT = 58 * 1024 * 1024


def cost_of(flops, size):
    return pl.CostEstimate(flops=flops // 64, bytes_accessed=size // 64, transcendentals=0)


def tie(*values):
    return lax.optimization_barrier(values)


def mul(left, right, dims=NN):
    return lax.dot_general(left, right, dims, preferred_element_type=FULL)


def rope_tables(sequence_length):
    half_width = HEAD_WIDTH // 2
    frequency = np.exp(
        np.arange(half_width, dtype=np.float32) * np.float32(-2.0 * math.log(10000.0) / HEAD_WIDTH)
    )
    angles = np.arange(sequence_length, dtype=np.float32)[:, None] * frequency[None, :]
    cosine, sine = np.cos(angles), np.sin(angles)
    return (
        jnp.asarray(np.concatenate([cosine, cosine], axis=1)),
        jnp.asarray(np.concatenate([-sine, sine], axis=1)),
    )


def entire(shape):
    return pl.BlockSpec(shape, lambda i: (0,) * len(shape))


def normalized(values):
    inverse = lax.rsqrt(jnp.mean(values * values, axis=-1, keepdims=True) + EPSILON)
    return inverse


def swapped(values):
    half = values.shape[1] // 2
    return jnp.concatenate([values[:, half:], values[:, :half]], axis=1)


def tiles_of(length, tile):
    return [(start, min(length, start + tile + BLOCK)) for start in range(0, length, tile)]


def front_body(heads, groups, x_ref, gain_ref, wq_ref, wk_ref, wv_ref, cos_ref, sin_ref,
               h_ref, q_ref, k_ref, v_ref):
    scale = HEAD_WIDTH ** (-0.5)
    x = x_ref[...].astype(FULL)
    h = (x * normalized(x) * gain_ref[...]).astype(LOW)
    h_ref[...] = h
    zq, zk, zv = mul(h, wq_ref[...]), mul(h, wk_ref[...]), mul(h, wv_ref[...])
    cosine, sine = cos_ref[...], sin_ref[...]
    for j in range(heads + groups):
        z, n = (zq, j) if j < heads else (zk, j - heads)
        part = z[:, n * HEAD_WIDTH : (n + 1) * HEAD_WIDTH]
        part = part * cosine + swapped(part) * sine
        if j < heads:
            q_ref[j] = (part.astype(LOW).astype(FULL) * scale).astype(LOW)
        else:
            k_ref[j - heads] = part.astype(LOW)
    for j in range(groups):
        v_ref[j] = zv[:, j * HEAD_WIDTH : (j + 1) * HEAD_WIDTH].astype(LOW)


def run_front(x, gain, weights, cosine, sine, heads, groups):
    length, width = x.shape
    tile = min(256, length)
    shape = jax.ShapeDtypeStruct
    fixed = lambda v: pl.BlockSpec(v.shape, lambda i: (0,) * v.ndim)
    strip = lambda columns: pl.BlockSpec((tile, columns), lambda i: (i, 0))
    of_heads = lambda n: pl.BlockSpec((n, tile, HEAD_WIDTH), lambda i: (0, i, 0))
    return pl.pallas_call(
        functools.partial(front_body, heads, groups),
        grid=(length // tile,),
        out_shape=[
            shape((length, width), LOW),
            shape((heads, length, HEAD_WIDTH), LOW),
            shape((groups, length, HEAD_WIDTH), LOW),
            shape((groups, length, HEAD_WIDTH), LOW),
        ],
        in_specs=[strip(width), fixed(gain)]
        + [fixed(w) for w in weights]
        + [strip(HEAD_WIDTH), strip(HEAD_WIDTH)],
        out_specs=[strip(width), of_heads(heads), of_heads(groups), of_heads(groups)],
        compiler_params=pltpu.CompilerParams(vmem_limit_bytes=VMEM_GRANT),
        cost_estimate=cost_of(8 * length * width * width, 12 * length * width),
        name="front",
    )(x, gain, *weights, cosine, sine)


def add_body(count, *refs):
    for i in range(count):
        total = refs[2 * i][...].astype(FULL) + refs[2 * i + 1][...].astype(FULL)
        refs[2 * count + i][...] = total.astype(LOW)


def run_adds(pairs):
    rows, width = pairs[0][0].shape
    tile = rows // 2
    count = len(pairs)
    block = pl.BlockSpec((tile, width), lambda i: (i, 0))
    specs, values = [], []
    for one in pairs:
        offset = one[2] // tile if len(one) > 2 else 0
        specs += [block, pl.BlockSpec((tile, width), lambda i, offset=offset: (i + offset, 0))]
        values += one[:2]
    return list(
        pl.pallas_call(
            functools.partial(add_body, count),
            grid=(rows // tile,),
            out_shape=[jax.ShapeDtypeStruct((rows, width), LOW)] * count,
            in_specs=specs,
            out_specs=[block] * count,
            compiler_params=pltpu.CompilerParams(vmem_limit_bytes=VMEM_GRANT),
            cost_estimate=cost_of(1000, 6 * count * rows * width),
            name="adds",
        )(*values)
    )


def attention_body(heads, groups, rows, tile, mine_ref, q_ref, k_ref, v_ref, wo_ref, column_ref,
                   row_ref, mix_ref, lse_ref, *rest):
    part_refs, (turned_ref, out_ref) = rest[:-2], rest[-2:]
    length = row_ref.shape[1]
    size = heads // groups
    for j in range(groups):
        turned_ref[j] = v_ref[j].astype(FULL).T.astype(LOW)

    for group in range(groups):
        for start, keys in tiles_of(length, tile):
            visible = column_ref[0:keys, :] <= row_ref[:, start : start + tile]

            @pl.loop(group * size, (group + 1) * size)
            def _(head, group=group, start=start, keys=keys, visible=visible):
                s = mul(k_ref[group, 0:keys, :], q_ref[head, start : start + tile, :], NT)
                s = jnp.where(visible, s, NEGATIVE)
                peak = jnp.max(s, axis=0, keepdims=True)
                p = jnp.exp(s - peak)
                total = jnp.sum(p, axis=0, keepdims=True)
                lse_ref[head, :, start : start + tile] = peak + jnp.log(total)
                o = mul(turned_ref[group, :, 0:keys], p.astype(LOW)) / total
                out_ref[head, start : start + tile, :] = o.T.astype(LOW)

    for head in range(heads):
        mix_ref[:, head * HEAD_WIDTH : (head + 1) * HEAD_WIDTH] = out_ref[head]
    for r, part_ref in enumerate(part_refs):
        at = pl.ds(pl.multiple_of((mine_ref[0] ^ r) * rows, rows), rows)
        part_ref[...] = mul(mix_ref[at, :], wo_ref[...]).astype(part_ref.dtype)


def run_attention(mine, q, k, v, output_weight, column, row, count):
    heads, length, _ = q.shape
    groups = k.shape[0]
    width = output_weight.shape[1]
    rows = length // count
    shape = jax.ShapeDtypeStruct
    results = pl.pallas_call(
        functools.partial(attention_body, heads, groups, rows, min(2 * TILE, length)),
        grid=(1,),
        out_shape=[
            shape((length, heads * HEAD_WIDTH), LOW),
            shape((heads, 1, length), FULL),
        ]
        + [shape((rows, width), LOW if r % 2 else FULL) for r in range(count)],
        in_specs=[pl.BlockSpec(memory_space=pltpu.SMEM)]
        + [entire(v.shape) for v in (q, k, v, output_weight, column, row)],
        out_specs=[entire((length, heads * HEAD_WIDTH)), entire((heads, 1, length))]
        + [entire((rows, width))] * count,
        scratch_shapes=[
            pltpu.VMEM((groups, HEAD_WIDTH, length), LOW),
            pltpu.VMEM((heads, length, HEAD_WIDTH), LOW),
        ],
        compiler_params=pltpu.CompilerParams(vmem_limit_bytes=VMEM_GRANT),
        cost_estimate=cost_of(12 * length * width * width, 12 * length * width),
        name="attention",
    )(mine, q, k, v, output_weight, column, row)
    return results[0], results[1], list(results[2:])


def back_body(count, group, size, rows, tile, split, mine_ref, *rest):
    da_refs = rest[:count]
    (h_in, wo_ref, mix_ref, q_ref, k_ref, v_ref, lse_ref, column_ref, row_ref, cos_ref, sin_ref,
     d_ref, *outs, da_ref, h_ref, do_ref, turned_ref, dk_ref, dv_ref, dq_ref,
     square_ref, landed) = rest[count:]
    length = row_ref.shape[1]
    scale = HEAD_WIDTH ** (-0.5)
    first = group * size
    loads = []
    for r in range(count):
        at = pl.ds(pl.multiple_of((mine_ref[0] ^ r) * rows, rows), rows)
        load = pltpu.make_async_copy(da_refs[r], da_ref.at[at], landed.at[r])
        load.start()
        loads.append(load)
    late = pltpu.make_async_copy(h_in, h_ref, landed.at[count])
    late.start()
    for load in loads:
        load.wait()
    turned_ref[...] = k_ref[group].astype(FULL).T.astype(LOW)
    dk_ref[...] = jnp.zeros(dk_ref.shape, FULL)
    dv_ref[...] = jnp.zeros(dv_ref.shape, FULL)
    span = slice(first * HEAD_WIDTH, (first + size) * HEAD_WIDTH)

    @pl.loop(0, length // tile)
    def _(i):
        at = pl.ds(pl.multiple_of(i * tile, tile), tile)
        z = mul(da_ref[at, :], wo_ref[span, :], NT).astype(LOW)
        for j in range(size):
            do_ref[j, at, :] = z[:, j * HEAD_WIDTH : (j + 1) * HEAD_WIDTH]

    for start, keys in tiles_of(length, tile):
        visible = column_ref[0:keys, :] <= row_ref[:, start : start + tile]
        cosine, sine = cos_ref[start : start + tile, :], sin_ref[start : start + tile, :]

        @pl.loop(0, size)
        def _(head, start=start, keys=keys, visible=visible, cosine=cosine, sine=sine):
            q = q_ref[first + head, start : start + tile, :]
            do = do_ref[head, start : start + tile, :]
            s = mul(k_ref[group, 0:keys, :], q, NT)
            p = jnp.where(visible, jnp.exp(s - lse_ref[first + head, :, start : start + tile]), 0.0)
            dp = mul(v_ref[group, 0:keys, :], do, NT)
            delta = jnp.sum(p * dp, axis=0, keepdims=True)
            ds = (p * (dp - delta)).astype(LOW)
            dv_ref[0:keys, :] += mul(p.astype(LOW), do)
            dk_ref[0:keys, :] += mul(ds, q)
            dq = mul(turned_ref[:, 0:keys], ds).T * scale
            dq = dq * cosine - swapped(dq) * sine
            dq_ref[head, start : start + tile, :] = dq.astype(LOW)

    for head in range(size):
        d_ref[:, head * HEAD_WIDTH : (head + 1) * HEAD_WIDTH] = dq_ref[head]
    dk = dk_ref[...]
    dk = dk * cos_ref[...] - swapped(dk) * sin_ref[...]
    d_ref[:, size * HEAD_WIDTH : (size + 1) * HEAD_WIDTH] = dk.astype(LOW)
    d_ref[:, (size + 1) * HEAD_WIDTH :] = dv_ref[...].astype(LOW)
    late.wait()
    depth = (size + 2) * HEAD_WIDTH
    square_ref[0:depth, :] = mul(d_ref[...], h_ref[...], TN)
    square_ref[depth:, :] = mul(mix_ref[:, span], da_ref[...], TN)
    if not split:
        outs[0][...] = square_ref[...].astype(LOW)
        return
    keep_ref, send_ref = outs
    half = keep_ref.shape[0]
    for side in range(2):

        @pl.when(mine_ref[1] == side)
        def _(side=side):
            keep_ref[...] = square_ref[side * half : (side + 1) * half, :]
            send_ref[0:half, :] = square_ref[(1 - side) * half : (2 - side) * half, :].astype(LOW)

    send_ref[half:, :] = jnp.zeros((EXTRA, send_ref.shape[1]), LOW)


def run_back(group, split, mine, da, hidden, output_weight, mixture, q, k, v, lse, column, row, cosine, sine):
    heads, length, _ = q.shape
    groups = k.shape[0]
    size = heads // groups
    rows, width = da[0].shape
    count = len(da)
    half = (size + 1) * HEAD_WIDTH
    shape = jax.ShapeDtypeStruct
    return pl.pallas_call(
        functools.partial(back_body, count, group, size, rows, min(TILE, length), split),
        grid=(1,),
        out_shape=[
            shape((length, (size + 2) * HEAD_WIDTH), LOW),
        ]
        + (
            [shape((half, width), FULL), shape((half + EXTRA, width), LOW)]
            if split
            else [shape((2 * half, width), LOW)]
        ),
        in_specs=[pl.BlockSpec(memory_space=pltpu.SMEM)]
        + [pl.BlockSpec(memory_space=pltpu.HBM)] * (count + 1)
        + [
            entire(v.shape)
            for v in (output_weight, mixture, q, k, v, lse, column, row, cosine, sine)
        ],
        out_specs=[entire((length, (size + 2) * HEAD_WIDTH))]
        + (
            [entire((half, width)), entire((half + EXTRA, width))]
            if split
            else [entire((2 * half, width))]
        ),
        scratch_shapes=[
            pltpu.VMEM((length, width), LOW),
            pltpu.VMEM((length, width), LOW),
            pltpu.VMEM((size, length, HEAD_WIDTH), LOW),
            pltpu.VMEM((HEAD_WIDTH, length), LOW),
            pltpu.VMEM((length, HEAD_WIDTH), FULL),
            pltpu.VMEM((length, HEAD_WIDTH), FULL),
            pltpu.VMEM((size, length, HEAD_WIDTH), LOW),
            pltpu.VMEM((2 * half, width), FULL),
            pltpu.SemaphoreType.DMA((count + 1,)),
        ],
        compiler_params=pltpu.CompilerParams(vmem_limit_bytes=VMEM_GRANT),
        cost_estimate=cost_of(8 * length * width * width, 12 * length * width),
        name="back",
    )(mine, *da, hidden, output_weight, mixture, q, k, v, lse, column, row, cosine, sine)


def first_body(groups, count, x_ref, *rest):
    d_refs, w_refs = rest[:groups], rest[groups : 2 * groups]
    out_refs, gain_ref = rest[2 * groups : -1], rest[-1]
    step = pl.program_id(0)
    d_first = mul(d_refs[0][...], w_refs[0][...], NT)
    for d_ref, w_ref in zip(d_refs[1:], w_refs[1:]):
        d_first = d_first + mul(d_ref[...], w_ref[...], NT)
    x = x_ref[...].astype(FULL)
    part = jnp.sum(d_first * (x * normalized(x)), axis=0, keepdims=True)

    @pl.when(step == 0)
    def _():
        gain_ref[...] = part

    @pl.when(step != 0)
    def _():
        gain_ref[...] += part

    for r in range(count):

        @pl.when(step == r)
        def _(r=r):
            out_refs[r][...] = d_first.astype(out_refs[r].dtype)


def run_first(mine, x, d_projected, weights, count):
    length, width = x.shape
    rows = length // count
    groups = len(weights)
    depth = weights[0].shape[1]
    strip = lambda columns: pl.BlockSpec((rows, columns), lambda r, m: (m[0] ^ r, 0))
    fixed = lambda shape: pl.BlockSpec(shape, lambda r, m: (0, 0))
    results = pl.pallas_call(
        lambda m, *refs: first_body(groups, count, *refs),
        grid_spec=pltpu.PrefetchScalarGridSpec(
            num_scalar_prefetch=1,
            grid=(count,),
            in_specs=[strip(width)]
            + [strip(depth)] * groups
            + [fixed((width, depth))] * groups,
            out_specs=[fixed((rows, width))] * count + [fixed((1, width))],
        ),
        out_shape=[
            jax.ShapeDtypeStruct((rows, width), LOW if r % 2 else FULL) for r in range(count)
        ]
        + [jax.ShapeDtypeStruct((1, width), FULL)],
        compiler_params=pltpu.CompilerParams(vmem_limit_bytes=VMEM_GRANT),
        cost_estimate=cost_of(1000, 1000),
        name="first_gradients",
    )(mine, x, *d_projected, *weights)
    return list(results[:-1]), results[-1]


def token_body(num_experts, came_ref, own_ref, h_ref, router_ref, code_ref, mid_ref, gain_ref,
               g_ref, mid_out, low_out, gain_out, router_out):
    width = h_ref.shape[1]
    total = came_ref[...].astype(FULL) + own_ref[...].astype(FULL)
    d_gates = jnp.zeros(code_ref.shape, FULL)
    for n in range(3):
        tile, turn = divmod(n * num_experts, LANES)
        part = total[:, width + tile * LANES : width + (tile + 1) * LANES]
        d_gates = d_gates + (pltpu.roll(part, LANES - turn, 1) if turn else part)
    h = h_ref[...]
    code = code_ref[...]
    logits = mul(h, router_ref[...])
    picked = code > 0.5
    peak = jnp.max(jnp.where(picked, logits, NEGATIVE), axis=1, keepdims=True)
    exponent = jnp.where(picked, jnp.exp(logits - peak), 0.0)
    gates = exponent / jnp.sum(exponent, axis=1, keepdims=True)
    d_gates = jnp.where(code > 1.5, d_gates, 0.0)
    d_logits = gates * (d_gates - jnp.sum(gates * d_gates, axis=1, keepdims=True))
    d_logits = d_logits.astype(LOW)
    d_hidden = total[:, :width] + mul(d_logits, router_ref[...], NT)
    router_out[...] = mul(d_logits, h, TN)[:num_experts]
    mid = mid_ref[...]
    inverse = normalized(mid)
    normed = mid * inverse
    gain_out[...] = jnp.sum(d_hidden * normed, axis=0, keepdims=True)
    scaled = d_hidden * gain_ref[...]
    d_mid = g_ref[...].astype(FULL) + inverse * (
        scaled - normed * jnp.mean(scaled * normed, axis=1, keepdims=True)
    )
    mid_out[...] = d_mid
    low_out[...] = d_mid.astype(LOW)


def run_token(came, own, h, router, code, mid, gain, g, num_experts):
    rows, width = h.shape
    values = (came, own, h, router, code, mid, gain, g)
    shape = jax.ShapeDtypeStruct
    outs = ((rows, width), FULL), ((rows, width), LOW), ((1, width), FULL), ((num_experts, width), FULL)
    return pl.pallas_call(
        functools.partial(token_body, num_experts),
        grid=(1,),
        in_specs=[entire(v.shape) for v in values],
        out_specs=[entire(size) for size, _ in outs],
        out_shape=[shape(size, kind) for size, kind in outs],
        compiler_params=pltpu.CompilerParams(vmem_limit_bytes=VMEM_GRANT),
        cost_estimate=cost_of(1000, 1000),
        name="token_gradients",
    )(*values)


def finish_body(size, groups, split, mine_ref, *refs):
    count = 2 * groups if split else groups
    q_ref, k_ref, v_ref, o_ref = refs[count : count + 4]
    if split:
        half = refs[0].shape[0]
        wholes = refs[count + 4 :]
        for n in range(groups):
            for side in range(2):
                near = slice(side * half, (side + 1) * half)
                other = slice((1 - side) * half, (2 - side) * half)

                @pl.when(mine_ref[1] == side)
                def _(n=n, near=near, other=other):
                    wholes[n][near, :] = refs[2 * n][...]
                    wholes[n][other, :] = refs[2 * n + 1][...]

    else:
        wholes = refs[:groups]
    cut = size * HEAD_WIDTH
    spans = ((q_ref, 0, cut), (k_ref, cut, cut + HEAD_WIDTH), (v_ref, cut + HEAD_WIDTH, cut + 2 * HEAD_WIDTH))
    for ref, start, end in spans:
        ref[...] = jnp.concatenate([w[start:end, :].astype(FULL) for w in wholes]).T
    end = cut + 2 * HEAD_WIDTH
    for i, w in enumerate(wholes):
        o_ref[i * cut : (i + 1) * cut, :] = w[end:, :].astype(FULL)


def run_finish(mine, wholes, size, halves=None):
    values = wholes if halves is None else [v for pair_of in halves for v in pair_of]
    groups = len(wholes if halves is None else halves)
    depth, width = values[0].shape
    tile = 256
    heads = size * groups * HEAD_WIDTH
    down = lambda n: pl.BlockSpec((tile, n), lambda i: (i, 0))
    along = lambda n: pl.BlockSpec((n, tile), lambda i: (0, i))
    shape = jax.ShapeDtypeStruct
    return pl.pallas_call(
        functools.partial(finish_body, size, groups, halves is not None),
        grid=(width // tile,),
        in_specs=[pl.BlockSpec(memory_space=pltpu.SMEM)] + [along(depth)] * len(values),
        out_specs=[down(heads), down(groups * HEAD_WIDTH), down(groups * HEAD_WIDTH), along(heads)],
        out_shape=[
            shape((width, heads), FULL),
            shape((width, groups * HEAD_WIDTH), FULL),
            shape((width, groups * HEAD_WIDTH), FULL),
            shape((heads, width), FULL),
        ],
        scratch_shapes=[]
        if halves is None
        else [pltpu.VMEM((2 * depth, tile), LOW)] * groups,
        compiler_params=pltpu.CompilerParams(vmem_limit_bytes=VMEM_GRANT),
        cost_estimate=cost_of(1000, 1000),
        name="finish",
    )(mine, *values)


def place_body(rows, mine_ref, *refs):
    for r, ref in enumerate(refs[:-1]):
        at = pl.ds(pl.multiple_of((mine_ref[0] ^ r) * rows, rows), rows)
        refs[-1][at, :] = ref[0:rows, :].astype(refs[-1].dtype)


def run_place(mine, blocks, kind):
    rows, width = blocks[0].shape
    whole = pl.BlockSpec(memory_space=pltpu.VMEM)
    return pl.pallas_call(
        functools.partial(place_body, rows),
        out_shape=jax.ShapeDtypeStruct((len(blocks) * rows, width), kind),
        in_specs=[pl.BlockSpec(memory_space=pltpu.SMEM)] + [whole] * len(blocks),
        out_specs=whole,
        compiler_params=pltpu.CompilerParams(vmem_limit_bytes=24 * 1024 * 1024),
        cost_estimate=cost_of(1000, 10 * len(blocks) * rows * width),
        name="place",
    )(mine, *blocks)


def gate_columns(num_experts):
    return -(-3 * num_experts // LANES) * LANES


def expert_body(places, block_count, local, hidden, row_tile, column_tile, num_experts, more,
                columns_ref, router_ref, *rest):
    rest = list(rest)
    take = lambda n: [rest.pop(0) for _ in range(n)]
    shard_count = len(places)
    h_refs, g_refs = take(block_count), take(block_count)
    w_refs = [take(3) for _ in range(shard_count)]
    before = take(3 * block_count) if more else None
    y_outs, dh_outs, sum_outs = take(block_count), take(block_count), take(block_count)
    (hid_out,) = take(1)
    (h_ref, g_ref, hid_ref, first_buffer, second_buffer, code_ref, kept_ref, y_ref, dh_ref,
     sum_ref) = take(10)
    arrived, landed, left = rest
    wide = local * hidden
    first = 2 * wide
    rows = h_refs[0].shape[0]
    total, width = h_ref.shape
    span = [pl.ds(i * rows, rows) for i in range(block_count)]

    def begin(source, target, flag):
        copy = pltpu.make_async_copy(source, target, flag)
        copy.start()
        return copy

    loads, olds = [], []
    for i in range(block_count):
        loads += [
            begin(h_refs[i], h_ref.at[span[i]], landed.at[i, 0]),
            begin(g_refs[i].at[:, pl.ds(0, width)], g_ref.at[span[i]], landed.at[i, 1]),
            begin(g_refs[i].at[:, pl.ds(width, LANES)], code_ref.at[span[i]], landed.at[i, 2]),
        ]
        if more:
            for j, target in enumerate((y_ref, dh_ref, sum_ref)):
                olds.append(
                    begin(before[j * block_count + i], target.at[span[i]], landed.at[i, 3 + j])
                )
    copies = []

    def fetch(s):
        targets = (
            first_buffer.at[pl.ds(s * first, wide)],
            first_buffer.at[pl.ds(s * first + wide, wide)],
            second_buffer.at[pl.ds(s * wide, wide)],
        )
        copies.append([begin(w_refs[s][j], targets[j], arrived.at[s, j]) for j in range(3)])

    for s in range(min(AHEAD, shard_count)):
        fetch(s)
    for load in loads:
        load.wait()
    code = code_ref[...].astype(FULL)
    logits = mul(h_ref[...], router_ref[...])
    picked = code > 0.5
    peak = jnp.max(jnp.where(picked, logits, NEGATIVE), axis=1, keepdims=True)
    exponent = jnp.where(picked, jnp.exp(logits - peak), 0.0)
    gates = exponent / jnp.sum(exponent, axis=1, keepdims=True)
    kept_ref[...] = jnp.where(code > 1.5, gates, 0.0).astype(LOW).astype(FULL)
    if more:
        for old in olds:
            old.wait()
    else:
        sum_ref[...] = jnp.zeros(sum_ref.shape, FULL)
    lane = lax.broadcasted_iota(jnp.int32, (row_tile, LANES), 1)
    owner = lax.broadcasted_iota(jnp.int32, (row_tile, wide), 1) // hidden
    for s in range(shard_count):
        for copy in copies[s]:
            copy.wait()
        if s + AHEAD < shard_count:
            fetch(s + AHEAD)
        place = local * places[s]

        @pl.loop(0, total // row_tile)
        def _(i, s=s, place=place):
            at = pl.ds(pl.multiple_of(i * row_tile, row_tile), row_tile)
            z = mul(h_ref[at, :], first_buffer[s * first : (s + 1) * first, :], NT)
            q = mul(g_ref[at, :], second_buffer[s * wide : (s + 1) * wide, :], NT)
            kept = kept_ref[at, :]
            hits = [lane == columns_ref[place + e] for e in range(local)]
            gate_of = jnp.zeros((row_tile, wide), FULL)
            for e in range(local):
                own = jnp.sum(jnp.where(hits[e], kept, 0.0), axis=1, keepdims=True)
                gate_of = jnp.where(owner == e, own, gate_of)
            gate, up = z[:, :wide], z[:, wide:]
            sigmoid = jax.nn.sigmoid(gate)
            silu = gate * sigmoid
            act = silu * up
            d_act = q * gate_of
            base = s * first
            hid_ref[at, base : base + wide] = (
                d_act * up * sigmoid * (1.0 + gate * (1.0 - sigmoid))
            ).astype(LOW)
            hid_ref[at, base + wide : base + first] = (d_act * silu).astype(LOW)
            base = shard_count * first + s * wide
            hid_ref[at, base : base + wide] = (act * gate_of).astype(LOW)
            product = act * q
            dgb = sum_ref[at, :]
            for e in range(local):
                part = jnp.sum(jnp.where(owner == e, product, 0.0), axis=1, keepdims=True)
                dgb = dgb + jnp.where(hits[e], part, 0.0)
            sum_ref[at, :] = dgb

    leaves = [begin(hid_ref, hid_out, left.at[0, 0])]
    rest_of = sum_ref[...]
    tiles = [jnp.zeros((total, LANES), FULL)] * (gate_columns(num_experts) // LANES)
    for n in range(3):
        piece = rest_of.astype(LOW).astype(FULL)
        rest_of = rest_of - piece
        tile, turn = divmod(n * num_experts, LANES)
        tiles[tile] = tiles[tile] + (pltpu.roll(piece, turn, 1) if turn else piece)
    for n, tile in enumerate(tiles):
        dh_ref[:, width + n * LANES : width + (n + 1) * LANES] = tile.astype(LOW)
    middle = shard_count * first
    for i in range(block_count):
        at = slice(i * rows, (i + 1) * rows)

        @pl.loop(0, width // column_tile)
        def _(j, i=i, at=at):
            cut = pl.ds(pl.multiple_of(j * column_tile, column_tile), column_tile)
            dh = mul(hid_ref[at, 0:middle], first_buffer[:, cut])
            y = mul(hid_ref[at, middle:], second_buffer[:, cut])
            if more:
                y = y + y_ref[at, cut].astype(FULL)
                dh = dh + dh_ref[at, cut].astype(FULL)
            dh_ref[at, cut] = dh.astype(LOW)
            y_ref[at, cut] = y.astype(LOW)

        leaves += [
            begin(y_ref.at[span[i]], y_outs[i], left.at[1 + i, 0]),
            begin(dh_ref.at[span[i]], dh_outs[i], left.at[1 + i, 1]),
            begin(sum_ref.at[span[i]], sum_outs[i], left.at[1 + i, 2]),
        ]
    for leave in leaves:
        leave.wait()


def run_experts(columns, router, h, g, weights, places, local, hidden, num_experts, before=None):
    count, blocks = len(weights), len(h)
    rows, width = h[0].shape
    wide = local * hidden
    depth = 3 * wide
    total = blocks * rows
    wider = width + gate_columns(num_experts)
    whole = pl.BlockSpec(memory_space=pltpu.VMEM)
    away = pl.BlockSpec(memory_space=pltpu.HBM)
    shape = jax.ShapeDtypeStruct
    extra = [] if before is None else before[0] + before[1] + before[2]
    results = pl.pallas_call(
        functools.partial(
            expert_body, tuple(places), blocks, local, hidden, total // -(-total // 512), width,
            num_experts, bool(extra),
        ),
        out_shape=[shape((rows, width), LOW)] * blocks
        + [shape((rows, wider), LOW)] * blocks
        + [shape((rows, LANES), FULL)] * blocks
        + [shape((total, count * depth), LOW)],
        in_specs=[pl.BlockSpec(memory_space=pltpu.SMEM), whole]
        + [away] * (2 * blocks + 3 * count + len(extra)),
        out_specs=[away] * (3 * blocks + 1),
        scratch_shapes=[
            pltpu.VMEM((total, width), LOW),
            pltpu.VMEM((total, width), LOW),
            pltpu.VMEM((total, count * depth), LOW),
            pltpu.VMEM((count * 2 * wide, width), LOW),
            pltpu.VMEM((count * wide, width), LOW),
            pltpu.VMEM((total, LANES), LOW),
            pltpu.VMEM((total, LANES), FULL),
            pltpu.VMEM((total, width), LOW),
            pltpu.VMEM((total, wider), LOW),
            pltpu.VMEM((total, LANES), FULL),
            pltpu.SemaphoreType.DMA((count, 3)),
            pltpu.SemaphoreType.DMA((blocks, 6)),
            pltpu.SemaphoreType.DMA((blocks + 1, 3)),
        ],
        compiler_params=pltpu.CompilerParams(
            vmem_limit_bytes=VMEM_GRANT
        ),
        cost_estimate=cost_of(4 * total * width * depth * count, depth * width * count * 2),
        name="experts",
    )(columns, router, *h, *g, *[piece for shard in weights for piece in shard], *extra)
    return (
        list(results[:blocks]),
        list(results[blocks : 2 * blocks]),
        list(results[2 * blocks : 3 * blocks]),
        results[-1],
    )


def weight_body(plan, rows, wide, *rest):
    rest = list(rest)
    take = lambda n: [rest.pop(0) for _ in range(n)]
    blocks = plan[0][1]
    shards_plan = plan[1]
    h_refs, g_refs = take(blocks), take(blocks)
    hid_refs = take(plan[0][0])
    stay = len(shards_plan) // 2
    out_refs = [take(3) for _ in range(stay)]
    loose = plan[2]
    away_refs = take(3 * loose + stay - loose)
    h_ref, g_ref, first_ref, second_ref, out_buffer, landed, arrived, left = rest
    loads = []
    for i in range(blocks):
        at = pl.ds(i * rows, rows)
        sources = (h_refs[i], g_refs[i].at[:, pl.ds(0, h_ref.shape[1])])
        for j, (source, target) in enumerate(zip(sources, (h_ref, g_ref))):
            load = pltpu.make_async_copy(source, target.at[at], landed.at[i, j])
            load.start()
            loads.append(load)

    def fetch(s):
        slot = s % 2
        group = []
        for n, (hid, first, second, start, count) in enumerate(shards_plan[s]):
            at = pl.ds(start, count)
            group.append(
                pltpu.make_async_copy(
                    hid_refs[hid].at[:, pl.ds(first, 2 * wide)],
                    first_ref.at[slot, at],
                    arrived.at[slot, n, 0],
                )
            )
            group.append(
                pltpu.make_async_copy(
                    hid_refs[hid].at[:, pl.ds(second, wide)],
                    second_ref.at[slot, at],
                    arrived.at[slot, n, 1],
                )
            )
        for copy in group:
            copy.start()
        return group

    waiting = fetch(0)
    leaves = []
    for load in loads:
        load.wait()
    for s in range(len(shards_plan)):
        following = fetch(s + 1) if s + 1 < len(shards_plan) else None
        for copy in waiting:
            copy.wait()
        slot = s % 2
        sums = (
            lambda: mul(first_ref[slot, :, 0:wide], h_ref[...], TN),
            lambda: mul(first_ref[slot, :, wide:], h_ref[...], TN),
            lambda: mul(second_ref[slot], g_ref[...], TN),
        )
        for j in range(3):
            start = 3 * s + j
            out_buffer[start * wide : (start + 1) * wide, :] = sums[j]().astype(LOW)
            if s < stay:
                target = out_refs[s][j]
            elif s - stay < loose:
                target = away_refs[3 * (s - stay) + j]
            else:
                target = away_refs[s - stay + 2 * loose].at[pl.ds(j * wide, wide)]
            leave = pltpu.make_async_copy(
                out_buffer.at[pl.ds(start * wide, wide)], target, left.at[start]
            )
            leave.start()
            leaves.append(leave)
        waiting = following
    for leave in leaves:
        leave.wait()


def run_weights(h, g, hids, shards_plan, wide, loose=0):
    blocks = len(h)
    rows, width = h[0].shape
    total = blocks * rows
    stay = len(shards_plan) // 2
    pieces = max(len(p) for p in shards_plan)
    away = pl.BlockSpec(memory_space=pltpu.HBM)
    plan = ((len(hids), blocks), tuple(tuple(p) for p in shards_plan), loose)
    results = pl.pallas_call(
        functools.partial(weight_body, plan, rows, wide),
        out_shape=[jax.ShapeDtypeStruct((wide, width), LOW)] * (3 * stay)
        + [jax.ShapeDtypeStruct((wide, width), LOW)] * (3 * loose)
        + [jax.ShapeDtypeStruct((3 * wide, width), LOW)] * (stay - loose),
        in_specs=[away] * (2 * blocks + len(hids)),
        out_specs=[away] * (4 * stay + 2 * loose),
        scratch_shapes=[
            pltpu.VMEM((total, width), LOW),
            pltpu.VMEM((total, width), LOW),
            pltpu.VMEM((2, total, 2 * wide), LOW),
            pltpu.VMEM((2, total, wide), LOW),
            pltpu.VMEM((6 * stay * wide, width), LOW),
            pltpu.SemaphoreType.DMA((blocks, 2)),
            pltpu.SemaphoreType.DMA((2, pieces, 2)),
            pltpu.SemaphoreType.DMA((6 * stay,)),
        ],
        compiler_params=pltpu.CompilerParams(vmem_limit_bytes=VMEM_GRANT),
        cost_estimate=cost_of(12 * total * width * wide * stay, total * 6 * wide * stay * 2),
        name="weight_gradients",
    )(*h, *g, *hids)
    chips = []
    for i in range(stay):
        start = 3 * (stay + i)
        other = list(results[start : start + 3]) if i < loose else results[3 * stay + 2 * loose + i]
        chips += [list(results[3 * i : 3 * i + 3]), other]
    return chips


def swap(values, axis, bit):
    count = lax.axis_size(axis)
    return lax.ppermute(values, axis, [(i, i ^ bit) for i in range(count)])


def pair(values):
    return swap(values, "expert", 1)


def ring(values):
    count = lax.axis_size("expert")
    return lax.ppermute(values, "expert", [(i, (i + 2) % count) for i in range(count)])


def pick(values, index):
    return lax.dynamic_index_in_dim(values, index, 0, keepdims=False)


def ring_gather(block):
    blocks = [block]
    for _ in range(lax.axis_size("expert") // 2 - 1):
        blocks.append(ring(blocks[-1]))
    return blocks


def ring_partial(blocks):
    running = blocks[1]
    for k in range(2, len(blocks) + 1):
        running = ring(running.astype(LOW))
        if k < len(blocks):
            running = running.astype(FULL) + blocks[k].astype(FULL)
    return running


def ring_sum(blocks):
    return ring_partial(blocks).astype(FULL) + blocks[0].astype(FULL)


def bits_of(count):
    return [1 << i for i in range(count.bit_length() - 1)]


def parts_sum(parts):
    parts = list(parts)
    for bit in bits_of(len(parts)):
        for r in reversed(range(0, len(parts), 2 * bit)):
            other = swap(parts[r + bit].astype(LOW), "tensor", bit)
            parts[r] = parts[r].astype(FULL) + other.astype(FULL)
    return parts[0]


def tensor_blocks(own):
    count = lax.axis_size("tensor")
    blocks = [own] * count
    for bit in reversed(bits_of(count)):
        for r in range(0, count, 2 * bit):
            blocks[r + bit] = swap(blocks[r], "tensor", bit)
    return blocks


def total_of(parts):
    return sum(part.astype(FULL) for part in parts)


def laid_z(blocks):
    size = len(blocks)
    place = lax.axis_index("expert") // 2
    whole = jnp.zeros((size,) + blocks[0].shape, blocks[0].dtype)
    for k, block in enumerate(blocks):
        whole = lax.dynamic_update_index_in_dim(whole, block, (place - k) % size, 0)
    return whole.reshape((-1,) + blocks[0].shape[1:])


def joined(half, other):
    low = lax.axis_index("expert") % 2 == 0
    return jnp.concatenate([jnp.where(low, half, other), jnp.where(low, other, half)])


def sum_everywhere(values):
    for axis in ("tensor", "expert"):
        for bit in bits_of(lax.axis_size(axis)):
            values = values + swap(values, axis, bit)
    return values


def shift(block, steps):
    count = lax.axis_size("expert")
    return lax.ppermute(block, "expert", [(i, (i + 2 * steps) % count) for i in range(count)])


def spread(block):
    return [block] + [shift(block, k) for k in range(1, lax.axis_size("expert") // 2)]


def with_cores(chips):
    shards_of = []
    for chip in chips:
        shards_of += [chip, [swap(piece, "tensor", 1) for piece in chip]]
    return shards_of


def gather_weights(own):
    near, far = [own], [[pair(piece) for piece in own]]
    for bit in bits_of(lax.axis_size("tensor"))[1:]:
        for i in range(len(near)):
            near.append([swap(piece, "tensor", bit) for piece in near[i]])
            far.append(
                [
                    pair(near[-1][0]),
                    swap(far[i][1], "tensor", bit),
                    pair(near[-1][2]),
                ]
            )
    return near, far


def scatter_weights(parts):
    full = lambda v: v.astype(FULL)
    sums = [[full(piece) for piece in chip] for chip in parts]
    near, far = sums[: len(sums) // 2], sums[len(sums) // 2 :]
    for bit in reversed(bits_of(lax.axis_size("tensor"))[1:]):
        count = len(near) // 2
        across = lambda v: full(swap(v.astype(LOW), "tensor", bit))
        beside = lambda v: full(pair(v.astype(LOW)))
        for i in range(count):
            last_near, last_far = near[count + i], far[count + i]
            last_near = [
                last_near[0] + beside(last_far[0]),
                last_near[1],
                last_near[2] + beside(last_far[2]),
            ]
            far[i] = [far[i][0], far[i][1] + across(last_far[1]), far[i][2]]
            near[i] = [one + across(two) for one, two in zip(near[i], last_near)]
        near, far = near[:count], far[:count]
    return [own + full(pair(other.astype(LOW))) for own, other in zip(near[0], far[0])]


def shards(
    activations,
    cotangent,
    block_ids,
    expert_ids,
    route_ranks,
    attention_gain,
    query_weight,
    key_matrix,
    value_matrix,
    output_weight,
    mixture_gain,
    router_weight,
    expert_gate,
    expert_up,
    expert_down,
):
    sequence_length, width = activations.shape
    heads = query_weight.shape[1] // HEAD_WIDTH
    groups = key_matrix.shape[1] // HEAD_WIDTH
    tensor_count = lax.axis_size("tensor")
    expert_count = lax.axis_size("expert")
    tensor_index = lax.axis_index("tensor")
    expert_index = lax.axis_index("expert")
    num_experts = router_weight.shape[1]
    local, _, hidden = expert_gate.shape
    picks = expert_ids.shape[1]
    capacity = sequence_length * picks // num_experts
    rows = sequence_length // tensor_count
    ring_size = expert_count // 2
    row_offset = tensor_index * rows
    own_rows = lambda v: lax.dynamic_slice_in_dim(v, row_offset, rows, 0)
    wide = local * hidden

    down = expert_down.reshape(wide, width)
    gate = expert_gate.transpose(0, 2, 1).reshape(wide, width)
    up = expert_up.transpose(0, 2, 1).reshape(wide, width)
    cotangent_own = own_rows(cotangent)
    ids_own, ranks_own = own_rows(expert_ids), own_rows(route_ranks)
    expert_range = jnp.arange(LANES, dtype=jnp.int32)
    pair_code = jnp.where(ranks_own < capacity, 2.0, 1.0)
    code = jnp.zeros((rows, LANES), FULL)
    for j in range(picks):
        code = code + jnp.where(
            ids_own[:, j, None] == expert_range[None, :], pair_code[:, j, None], 0.0
        )
    cosine, sine = rope_tables(sequence_length)
    gain_first = attention_gain.astype(FULL)[None]
    mine = jnp.stack([tensor_index, expert_index % 2]).astype(jnp.int32)
    row = block_ids
    column = block_ids.reshape(sequence_length, 1)
    fine = tensor_count == 4 and ring_size == 4
    x_in = activations
    across = lambda v: swap(v, "tensor", 2)
    sent = jnp.concatenate([cotangent_own, code.astype(LOW)], axis=1)
    x_own = own_rows(activations)
    core = lambda v: swap(v, "tensor", 1)
    if fine:
        sent = tie(sent)[0]
        moved = [pair(down), across(down), ring(sent), core(down)]
    hidden_first, q, k, v = run_front(
        x_in, gain_first, (query_weight, key_matrix, value_matrix), cosine, sine, heads, groups
    )
    if fine:
        moved, hidden_first, q, k, v, gate, up, x_own, column = tie(
            moved, hidden_first, q, k, v, gate, up, x_own, column
        )
        down_x, down_y, g_1, down_c = moved
        moved = [pair(gate), across(gate), ring(g_1), core(down_x), core(up)]
    mixture, lse, parts = run_attention(mine, q, k, v, output_weight, column, row, tensor_count)
    if fine:
        moved, mixture, lse, parts, up = tie(moved, mixture, lse, parts, up)
        gate_x, gate_y, g_2, down_xc, up_c = moved
        parts = tie(parts[0], parts[2], core(parts[3]), core(parts[1]))
        to_send = (parts[1] + parts[2].astype(FULL)).astype(LOW)
        attention_out = parts[0] + parts[3].astype(FULL)
        to_send, attention_out, up, g_2, gate_x, down_y, gate = tie(
            to_send, attention_out, up, g_2, gate_x, down_y, gate
        )
        moved = [across(to_send), pair(up), ring(g_2), core(gate_x), core(gate)]
        moved, gate_y, down_y = tie(moved, gate_y, down_y)
        attention_out = attention_out + moved[0].astype(FULL)
        up_x, g_3, gate_xc, gate_c = moved[1:]
        g = [sent, g_1, g_2, g_3]
    else:
        attention_out = parts_sum(parts)

    gain_second = mixture_gain.astype(FULL)
    residual_mid = x_own.astype(FULL) + attention_out
    inverse_second = normalized(residual_mid)
    normed_second = residual_mid * inverse_second
    hidden_second = (normed_second * gain_second).astype(LOW)

    router_wide = jnp.pad(router_weight, ((0, 0), (0, LANES - num_experts)))
    columns = jnp.concatenate(
        [
            expert_index * local + jnp.arange(local, dtype=jnp.int32),
            (expert_index ^ 1) * local + jnp.arange(local, dtype=jnp.int32),
        ]
    ).astype(jnp.int32)
    experts = lambda h, g, weights, places, before=None: run_experts(
        columns, router_wide, h, g, weights, places, local, hidden, num_experts, before
    )
    first = 2 * wide
    low = lambda v: v.astype(LOW)
    full = lambda v: v.astype(FULL)

    def token_gradients(came, own):
        d_mid, d_a, grad_gain, grad_router = run_token(
            came, own, hidden_second, router_wide, code, residual_mid, gain_second[None],
            cotangent_own, num_experts,
        )
        return d_mid, d_a, jnp.concatenate([grad_gain, grad_router])

    back = lambda group, da, split=True: run_back(
        group, split, mine, da, hidden_first, output_weight, mixture, q, k, v, lse, column, row, cosine, sine
    )
    size = heads // groups
    cut = size * HEAD_WIDTH
    group_weights = [
        jnp.concatenate(
            [
                query_weight[:, i * cut : (i + 1) * cut],
                key_matrix[:, i * HEAD_WIDTH : (i + 1) * HEAD_WIDTH],
                value_matrix[:, i * HEAD_WIDTH : (i + 1) * HEAD_WIDTH],
            ],
            axis=1,
        )
        for i in range(groups)
    ]

    first_gradients = lambda d_projected: run_first(
        mine, activations, d_projected, group_weights, tensor_count
    )

    def input_rows(d_first, d_mid):
        values = full(x_own)
        inverse = normalized(values)
        normed = values * inverse
        scaled = d_first * gain_first
        return low(
            d_mid
            + inverse * (scaled - normed * jnp.mean(scaled * normed, axis=-1, keepdims=True))
        )

    if fine:
        h = [hidden_second]
        moved = [ring(h[0]), across(up), pair(down_y)]
        up_xc, gate_yc = core(up_x), core(gate_y)
        side = [
            [gate, up, down], [gate_c, up_c, down_c],
            [gate_x, up_x, down_x], [gate_xc, up_xc, down_xc],
        ]
        side_places = [0, 0, 1, 1]
        start = experts(h[:1], g[:1], side, side_places)
        moved, start, group_weights, gate_yc = tie(moved, start, group_weights, gate_yc)
        y_0, dh_0, dgb_0, hid_0 = start
        h.append(moved[0])
        up_y, down_far = moved[1:]

        moved = [ring(h[1]), across(gate_x), pair(up_y)]
        up_yc, down_yc = core(up_y), core(down_y)
        y_1, dh_1, dgb_1, hid_1 = experts(h[1:2], g[1:2], side, side_places)
        beside = [[gate_y, up_y, down_y], [gate_yc, up_yc, down_yc]]
        second = experts(
            h[:2], g[:2], beside, [0, 0], (y_0 + y_1, dh_0 + dh_1, dgb_0 + dgb_1)
        )
        moved, second, hid_1, down_far = tie(moved, second, hid_1, down_far)
        y_1, dh_1, dgb_1, hid_y = second
        h.append(moved[0])
        gate_far, up_far = moved[1:]

        moved = [ring(h[2])]
        gate_farc, up_farc, down_farc = core(gate_far), core(up_far), core(down_far)
        y_2, dh_2, dgb_2, hid_2 = experts(h[2:3], g[2:3], side + beside, side_places + [0, 0])
        distant = [[gate_far, up_far, down_far], [gate_farc, up_farc, down_farc]]
        third = experts(
            h[:3], g[:3], distant, [1, 1], (y_1 + y_2, dh_1 + dh_2, dgb_1 + dgb_2)
        )
        moved, third, hid_2, distant = tie(moved, third, hid_2, distant)
        y_parts, dh_parts, dgb_parts, hid_far = third
        h.append(moved[0])

        moved = ring(dh_parts[1])
        last = experts(h[3:], g[3:], side + beside + distant, side_places + [0, 0, 1, 1])
        moved, last = tie(moved, last)
        y, dh, _, hid_last = last
        y_parts, dh_parts = y_parts + y, dh_parts + dh

        (running,) = run_adds([(moved, dh_parts[2])])
        hids = [hid_0, hid_1, hid_y, hid_2, hid_far, hid_last]
        plan = []
        for s in range(8):
            place_of = lambda n, i: (i * first, n * first + i * wide)
            if s < 4:
                head = [(b, *place_of(4, s), b * rows, rows) for b in (0, 1)]
                head.append((3, *place_of(6, s), 2 * rows, rows))
            elif s < 6:
                head = [(2, *place_of(2, s - 4), 0, 2 * rows)]
                head.append((3, *place_of(6, s), 2 * rows, rows))
            else:
                head = [(4, *place_of(2, s - 6), 0, 3 * rows)]
            plan.append(head + [(5, *place_of(8, s), 3 * rows, rows)])
        weights_of = lambda which, loose=0: run_weights(
            h, g, hids, [plan[s] for s in which], wide, loose
        )
        take_all = lambda kept, other, start: [
            (piece, other, (start + i) * wide) for i, piece in enumerate(kept)
        ]
        running, hids = tie(running, hids)
        far, far_other, beside_kept, beside_other = weights_of([6, 4, 7, 5], 1)
        far_other = [core(v) for v in far_other]
        moved = ring(running)
        moved, far, far_other, beside_kept, beside_other = tie(
            moved, far, far_other, beside_kept, beside_other
        )

        (running,) = run_adds([(moved, dh_parts[3])])
        running, far, far_other, h = tie(running, far, far_other, h)
        far = run_adds(list(zip(far, far_other)))
        moved = [ring(running), pair(far[0]), across(far[1]), core(beside_other)]
        x_kept, x_other, own_kept, own_other = weights_of([2, 0, 3, 1])
        moved, x_kept, x_other, own_kept, own_other, beside_kept = tie(
            moved, x_kept, x_other, own_kept, own_other, beside_kept
        )
        running, moved_gate, moved_up, beside_other = moved
        d_mid, d_a, small = token_gradients(running, dh_parts[0])
        d_a, d_mid, small, y_run, moved_gate, moved_up, beside_other = tie(
            d_a, d_mid, small, y_parts[1], moved_gate, moved_up, beside_other
        )

        moved = [across(d_a), pair(far[2]), ring(y_run), core(d_a), core(x_other)]
        y_sum = run_adds(take_all(beside_kept, beside_other, 0))
        (y_sum[0],) = run_adds([(y_sum[0], moved_gate)])
        x_other = moved.pop()
        x_sum = run_adds(take_all(x_kept, x_other, 0))
        moved, y_sum, x_sum = tie(moved, y_sum, x_sum)
        x_gate, x_up, x_down = x_sum
        da = [d_a, moved[3], moved[0]]
        moved_down, y_run = moved[1], moved[2]
        own_other, y_run, da_3 = tie(
            own_other, run_adds([(y_run, y_parts[2])])[0], core(da[2])
        )
        da.append(da_3)

        moved = [across(y_sum[0]), pair(x_gate), ring(y_run), core(own_other)]
        d_one, keep_one, send_one = back(0, da)
        moved, d_one, keep_one, send_one, da = tie(moved, d_one, keep_one, send_one, da)
        arrived_y, arrived_x, own_other = [moved[0]], [moved[1]], moved[3]
        y_down, x_up, y_run = run_adds(
            [(y_sum[2], moved_down), (x_up, moved_up), (moved[2], y_parts[3])]
        )
        y_down, x_up, y_run = tie(y_down, x_up, y_run)

        moved = [across(y_down), pair(send_one), ring(y_run), across(y_sum[1]), pair(x_up)]
        d_two, keep_two, send_two = back(1, da)
        d_parts, grad_gain_first = first_gradients([d_one, d_two])
        moved, d_parts, keep_two, send_two, grad_gain_first = tie(
            moved, d_parts, keep_two, send_two, grad_gain_first
        )
        arrived_y += [moved[0], moved[3]]
        arrived_x.append(moved[4])
        summed, from_one = moved[2], moved[1]
        extra = jnp.concatenate([small, grad_gain_first])
        send_two = lax.dynamic_update_slice(send_two, low(extra), (keep_two.shape[0], 0))
        d_parts, send_two, extra = tie(d_parts, send_two, extra)
        d_others = tie(core(d_parts[3]), core(d_parts[1]))
        to_send = low(d_parts[2] + full(d_others[0]))
        d_first = d_parts[0] + full(d_others[1])
        n = keep_two.shape[0]
        place = expert_index // 2

        def quarters(half):
            cuts = half.reshape(ring_size, n // ring_size, width)
            goes = [low(pick(cuts, (place + k) % ring_size)) for k in range(1, ring_size)]
            return pick(cuts, place), goes

        stay_one, go_one = quarters(keep_one + full(from_one[:n]))
        to_send, d_first, send_two, stay_one, go_one = tie(
            to_send, d_first, send_two, stay_one, go_one
        )

        moved = tie(
            across(to_send), pair(send_two), [shift(v, k + 1) for k, v in enumerate(go_one)]
        )
        d_in = input_rows(d_first + full(moved[0]), d_mid)
        stay_two, go_two = quarters(keep_two + full(moved[1][:n]))
        count = extra.shape[0]
        extra = extra + full(moved[1][n : n + count])
        wider = jnp.pad(low(extra), ((0, EXTRA - count), (0, 0)))
        go_two = [jnp.concatenate([v, wider]) for v in go_two]
        from_one = moved[2]
        d_in, go_two, stay_two, extra = tie(d_in, go_two, stay_two, extra)

        moved = [across(d_in), pair(x_down), [shift(v, k + 1) for k, v in enumerate(go_two)]]
        out_own = low(residual_mid + full(summed) + full(y_parts[0]))
        own_sum = run_adds(take_all(own_kept, own_other, 0))
        quarter_one = low(total_of([stay_one] + from_one))
        moved, out_own, own_sum, quarter_one = tie(moved, out_own, own_sum, quarter_one)
        arrived_x.append(moved[1])
        q = stay_two.shape[0]
        quarter_two = low(total_of([stay_two] + [v[:q] for v in moved[2]]))
        extra = total_of([extra] + [v[q : q + count] for v in moved[2]])
        out_more = jnp.concatenate([out_own, jnp.pad(low(extra), ((0, EXTRA - count), (0, 0)))])
        input_blocks = [d_in, core(d_in), moved[0], core(moved[0])]
        input_blocks, quarter_one, quarter_two, extra, out_more, arrived_x = tie(
            input_blocks, quarter_one, quarter_two, extra, out_more, arrived_x
        )

        moved = [across(out_more), core(out_more)]
        from_one = [shift(quarter_one, k) for k in range(1, ring_size)]
        input_gradient = run_place(mine, input_blocks, FULL)
        moved, from_one, input_gradient = tie(moved, from_one, input_gradient)
        one = laid_z([quarter_one] + from_one)
        one, quarter_two, arrived_x, arrived_y = tie(one, quarter_two, arrived_x, arrived_y)

        from_two = [shift(quarter_two, k) for k in range(1, ring_size)]
        one_other, out_3 = pair(one), core(moved[0])
        grads = [
            total_of([own_sum[0], arrived_y[0], arrived_x[0]]),
            total_of([own_sum[1], arrived_y[2], arrived_x[1]]),
            total_of([own_sum[2], arrived_y[1], arrived_x[2]]),
        ]
        unturned = lambda v: v.reshape(local, hidden, width).transpose(0, 2, 1)
        grad_gate, grad_up, grad_down = unturned(grads[0]), unturned(grads[1]), grads[2]
        from_two, one_other, out_3, grad_gate, grad_up, grad_down = tie(
            from_two, one_other, out_3, grad_gate, grad_up, grad_down
        )
        two = laid_z([quarter_two] + from_two)

        output = run_place(mine, [out_own, moved[1], moved[0], out_3], LOW)
        sums = total_of(
            [extra] + [v[rows : rows + count] for v in (moved[1], moved[0], out_3)]
        )
        two_other, output, sums = tie(pair(two), output, sums)
        finished = run_finish(mine, None, size, [(one, one_other), (two, two_other)])
    else:
        g = spread(sent)
        h = ring_gather(hidden_second)
        near, far = gather_weights([gate, up, down])
        places = [0] * (2 * len(near)) + [1] * (2 * len(far))
        weights = with_cores(near + far)
        step = max(1, min(ring_size, 1024 // rows))
        y_parts, dh_parts, dgb_parts, hids, plan = [], [], [], [], [[] for _ in weights]
        for i in range(0, ring_size, step):
            at = slice(i, i + step)
            y, dh, dgb, hid = experts(h[at], g[at], weights, places)
            y_parts, dh_parts, dgb_parts = y_parts + y, dh_parts + dh, dgb_parts + dgb
            for s in range(len(weights)):
                base = len(weights) * first + s * wide
                plan[s].append((len(hids), s * first, base, i * rows, step * rows))
            hids.append(hid)
        grad_parts = []
        for i in range(0, len(weights), 4):
            chips = run_weights(
                h, g, hids, [plan[i], plan[i + 2], plan[i + 1], plan[i + 3]], wide
            )
            for kept, other in ((chips[0], core(chips[1])), (chips[2], core(chips[3]))):
                grad_parts.append(
                    run_adds([(piece, other, j * wide) for j, piece in enumerate(kept)])
                )
        grad_gate, grad_up, grad_down = scatter_weights(grad_parts)
        unturned = lambda v: v.reshape(local, hidden, width).transpose(0, 2, 1)
        grad_gate, grad_up = unturned(grad_gate), unturned(grad_up)
        running = low(full(ring_partial(dh_parts)))
        d_mid, d_a, small = token_gradients(running, dh_parts[0])
        da = tensor_blocks(d_a)
        backs = [back(i, da, False) for i in range(groups)]
        d_parts, grad_gain_first = first_gradients([d for d, _ in backs])
        d_first = parts_sum(d_parts)
        input_blocks = tensor_blocks(input_rows(d_first, d_mid))
        input_gradient = run_place(mine, input_blocks, FULL)
        output = run_place(
            mine, tensor_blocks(low(residual_mid + ring_sum(y_parts))), LOW
        )
        finished = run_finish(
            mine, [lax.psum(square, "expert") for _, square in backs], size
        )
        sums = sum_everywhere(jnp.concatenate([small, grad_gain_first]))

    grad_query, grad_key, grad_value, grad_output = finished
    return (
        output,
        input_gradient,
        sums[-1],
        grad_query,
        grad_key,
        grad_value,
        grad_output,
        sums[0],
        sums[1:-1].T,
        grad_gate,
        grad_up,
        grad_down.reshape(local, hidden, width),
    )


def solution(mesh):
    in_specs = (
        P("expert", None),
        P("expert", None),
        P("expert", None),
        P("expert", None),
        P("expert", None),
        P(),
        P(None, "tensor"),
        P(None, "tensor"),
        P(None, "tensor"),
        P("tensor", None),
        P(),
        P(),
        P("expert", None, "tensor"),
        P("expert", None, "tensor"),
        P("expert", "tensor", None),
    )
    out_specs = (
        P("expert", None),
        P("expert", None),
        P(),
        P(None, "tensor"),
        P(None, "tensor"),
        P(None, "tensor"),
        P("tensor", None),
        P(),
        P(),
        P("expert", None, "tensor"),
        P("expert", None, "tensor"),
        P("expert", "tensor", None),
    )
    return jax.shard_map(shards, mesh=mesh, in_specs=in_specs, out_specs=out_specs, check_vma=False)
```

```python
import functools
import math

import jax
import jax.numpy as jnp
import numpy as np
from jax import lax
from jax.experimental import pallas as pl
from jax.experimental.pallas import tpu as pltpu
from jax.sharding import PartitionSpec as P

HEAD_WIDTH = 64
EPSILON = 1e-05
NEGATIVE = -1e30
LANES = 128
LOW = jnp.bfloat16
FULL = jnp.float32
NN = (((1,), (0,)), ((), ()))
NT = (((1,), (1,)), ((), ()))
TN = (((0,), (0,)), ((), ()))
BLOCK = 256
EXTRA = 32
AHEAD = 3
BUNCH = 2
TILE = 512
VMEM_GRANT = 58 * 1024 * 1024


def cost_of(flops, size):
    return pl.CostEstimate(flops=flops // 64, bytes_accessed=size // 64, transcendentals=0)


def tie(*values):
    return lax.optimization_barrier(values)


def mul(left, right, dims=NN):
    return lax.dot_general(left, right, dims, preferred_element_type=FULL)


def rope_tables(sequence_length):
    half_width = HEAD_WIDTH // 2
    frequency = np.exp(
        np.arange(half_width, dtype=np.float32) * np.float32(-2.0 * math.log(10000.0) / HEAD_WIDTH)
    )
    angles = np.arange(sequence_length, dtype=np.float32)[:, None] * frequency[None, :]
    cosine, sine = np.cos(angles), np.sin(angles)
    return (
        jnp.asarray(np.concatenate([cosine, cosine], axis=1)),
        jnp.asarray(np.concatenate([-sine, sine], axis=1)),
    )


def entire(shape):
    return pl.BlockSpec(shape, lambda i: (0,) * len(shape))


def normalized(values):
    inverse = lax.rsqrt(jnp.mean(values * values, axis=-1, keepdims=True) + EPSILON)
    return inverse


def swapped(values):
    half = values.shape[1] // 2
    return jnp.concatenate([values[:, half:], values[:, :half]], axis=1)


def tiles_of(length, tile):
    return [(start, min(length, start + tile + BLOCK)) for start in range(0, length, tile)]


def front_body(heads, groups, x_ref, gain_ref, wq_ref, wk_ref, wv_ref, cos_ref, sin_ref,
               h_ref, q_ref, k_ref, v_ref):
    scale = HEAD_WIDTH ** (-0.5)
    x = x_ref[...].astype(FULL)
    h = (x * normalized(x) * gain_ref[...]).astype(LOW)
    h_ref[...] = h
    zq, zk, zv = mul(h, wq_ref[...]), mul(h, wk_ref[...]), mul(h, wv_ref[...])
    cosine, sine = cos_ref[...], sin_ref[...]
    for j in range(heads + groups):
        z, n = (zq, j) if j < heads else (zk, j - heads)
        part = z[:, n * HEAD_WIDTH : (n + 1) * HEAD_WIDTH]
        part = part * cosine + swapped(part) * sine
        if j < heads:
            q_ref[j] = (part.astype(LOW).astype(FULL) * scale).astype(LOW)
        else:
            k_ref[j - heads] = part.astype(LOW)
    for j in range(groups):
        v_ref[j] = zv[:, j * HEAD_WIDTH : (j + 1) * HEAD_WIDTH].astype(LOW)


def run_front(x, gain, weights, cosine, sine, heads, groups):
    length, width = x.shape
    tile = min(256, length)
    shape = jax.ShapeDtypeStruct
    fixed = lambda v: pl.BlockSpec(v.shape, lambda i: (0,) * v.ndim)
    strip = lambda columns: pl.BlockSpec((tile, columns), lambda i: (i, 0))
    of_heads = lambda n: pl.BlockSpec((n, tile, HEAD_WIDTH), lambda i: (0, i, 0))
    return pl.pallas_call(
        functools.partial(front_body, heads, groups),
        grid=(length // tile,),
        out_shape=[
            shape((length, width), LOW),
            shape((heads, length, HEAD_WIDTH), LOW),
            shape((groups, length, HEAD_WIDTH), LOW),
            shape((groups, length, HEAD_WIDTH), LOW),
        ],
        in_specs=[strip(width), fixed(gain)]
        + [fixed(w) for w in weights]
        + [strip(HEAD_WIDTH), strip(HEAD_WIDTH)],
        out_specs=[strip(width), of_heads(heads), of_heads(groups), of_heads(groups)],
        compiler_params=pltpu.CompilerParams(vmem_limit_bytes=VMEM_GRANT),
        cost_estimate=cost_of(8 * length * width * width, 12 * length * width),
        name="front",
    )(x, gain, *weights, cosine, sine)


def add_body(count, *refs):
    for i in range(count):
        total = refs[2 * i][...].astype(FULL) + refs[2 * i + 1][...].astype(FULL)
        refs[2 * count + i][...] = total.astype(LOW)


def run_adds(pairs):
    rows, width = pairs[0][0].shape
    tile = rows // 2
    count = len(pairs)
    block = pl.BlockSpec((tile, width), lambda i: (i, 0))
    specs, values = [], []
    for one in pairs:
        offset = one[2] // tile if len(one) > 2 else 0
        specs += [block, pl.BlockSpec((tile, width), lambda i, offset=offset: (i + offset, 0))]
        values += one[:2]
    return list(
        pl.pallas_call(
            functools.partial(add_body, count),
            grid=(rows // tile,),
            out_shape=[jax.ShapeDtypeStruct((rows, width), LOW)] * count,
            in_specs=specs,
            out_specs=[block] * count,
            compiler_params=pltpu.CompilerParams(vmem_limit_bytes=20 * 1024 * 1024),
            cost_estimate=cost_of(1000, 6 * count * rows * width),
            name="adds",
        )(*values)
    )


def attention_body(heads, groups, rows, tile, mine_ref, q_ref, k_ref, v_ref, wo_ref, column_ref,
                   row_ref, mix_ref, lse_ref, *rest):
    part_refs, (turned_ref, out_ref) = rest[:-2], rest[-2:]
    length = row_ref.shape[1]
    size = heads // groups
    for j in range(groups):
        turned_ref[j] = v_ref[j].astype(FULL).T.astype(LOW)

    for group in range(groups):
        for start, keys in tiles_of(length, tile):
            visible = column_ref[0:keys, :] <= row_ref[:, start : start + tile]

            @pl.loop(group * size, (group + 1) * size)
            def _(head, group=group, start=start, keys=keys, visible=visible):
                s = mul(k_ref[group, 0:keys, :], q_ref[head, start : start + tile, :], NT)
                s = jnp.where(visible, s, NEGATIVE)
                peak = jnp.max(s, axis=0, keepdims=True)
                p = jnp.exp(s - peak)
                total = jnp.sum(p, axis=0, keepdims=True)
                lse_ref[head, :, start : start + tile] = peak + jnp.log(total)
                o = mul(turned_ref[group, :, 0:keys], p.astype(LOW)) / total
                out_ref[head, start : start + tile, :] = o.T.astype(LOW)

    for head in range(heads):
        mix_ref[:, head * HEAD_WIDTH : (head + 1) * HEAD_WIDTH] = out_ref[head]
    for r, part_ref in enumerate(part_refs):
        at = pl.ds(pl.multiple_of((mine_ref[0] ^ r) * rows, rows), rows)
        part_ref[...] = mul(mix_ref[at, :], wo_ref[...]).astype(part_ref.dtype)


def run_attention(mine, q, k, v, output_weight, column, row, count):
    heads, length, _ = q.shape
    groups = k.shape[0]
    width = output_weight.shape[1]
    rows = length // count
    shape = jax.ShapeDtypeStruct
    results = pl.pallas_call(
        functools.partial(attention_body, heads, groups, rows, min(2 * TILE, length)),
        grid=(1,),
        out_shape=[
            shape((length, heads * HEAD_WIDTH), LOW),
            shape((heads, 1, length), FULL),
        ]
        + [shape((rows, width), LOW if r % 2 else FULL) for r in range(count)],
        in_specs=[pl.BlockSpec(memory_space=pltpu.SMEM)]
        + [entire(v.shape) for v in (q, k, v, output_weight, column, row)],
        out_specs=[entire((length, heads * HEAD_WIDTH)), entire((heads, 1, length))]
        + [entire((rows, width))] * count,
        scratch_shapes=[
            pltpu.VMEM((groups, HEAD_WIDTH, length), LOW),
            pltpu.VMEM((heads, length, HEAD_WIDTH), LOW),
        ],
        compiler_params=pltpu.CompilerParams(vmem_limit_bytes=VMEM_GRANT),
        cost_estimate=cost_of(12 * length * width * width, 12 * length * width),
        name="attention",
    )(mine, q, k, v, output_weight, column, row)
    return results[0], results[1], list(results[2:])


def back_body(count, group, size, rows, tile, split, mine_ref, *rest):
    da_refs = rest[:count]
    (h_in, wo_ref, mix_ref, q_ref, k_ref, v_ref, lse_ref, column_ref, row_ref, cos_ref, sin_ref,
     d_ref, *outs, da_ref, h_ref, do_ref, turned_ref, dk_ref, dv_ref, dq_ref,
     square_ref, landed) = rest[count:]
    length = row_ref.shape[1]
    scale = HEAD_WIDTH ** (-0.5)
    first = group * size
    loads = []
    for r in range(count):
        at = pl.ds(pl.multiple_of((mine_ref[0] ^ r) * rows, rows), rows)
        load = pltpu.make_async_copy(da_refs[r], da_ref.at[at], landed.at[r])
        load.start()
        loads.append(load)
    late = pltpu.make_async_copy(h_in, h_ref, landed.at[count])
    late.start()
    turned_ref[...] = k_ref[group].astype(FULL).T.astype(LOW)
    dk_ref[...] = jnp.zeros(dk_ref.shape, FULL)
    dv_ref[...] = jnp.zeros(dv_ref.shape, FULL)
    for load in loads:
        load.wait()
    span = slice(first * HEAD_WIDTH, (first + size) * HEAD_WIDTH)

    @pl.loop(0, length // tile)
    def _(i):
        at = pl.ds(pl.multiple_of(i * tile, tile), tile)
        z = mul(da_ref[at, :], wo_ref[span, :], NT).astype(LOW)
        for j in range(size):
            do_ref[j, at, :] = z[:, j * HEAD_WIDTH : (j + 1) * HEAD_WIDTH]

    for start, keys in tiles_of(length, tile):
        visible = column_ref[0:keys, :] <= row_ref[:, start : start + tile]
        cosine, sine = cos_ref[start : start + tile, :], sin_ref[start : start + tile, :]

        @pl.loop(0, size)
        def _(head, start=start, keys=keys, visible=visible, cosine=cosine, sine=sine):
            q = q_ref[first + head, start : start + tile, :]
            do = do_ref[head, start : start + tile, :]
            s = mul(k_ref[group, 0:keys, :], q, NT)
            p = jnp.where(visible, jnp.exp(s - lse_ref[first + head, :, start : start + tile]), 0.0)
            dp = mul(v_ref[group, 0:keys, :], do, NT)
            delta = jnp.sum(p * dp, axis=0, keepdims=True)
            ds = (p * (dp - delta)).astype(LOW)
            dv_ref[0:keys, :] += mul(p.astype(LOW), do)
            dk_ref[0:keys, :] += mul(ds, q)
            dq = mul(turned_ref[:, 0:keys], ds).T * scale
            dq = dq * cosine - swapped(dq) * sine
            dq_ref[head, start : start + tile, :] = dq.astype(LOW)

    for head in range(size):
        d_ref[:, head * HEAD_WIDTH : (head + 1) * HEAD_WIDTH] = dq_ref[head]
    dk = dk_ref[...]
    dk = dk * cos_ref[...] - swapped(dk) * sin_ref[...]
    d_ref[:, size * HEAD_WIDTH : (size + 1) * HEAD_WIDTH] = dk.astype(LOW)
    d_ref[:, (size + 1) * HEAD_WIDTH :] = dv_ref[...].astype(LOW)
    late.wait()
    depth = (size + 2) * HEAD_WIDTH
    square_ref[0:depth, :] = mul(d_ref[...], h_ref[...], TN)
    square_ref[depth:, :] = mul(mix_ref[:, span], da_ref[...], TN)
    if not split:
        outs[0][...] = square_ref[...].astype(LOW)
        return
    keep_ref, send_ref = outs
    half = keep_ref.shape[0]
    for side in range(2):

        @pl.when(mine_ref[1] == side)
        def _(side=side):
            keep_ref[...] = square_ref[side * half : (side + 1) * half, :]
            send_ref[0:half, :] = square_ref[(1 - side) * half : (2 - side) * half, :].astype(LOW)

    send_ref[half:, :] = jnp.zeros((EXTRA, send_ref.shape[1]), LOW)


def run_back(group, split, mine, da, hidden, output_weight, mixture, q, k, v, lse, column, row, cosine, sine):
    heads, length, _ = q.shape
    groups = k.shape[0]
    size = heads // groups
    rows, width = da[0].shape
    count = len(da)
    half = (size + 1) * HEAD_WIDTH
    shape = jax.ShapeDtypeStruct
    return pl.pallas_call(
        functools.partial(back_body, count, group, size, rows, min(TILE, length), split),
        grid=(1,),
        out_shape=[
            shape((length, (size + 2) * HEAD_WIDTH), LOW),
        ]
        + (
            [shape((half, width), FULL), shape((half + EXTRA, width), LOW)]
            if split
            else [shape((2 * half, width), LOW)]
        ),
        in_specs=[pl.BlockSpec(memory_space=pltpu.SMEM)]
        + [pl.BlockSpec(memory_space=pltpu.HBM)] * (count + 1)
        + [
            entire(v.shape)
            for v in (output_weight, mixture, q, k, v, lse, column, row, cosine, sine)
        ],
        out_specs=[entire((length, (size + 2) * HEAD_WIDTH))]
        + (
            [entire((half, width)), entire((half + EXTRA, width))]
            if split
            else [entire((2 * half, width))]
        ),
        scratch_shapes=[
            pltpu.VMEM((length, width), LOW),
            pltpu.VMEM((length, width), LOW),
            pltpu.VMEM((size, length, HEAD_WIDTH), LOW),
            pltpu.VMEM((HEAD_WIDTH, length), LOW),
            pltpu.VMEM((length, HEAD_WIDTH), FULL),
            pltpu.VMEM((length, HEAD_WIDTH), FULL),
            pltpu.VMEM((size, length, HEAD_WIDTH), LOW),
            pltpu.VMEM((2 * half, width), FULL),
            pltpu.SemaphoreType.DMA((count + 1,)),
        ],
        compiler_params=pltpu.CompilerParams(vmem_limit_bytes=VMEM_GRANT),
        cost_estimate=cost_of(8 * length * width * width, 12 * length * width),
        name="back",
    )(mine, *da, hidden, output_weight, mixture, q, k, v, lse, column, row, cosine, sine)


def first_body(groups, x_ref, *rest):
    d_refs, w_refs = rest[:groups], rest[groups : 2 * groups]
    keep_ref, send_ref, gain_ref = rest[2 * groups :]
    step = pl.program_id(0)
    d_first = mul(d_refs[0][...], w_refs[0][...], NT)
    for d_ref, w_ref in zip(d_refs[1:], w_refs[1:]):
        d_first = d_first + mul(d_ref[...], w_ref[...], NT)

    @pl.when(step % 2 == 0)
    def _():
        keep_ref[...] = d_first

    @pl.when(step % 2 == 1)
    def _():
        send_ref[...] = d_first.astype(LOW)

    x = x_ref[...].astype(FULL)
    part = jnp.sum(d_first * (x * normalized(x)), axis=0, keepdims=True)

    @pl.when(step == 0)
    def _():
        gain_ref[...] = part

    @pl.when(step != 0)
    def _():
        gain_ref[...] += part


def run_first(mine, x, d_projected, weights, count):
    length, width = x.shape
    rows = length // count
    groups = len(weights)
    depth = weights[0].shape[1]
    strip = lambda columns: pl.BlockSpec((rows, columns), lambda r, m: (m[0] ^ r, 0))
    fixed = lambda shape: pl.BlockSpec(shape, lambda r, m: (0, 0))
    half = pl.BlockSpec((rows, width), lambda r, m: (r // 2, 0))
    return pl.pallas_call(
        lambda m, *refs: first_body(groups, *refs),
        grid_spec=pltpu.PrefetchScalarGridSpec(
            num_scalar_prefetch=1,
            grid=(count,),
            in_specs=[strip(width)]
            + [strip(depth)] * groups
            + [fixed((width, depth))] * groups,
            out_specs=[half, half, fixed((1, width))],
        ),
        out_shape=[
            jax.ShapeDtypeStruct((length // 2, width), FULL),
            jax.ShapeDtypeStruct((length // 2, width), LOW),
            jax.ShapeDtypeStruct((1, width), FULL),
        ],
        compiler_params=pltpu.CompilerParams(vmem_limit_bytes=VMEM_GRANT),
        cost_estimate=cost_of(1000, 1000),
        name="first_gradients",
    )(mine, x, *d_projected, *weights)


def token_body(num_experts, came_ref, own_ref, h_ref, router_ref, code_ref, mid_ref, gain_ref,
               g_ref, mid_out, low_out, gain_out, router_out):
    width = h_ref.shape[1]
    total = came_ref[...].astype(FULL) + own_ref[...].astype(FULL)
    d_gates = jnp.zeros(code_ref.shape, FULL)
    for n in range(3):
        tile, turn = divmod(n * num_experts, LANES)
        part = total[:, width + tile * LANES : width + (tile + 1) * LANES]
        d_gates = d_gates + (pltpu.roll(part, LANES - turn, 1) if turn else part)
    h = h_ref[...]
    code = code_ref[...]
    logits = mul(h, router_ref[...])
    picked = code > 0.5
    peak = jnp.max(jnp.where(picked, logits, NEGATIVE), axis=1, keepdims=True)
    exponent = jnp.where(picked, jnp.exp(logits - peak), 0.0)
    gates = exponent / jnp.sum(exponent, axis=1, keepdims=True)
    d_gates = jnp.where(code > 1.5, d_gates, 0.0)
    d_logits = gates * (d_gates - jnp.sum(gates * d_gates, axis=1, keepdims=True))
    d_logits = d_logits.astype(LOW)
    d_hidden = total[:, :width] + mul(d_logits, router_ref[...], NT)
    router_out[...] = mul(d_logits, h, TN)[:num_experts]
    mid = mid_ref[...]
    inverse = normalized(mid)
    normed = mid * inverse
    gain_out[...] = jnp.sum(d_hidden * normed, axis=0, keepdims=True)
    scaled = d_hidden * gain_ref[...]
    d_mid = g_ref[...].astype(FULL) + inverse * (
        scaled - normed * jnp.mean(scaled * normed, axis=1, keepdims=True)
    )
    mid_out[...] = d_mid
    low_out[...] = d_mid.astype(LOW)


def run_token(came, own, h, router, code, mid, gain, g, num_experts):
    rows, width = h.shape
    values = (came, own, h, router, code, mid, gain, g)
    shape = jax.ShapeDtypeStruct
    outs = ((rows, width), FULL), ((rows, width), LOW), ((1, width), FULL), ((num_experts, width), FULL)
    return pl.pallas_call(
        functools.partial(token_body, num_experts),
        grid=(1,),
        in_specs=[entire(v.shape) for v in values],
        out_specs=[entire(size) for size, _ in outs],
        out_shape=[shape(size, kind) for size, kind in outs],
        compiler_params=pltpu.CompilerParams(vmem_limit_bytes=28 * 1024 * 1024),
        cost_estimate=cost_of(1000, 1000),
        name="token_gradients",
    )(*values)


def finish_body(size, groups, split, mine_ref, *refs):
    count = 2 * groups if split else groups
    q_ref, k_ref, v_ref, o_ref = refs[count : count + 4]
    if split:
        half = refs[0].shape[0]
        wholes = refs[count + 4 :]
        for n in range(groups):
            for side in range(2):
                near = slice(side * half, (side + 1) * half)
                other = slice((1 - side) * half, (2 - side) * half)

                @pl.when(mine_ref[1] == side)
                def _(n=n, near=near, other=other):
                    wholes[n][near, :] = refs[2 * n][...]
                    wholes[n][other, :] = refs[2 * n + 1][...]

    else:
        wholes = refs[:groups]
    cut = size * HEAD_WIDTH
    spans = ((q_ref, 0, cut), (k_ref, cut, cut + HEAD_WIDTH), (v_ref, cut + HEAD_WIDTH, cut + 2 * HEAD_WIDTH))
    for ref, start, end in spans:
        ref[...] = jnp.concatenate([w[start:end, :].astype(FULL) for w in wholes]).T
    end = cut + 2 * HEAD_WIDTH
    for i, w in enumerate(wholes):
        o_ref[i * cut : (i + 1) * cut, :] = w[end:, :].astype(FULL)


def run_finish(mine, wholes, size, halves=None):
    values = wholes if halves is None else [v for pair_of in halves for v in pair_of]
    groups = len(wholes if halves is None else halves)
    depth, width = values[0].shape
    tile = 256
    heads = size * groups * HEAD_WIDTH
    down = lambda n: pl.BlockSpec((tile, n), lambda i: (i, 0))
    along = lambda n: pl.BlockSpec((n, tile), lambda i: (0, i))
    shape = jax.ShapeDtypeStruct
    return pl.pallas_call(
        functools.partial(finish_body, size, groups, halves is not None),
        grid=(width // tile,),
        in_specs=[pl.BlockSpec(memory_space=pltpu.SMEM)] + [along(depth)] * len(values),
        out_specs=[down(heads), down(groups * HEAD_WIDTH), down(groups * HEAD_WIDTH), along(heads)],
        out_shape=[
            shape((width, heads), FULL),
            shape((width, groups * HEAD_WIDTH), FULL),
            shape((width, groups * HEAD_WIDTH), FULL),
            shape((heads, width), FULL),
        ],
        scratch_shapes=[]
        if halves is None
        else [pltpu.VMEM((2 * depth, tile), LOW)] * groups,
        compiler_params=pltpu.CompilerParams(vmem_limit_bytes=24 * 1024 * 1024),
        cost_estimate=cost_of(1000, 1000),
        name="finish",
    )(mine, *values)


def place_body(rows, mine_ref, *refs):
    for r, ref in enumerate(refs[:-1]):
        at = pl.ds(pl.multiple_of((mine_ref[0] ^ r) * rows, rows), rows)
        refs[-1][at, :] = ref[0:rows, :].astype(refs[-1].dtype)


def run_place(mine, blocks, kind):
    rows, width = blocks[0].shape
    whole = pl.BlockSpec(memory_space=pltpu.VMEM)
    return pl.pallas_call(
        functools.partial(place_body, rows),
        out_shape=jax.ShapeDtypeStruct((len(blocks) * rows, width), kind),
        in_specs=[pl.BlockSpec(memory_space=pltpu.SMEM)] + [whole] * len(blocks),
        out_specs=whole,
        compiler_params=pltpu.CompilerParams(vmem_limit_bytes=24 * 1024 * 1024),
        cost_estimate=cost_of(1000, 10 * len(blocks) * rows * width),
        name="place",
    )(mine, *blocks)


def gate_columns(num_experts):
    return -(-3 * num_experts // LANES) * LANES


def expert_body(places, block_count, local, hidden, row_tile, column_tile, num_experts, more,
                columns_ref, router_ref, *rest):
    rest = list(rest)
    take = lambda n: [rest.pop(0) for _ in range(n)]
    shard_count = len(places)
    h_refs, g_refs = take(block_count), take(block_count)
    w_refs = [take(3) for _ in range(shard_count)]
    before = take(3 * block_count) if more else None
    y_outs, dh_outs, sum_outs = take(block_count), take(block_count), take(block_count)
    (hid_out,) = take(1)
    (h_ref, g_ref, hid_ref, first_buffer, second_buffer, code_ref, kept_ref, y_ref, dh_ref,
     sum_ref) = take(10)
    arrived, landed, left = rest
    wide = local * hidden
    first = 2 * wide
    rows = h_refs[0].shape[0]
    total, width = h_ref.shape
    span = [pl.ds(i * rows, rows) for i in range(block_count)]

    def begin(source, target, flag):
        copy = pltpu.make_async_copy(source, target, flag)
        copy.start()
        return copy

    loads, olds = [], []
    for i in range(block_count):
        loads += [
            begin(h_refs[i], h_ref.at[span[i]], landed.at[i, 0]),
            begin(g_refs[i].at[:, pl.ds(0, width)], g_ref.at[span[i]], landed.at[i, 1]),
            begin(g_refs[i].at[:, pl.ds(width, LANES)], code_ref.at[span[i]], landed.at[i, 2]),
        ]
        if more:
            for j, target in enumerate((y_ref, dh_ref, sum_ref)):
                olds.append(
                    begin(before[j * block_count + i], target.at[span[i]], landed.at[i, 3 + j])
                )
    copies = []

    def fetch(s):
        targets = (
            first_buffer.at[pl.ds(s * first, wide)],
            first_buffer.at[pl.ds(s * first + wide, wide)],
            second_buffer.at[pl.ds(s * wide, wide)],
        )
        copies.append([begin(w_refs[s][j], targets[j], arrived.at[s, j]) for j in range(3)])

    for s in range(min(AHEAD, shard_count)):
        fetch(s)
    for load in loads:
        load.wait()

    def find_gates():
        code = code_ref[...].astype(FULL)
        logits = mul(h_ref[...], router_ref[...])
        picked = code > 0.5
        peak = jnp.max(jnp.where(picked, logits, NEGATIVE), axis=1, keepdims=True)
        exponent = jnp.where(picked, jnp.exp(logits - peak), 0.0)
        gates = exponent / jnp.sum(exponent, axis=1, keepdims=True)
        kept_ref[...] = jnp.where(code > 1.5, gates, 0.0).astype(LOW).astype(FULL)

    if more:
        for old in olds:
            old.wait()
    else:
        sum_ref[...] = jnp.zeros(sum_ref.shape, FULL)
    lane = lax.broadcasted_iota(jnp.int32, (row_tile, LANES), 1)
    owner = lax.broadcasted_iota(jnp.int32, (row_tile, wide), 1) // hidden
    for base in range(0, shard_count, BUNCH):
        bunch = range(base, min(base + BUNCH, shard_count))
        for s in bunch:
            for copy in copies[s]:
                copy.wait()
        for s in range(len(copies), min(base + len(bunch) + AHEAD, shard_count)):
            fetch(s)
        for i in range(total // row_tile):
            at = slice(i * row_tile, (i + 1) * row_tile)
            zs = mul(h_ref[at, :], first_buffer[base * first : (bunch[-1] + 1) * first, :], NT)
            qs = mul(g_ref[at, :], second_buffer[base * wide : (bunch[-1] + 1) * wide, :], NT)
            if base == 0 and i == 0:
                find_gates()
            kept = kept_ref[at, :]
            dgb = sum_ref[at, :]
            for n, s in enumerate(bunch):
                hits = [lane == columns_ref[local * places[s] + e] for e in range(local)]
                gate_of = jnp.zeros((row_tile, wide), FULL)
                for e in range(local):
                    own = jnp.sum(jnp.where(hits[e], kept, 0.0), axis=1, keepdims=True)
                    gate_of = jnp.where(owner == e, own, gate_of)
                gate = zs[:, n * first : n * first + wide]
                up = zs[:, n * first + wide : (n + 1) * first]
                q = qs[:, n * wide : (n + 1) * wide]
                sigmoid = jax.nn.sigmoid(gate)
                silu = gate * sigmoid
                act = silu * up
                d_act = q * gate_of
                start = s * first
                hid_ref[at, start : start + wide] = (
                    d_act * up * sigmoid * (1.0 + gate * (1.0 - sigmoid))
                ).astype(LOW)
                hid_ref[at, start + wide : start + first] = (d_act * silu).astype(LOW)
                start = shard_count * first + s * wide
                hid_ref[at, start : start + wide] = (act * gate_of).astype(LOW)
                product = act * q
                for e in range(local):
                    part = jnp.sum(jnp.where(owner == e, product, 0.0), axis=1, keepdims=True)
                    dgb = dgb + jnp.where(hits[e], part, 0.0)
            sum_ref[at, :] = dgb

    leaves = [begin(hid_ref, hid_out, left.at[0, 0])]
    rest_of = sum_ref[...]
    tiles = [jnp.zeros((total, LANES), FULL)] * (gate_columns(num_experts) // LANES)
    for n in range(3):
        piece = rest_of.astype(LOW).astype(FULL)
        rest_of = rest_of - piece
        tile, turn = divmod(n * num_experts, LANES)
        tiles[tile] = tiles[tile] + (pltpu.roll(piece, turn, 1) if turn else piece)
    for n, tile in enumerate(tiles):
        dh_ref[:, width + n * LANES : width + (n + 1) * LANES] = tile.astype(LOW)
    middle = shard_count * first
    for i in range(block_count):
        at = slice(i * rows, (i + 1) * rows)

        y = mul(hid_ref[at, middle:], second_buffer[...])
        if more:
            y = y + y_ref[at, :].astype(FULL)
        y_ref[at, :] = y.astype(LOW)
        leaves.append(begin(y_ref.at[span[i]], y_outs[i], left.at[1 + i, 0]))
        dh = mul(hid_ref[at, 0:middle], first_buffer[...])
        if more:
            dh = dh + dh_ref[at, 0:width].astype(FULL)
        dh_ref[at, 0:width] = dh.astype(LOW)
        leaves += [
            begin(dh_ref.at[span[i]], dh_outs[i], left.at[1 + i, 1]),
            begin(sum_ref.at[span[i]], sum_outs[i], left.at[1 + i, 2]),
        ]
    for leave in leaves:
        leave.wait()


def run_experts(columns, router, h, g, weights, places, local, hidden, num_experts, before=None):
    count, blocks = len(weights), len(h)
    rows, width = h[0].shape
    wide = local * hidden
    depth = 3 * wide
    total = blocks * rows
    wider = width + gate_columns(num_experts)
    whole = pl.BlockSpec(memory_space=pltpu.VMEM)
    away = pl.BlockSpec(memory_space=pltpu.HBM)
    shape = jax.ShapeDtypeStruct
    extra = [] if before is None else before[0] + before[1] + before[2]
    results = pl.pallas_call(
        functools.partial(
            expert_body, tuple(places), blocks, local, hidden, total // -(-total // 256), width,
            num_experts, bool(extra),
        ),
        out_shape=[shape((rows, width), LOW)] * blocks
        + [shape((rows, wider), LOW)] * blocks
        + [shape((rows, LANES), FULL)] * blocks
        + [shape((total, count * depth), LOW)],
        in_specs=[pl.BlockSpec(memory_space=pltpu.SMEM), whole]
        + [away] * (2 * blocks + 3 * count + len(extra)),
        out_specs=[away] * (3 * blocks + 1),
        scratch_shapes=[
            pltpu.VMEM((total, width), LOW),
            pltpu.VMEM((total, width), LOW),
            pltpu.VMEM((total, count * depth), LOW),
            pltpu.VMEM((count * 2 * wide, width), LOW),
            pltpu.VMEM((count * wide, width), LOW),
            pltpu.VMEM((total, LANES), LOW),
            pltpu.VMEM((total, LANES), FULL),
            pltpu.VMEM((total, width), LOW),
            pltpu.VMEM((total, wider), LOW),
            pltpu.VMEM((total, LANES), FULL),
            pltpu.SemaphoreType.DMA((count, 3)),
            pltpu.SemaphoreType.DMA((blocks, 6)),
            pltpu.SemaphoreType.DMA((blocks + 1, 3)),
        ],
        compiler_params=pltpu.CompilerParams(
            vmem_limit_bytes=VMEM_GRANT
        ),
        cost_estimate=cost_of(4 * total * width * depth * count, depth * width * count * 2),
        name="experts",
    )(columns, router, *h, *g, *[piece for shard in weights for piece in shard], *extra)
    return (
        list(results[:blocks]),
        list(results[blocks : 2 * blocks]),
        list(results[2 * blocks : 3 * blocks]),
        results[-1],
    )


def weight_body(plan, rows, wide, *rest):
    rest = list(rest)
    take = lambda n: [rest.pop(0) for _ in range(n)]
    blocks = plan[0][1]
    shards_plan = plan[1]
    h_refs, g_refs = take(blocks), take(blocks)
    hid_refs = take(plan[0][0])
    stay = len(shards_plan) // 2
    out_refs = [take(3) for _ in range(stay)]
    loose = plan[2]
    away_refs = take(3 * loose + stay - loose)
    h_ref, g_ref, first_ref, second_ref, out_buffer, landed, arrived, left = rest
    loads = []
    for i in range(blocks):
        at = pl.ds(i * rows, rows)
        sources = (h_refs[i], g_refs[i].at[:, pl.ds(0, h_ref.shape[1])])
        for j, (source, target) in enumerate(zip(sources, (h_ref, g_ref))):
            load = pltpu.make_async_copy(source, target.at[at], landed.at[i, j])
            load.start()
            loads.append(load)

    def fetch(s):
        slot = s % 2
        group = []
        for n, (hid, first, second, start, count) in enumerate(shards_plan[s]):
            at = pl.ds(start, count)
            group.append(
                pltpu.make_async_copy(
                    hid_refs[hid].at[:, pl.ds(first, 2 * wide)],
                    first_ref.at[slot, at],
                    arrived.at[slot, n, 0],
                )
            )
            group.append(
                pltpu.make_async_copy(
                    hid_refs[hid].at[:, pl.ds(second, wide)],
                    second_ref.at[slot, at],
                    arrived.at[slot, n, 1],
                )
            )
        for copy in group:
            copy.start()
        return group

    waiting = fetch(0)
    leaves = []
    for load in loads:
        load.wait()
    for s in range(len(shards_plan)):
        following = fetch(s + 1) if s + 1 < len(shards_plan) else None
        for copy in waiting:
            copy.wait()
        slot = s % 2
        sums = (
            lambda: mul(first_ref[slot, :, 0:wide], h_ref[...], TN),
            lambda: mul(first_ref[slot, :, wide:], h_ref[...], TN),
            lambda: mul(second_ref[slot], g_ref[...], TN),
        )
        for j in range(3):
            start = 3 * s + j
            out_buffer[start * wide : (start + 1) * wide, :] = sums[j]().astype(LOW)
            if s < stay:
                target = out_refs[s][j]
            elif s - stay < loose:
                target = away_refs[3 * (s - stay) + j]
            else:
                target = away_refs[s - stay + 2 * loose].at[pl.ds(j * wide, wide)]
            leave = pltpu.make_async_copy(
                out_buffer.at[pl.ds(start * wide, wide)], target, left.at[start]
            )
            leave.start()
            leaves.append(leave)
        waiting = following
    for leave in leaves:
        leave.wait()


def run_weights(h, g, hids, shards_plan, wide, loose=0):
    blocks = len(h)
    rows, width = h[0].shape
    total = blocks * rows
    stay = len(shards_plan) // 2
    pieces = max(len(p) for p in shards_plan)
    away = pl.BlockSpec(memory_space=pltpu.HBM)
    plan = ((len(hids), blocks), tuple(tuple(p) for p in shards_plan), loose)
    results = pl.pallas_call(
        functools.partial(weight_body, plan, rows, wide),
        out_shape=[jax.ShapeDtypeStruct((wide, width), LOW)] * (3 * stay)
        + [jax.ShapeDtypeStruct((wide, width), LOW)] * (3 * loose)
        + [jax.ShapeDtypeStruct((3 * wide, width), LOW)] * (stay - loose),
        in_specs=[away] * (2 * blocks + len(hids)),
        out_specs=[away] * (4 * stay + 2 * loose),
        scratch_shapes=[
            pltpu.VMEM((total, width), LOW),
            pltpu.VMEM((total, width), LOW),
            pltpu.VMEM((2, total, 2 * wide), LOW),
            pltpu.VMEM((2, total, wide), LOW),
            pltpu.VMEM((6 * stay * wide, width), LOW),
            pltpu.SemaphoreType.DMA((blocks, 2)),
            pltpu.SemaphoreType.DMA((2, pieces, 2)),
            pltpu.SemaphoreType.DMA((6 * stay,)),
        ],
        compiler_params=pltpu.CompilerParams(vmem_limit_bytes=VMEM_GRANT),
        cost_estimate=cost_of(12 * total * width * wide * stay, total * 6 * wide * stay * 2),
        name="weight_gradients",
    )(*h, *g, *hids)
    chips = []
    for i in range(stay):
        start = 3 * (stay + i)
        other = list(results[start : start + 3]) if i < loose else results[3 * stay + 2 * loose + i]
        chips += [list(results[3 * i : 3 * i + 3]), other]
    return chips


def swap(values, axis, bit):
    count = lax.axis_size(axis)
    return lax.ppermute(values, axis, [(i, i ^ bit) for i in range(count)])


def pair(values):
    return swap(values, "expert", 1)


def ring(values):
    count = lax.axis_size("expert")
    return lax.ppermute(values, "expert", [(i, (i + 2) % count) for i in range(count)])


def pick(values, index):
    return lax.dynamic_index_in_dim(values, index, 0, keepdims=False)


def ring_gather(block):
    blocks = [block]
    for _ in range(lax.axis_size("expert") // 2 - 1):
        blocks.append(ring(blocks[-1]))
    return blocks


def ring_partial(blocks):
    running = blocks[1]
    for k in range(2, len(blocks) + 1):
        running = ring(running.astype(LOW))
        if k < len(blocks):
            running = running.astype(FULL) + blocks[k].astype(FULL)
    return running


def ring_sum(blocks):
    return ring_partial(blocks).astype(FULL) + blocks[0].astype(FULL)


def bits_of(count):
    return [1 << i for i in range(count.bit_length() - 1)]


def parts_sum(parts):
    parts = list(parts)
    for bit in bits_of(len(parts)):
        for r in reversed(range(0, len(parts), 2 * bit)):
            other = swap(parts[r + bit].astype(LOW), "tensor", bit)
            parts[r] = parts[r].astype(FULL) + other.astype(FULL)
    return parts[0]


def tensor_blocks(own):
    count = lax.axis_size("tensor")
    blocks = [own] * count
    for bit in reversed(bits_of(count)):
        for r in range(0, count, 2 * bit):
            blocks[r + bit] = swap(blocks[r], "tensor", bit)
    return blocks


def total_of(parts):
    return sum(part.astype(FULL) for part in parts)


def laid_z(blocks):
    size = len(blocks)
    place = lax.axis_index("expert") // 2
    whole = jnp.zeros((size,) + blocks[0].shape, blocks[0].dtype)
    for k, block in enumerate(blocks):
        whole = lax.dynamic_update_index_in_dim(whole, block, (place - k) % size, 0)
    return whole.reshape((-1,) + blocks[0].shape[1:])


def joined(half, other):
    low = lax.axis_index("expert") % 2 == 0
    return jnp.concatenate([jnp.where(low, half, other), jnp.where(low, other, half)])


def sum_everywhere(values):
    for axis in ("tensor", "expert"):
        for bit in bits_of(lax.axis_size(axis)):
            values = values + swap(values, axis, bit)
    return values


def shift(block, steps):
    count = lax.axis_size("expert")
    return lax.ppermute(block, "expert", [(i, (i + 2 * steps) % count) for i in range(count)])


def spread(block):
    return [block] + [shift(block, k) for k in range(1, lax.axis_size("expert") // 2)]


def with_cores(chips):
    shards_of = []
    for chip in chips:
        shards_of += [chip, [swap(piece, "tensor", 1) for piece in chip]]
    return shards_of


def gather_weights(own):
    near, far = [own], [[pair(piece) for piece in own]]
    for bit in bits_of(lax.axis_size("tensor"))[1:]:
        for i in range(len(near)):
            near.append([swap(piece, "tensor", bit) for piece in near[i]])
            far.append(
                [
                    pair(near[-1][0]),
                    swap(far[i][1], "tensor", bit),
                    pair(near[-1][2]),
                ]
            )
    return near, far


def scatter_weights(parts):
    full = lambda v: v.astype(FULL)
    sums = [[full(piece) for piece in chip] for chip in parts]
    near, far = sums[: len(sums) // 2], sums[len(sums) // 2 :]
    for bit in reversed(bits_of(lax.axis_size("tensor"))[1:]):
        count = len(near) // 2
        across = lambda v: full(swap(v.astype(LOW), "tensor", bit))
        beside = lambda v: full(pair(v.astype(LOW)))
        for i in range(count):
            last_near, last_far = near[count + i], far[count + i]
            last_near = [
                last_near[0] + beside(last_far[0]),
                last_near[1],
                last_near[2] + beside(last_far[2]),
            ]
            far[i] = [far[i][0], far[i][1] + across(last_far[1]), far[i][2]]
            near[i] = [one + across(two) for one, two in zip(near[i], last_near)]
        near, far = near[:count], far[:count]
    return [own + full(pair(other.astype(LOW))) for own, other in zip(near[0], far[0])]


def shards(
    activations,
    cotangent,
    block_ids,
    expert_ids,
    route_ranks,
    attention_gain,
    query_weight,
    key_matrix,
    value_matrix,
    output_weight,
    mixture_gain,
    router_weight,
    expert_gate,
    expert_up,
    expert_down,
):
    sequence_length, width = activations.shape
    heads = query_weight.shape[1] // HEAD_WIDTH
    groups = key_matrix.shape[1] // HEAD_WIDTH
    tensor_count = lax.axis_size("tensor")
    expert_count = lax.axis_size("expert")
    tensor_index = lax.axis_index("tensor")
    expert_index = lax.axis_index("expert")
    num_experts = router_weight.shape[1]
    local, _, hidden = expert_gate.shape
    picks = expert_ids.shape[1]
    capacity = sequence_length * picks // num_experts
    rows = sequence_length // tensor_count
    ring_size = expert_count // 2
    row_offset = tensor_index * rows
    own_rows = lambda v: lax.dynamic_slice_in_dim(v, row_offset, rows, 0)
    wide = local * hidden

    down = expert_down.reshape(wide, width)
    gate = expert_gate.transpose(0, 2, 1).reshape(wide, width)
    up = expert_up.transpose(0, 2, 1).reshape(wide, width)
    cotangent_own = own_rows(cotangent)
    ids_own, ranks_own = own_rows(expert_ids), own_rows(route_ranks)
    expert_range = jnp.arange(LANES, dtype=jnp.int32)
    pair_code = jnp.where(ranks_own < capacity, 2.0, 1.0)
    code = jnp.zeros((rows, LANES), FULL)
    for j in range(picks):
        code = code + jnp.where(
            ids_own[:, j, None] == expert_range[None, :], pair_code[:, j, None], 0.0
        )
    cosine, sine = rope_tables(sequence_length)
    gain_first = attention_gain.astype(FULL)[None]
    mine = jnp.stack([tensor_index, expert_index % 2]).astype(jnp.int32)
    row = block_ids
    column = block_ids.reshape(sequence_length, 1)
    fine = tensor_count == 4 and ring_size == 4
    x_in = activations
    across = lambda v: swap(v, "tensor", 2)
    sent = jnp.concatenate([cotangent_own, code.astype(LOW)], axis=1)
    x_own = own_rows(activations)
    core = lambda v: swap(v, "tensor", 1)
    if fine:
        sent = tie(sent)[0]
        moved = [pair(down), across(down), ring(sent), core(down)]
    hidden_first, q, k, v = run_front(
        x_in, gain_first, (query_weight, key_matrix, value_matrix), cosine, sine, heads, groups
    )
    if fine:
        moved, hidden_first, q, k, v, gate, up, x_own, column = tie(
            moved, hidden_first, q, k, v, gate, up, x_own, column
        )
        down_x, down_y, g_1, down_c = moved
        moved = [pair(gate), across(gate), ring(g_1), core(down_x), core(up)]
    mixture, lse, parts = run_attention(mine, q, k, v, output_weight, column, row, tensor_count)
    if fine:
        moved, mixture, lse, parts, up = tie(moved, mixture, lse, parts, up)
        gate_x, gate_y, g_2, down_xc, up_c = moved
        parts = tie(parts[0], parts[2], core(parts[3]), core(parts[1]))
        to_send = (parts[1] + parts[2].astype(FULL)).astype(LOW)
        attention_out = parts[0] + parts[3].astype(FULL)
        to_send, attention_out, up, g_2, gate_x, down_y, gate = tie(
            to_send, attention_out, up, g_2, gate_x, down_y, gate
        )
        moved = [across(to_send), pair(up), ring(g_2), core(gate_x), core(gate)]
        moved, gate_y, down_y = tie(moved, gate_y, down_y)
        attention_out = attention_out + moved[0].astype(FULL)
        up_x, g_3, gate_xc, gate_c = moved[1:]
        g = [sent, g_1, g_2, g_3]
    else:
        attention_out = parts_sum(parts)

    gain_second = mixture_gain.astype(FULL)
    residual_mid = x_own.astype(FULL) + attention_out
    inverse_second = normalized(residual_mid)
    normed_second = residual_mid * inverse_second
    hidden_second = (normed_second * gain_second).astype(LOW)

    router_wide = jnp.pad(router_weight, ((0, 0), (0, LANES - num_experts)))
    columns = jnp.concatenate(
        [
            expert_index * local + jnp.arange(local, dtype=jnp.int32),
            (expert_index ^ 1) * local + jnp.arange(local, dtype=jnp.int32),
        ]
    ).astype(jnp.int32)
    experts = lambda h, g, weights, places, before=None: run_experts(
        columns, router_wide, h, g, weights, places, local, hidden, num_experts, before
    )
    first = 2 * wide
    low = lambda v: v.astype(LOW)
    full = lambda v: v.astype(FULL)

    def token_gradients(came, own):
        d_mid, d_a, grad_gain, grad_router = run_token(
            came, own, hidden_second, router_wide, code, residual_mid, gain_second[None],
            cotangent_own, num_experts,
        )
        return d_mid, d_a, jnp.concatenate([grad_gain, grad_router])

    back = lambda group, da, split=True: run_back(
        group, split, mine, da, hidden_first, output_weight, mixture, q, k, v, lse, column, row, cosine, sine
    )
    size = heads // groups
    cut = size * HEAD_WIDTH
    group_weights = [
        jnp.concatenate(
            [
                query_weight[:, i * cut : (i + 1) * cut],
                key_matrix[:, i * HEAD_WIDTH : (i + 1) * HEAD_WIDTH],
                value_matrix[:, i * HEAD_WIDTH : (i + 1) * HEAD_WIDTH],
            ],
            axis=1,
        )
        for i in range(groups)
    ]

    first_gradients = lambda d_projected: run_first(
        mine, activations, d_projected, group_weights, tensor_count
    )

    def input_rows(d_first, d_mid):
        values = full(x_own)
        inverse = normalized(values)
        normed = values * inverse
        scaled = d_first * gain_first
        return low(
            d_mid
            + inverse * (scaled - normed * jnp.mean(scaled * normed, axis=-1, keepdims=True))
        )

    if fine:
        h = [hidden_second]
        moved = [ring(h[0]), across(up), pair(down_y)]
        up_xc, gate_yc = core(up_x), core(gate_y)
        side = [
            [gate, up, down], [gate_c, up_c, down_c],
            [gate_x, up_x, down_x], [gate_xc, up_xc, down_xc],
        ]
        side_places = [0, 0, 1, 1]
        start = experts(h[:1], g[:1], side, side_places)
        moved, start, group_weights, gate_yc = tie(moved, start, group_weights, gate_yc)
        y_0, dh_0, dgb_0, hid_0 = start
        h.append(moved[0])
        up_y, down_far = moved[1:]

        moved = [ring(h[1]), across(gate_x), pair(up_y)]
        up_yc, down_yc = core(up_y), core(down_y)
        y_1, dh_1, dgb_1, hid_1 = experts(h[1:2], g[1:2], side, side_places)
        beside = [[gate_y, up_y, down_y], [gate_yc, up_yc, down_yc]]
        second = experts(
            h[:2], g[:2], beside, [0, 0], (y_0 + y_1, dh_0 + dh_1, dgb_0 + dgb_1)
        )
        moved, second, hid_1, down_far = tie(moved, second, hid_1, down_far)
        y_1, dh_1, dgb_1, hid_y = second
        h.append(moved[0])
        gate_far, up_far = moved[1:]

        moved = [ring(h[2])]
        gate_farc, up_farc, down_farc = core(gate_far), core(up_far), core(down_far)
        y_2, dh_2, dgb_2, hid_2 = experts(h[2:3], g[2:3], side + beside, side_places + [0, 0])
        distant = [[gate_far, up_far, down_far], [gate_farc, up_farc, down_farc]]
        third = experts(
            h[:3], g[:3], distant, [1, 1], (y_1 + y_2, dh_1 + dh_2, dgb_1 + dgb_2)
        )
        moved, third, hid_2, distant = tie(moved, third, hid_2, distant)
        y_parts, dh_parts, dgb_parts, hid_far = third
        h.append(moved[0])

        moved = ring(dh_parts[1])
        last = experts(h[3:], g[3:], side + beside + distant, side_places + [0, 0, 1, 1])
        moved, last = tie(moved, last)
        y, dh, _, hid_last = last
        y_parts, dh_parts = y_parts + y, dh_parts + dh

        (running,) = run_adds([(moved, dh_parts[2])])
        hids = [hid_0, hid_1, hid_y, hid_2, hid_far, hid_last]
        plan = []
        for s in range(8):
            place_of = lambda n, i: (i * first, n * first + i * wide)
            if s < 4:
                head = [(b, *place_of(4, s), b * rows, rows) for b in (0, 1)]
                head.append((3, *place_of(6, s), 2 * rows, rows))
            elif s < 6:
                head = [(2, *place_of(2, s - 4), 0, 2 * rows)]
                head.append((3, *place_of(6, s), 2 * rows, rows))
            else:
                head = [(4, *place_of(2, s - 6), 0, 3 * rows)]
            plan.append(head + [(5, *place_of(8, s), 3 * rows, rows)])
        weights_of = lambda which, loose=0: run_weights(
            h, g, hids, [plan[s] for s in which], wide, loose
        )
        take_all = lambda kept, other, start: [
            (piece, other, (start + i) * wide) for i, piece in enumerate(kept)
        ]
        running, hids = tie(running, hids)
        far, far_other, beside_kept, beside_other = weights_of([6, 4, 7, 5], 1)
        far_other = [core(v) for v in far_other]
        moved = ring(running)
        moved, far, far_other, beside_kept, beside_other = tie(
            moved, far, far_other, beside_kept, beside_other
        )

        (running,) = run_adds([(moved, dh_parts[3])])
        running, far, far_other, h = tie(running, far, far_other, h)
        far = run_adds(list(zip(far, far_other)))
        moved = [ring(running), pair(far[0]), across(far[1]), core(beside_other)]
        x_kept, x_other, own_kept, own_other = weights_of([2, 0, 3, 1])
        moved, x_kept, x_other, own_kept, own_other, beside_kept = tie(
            moved, x_kept, x_other, own_kept, own_other, beside_kept
        )
        running, moved_gate, moved_up, beside_other = moved
        d_mid, d_a, small = token_gradients(running, dh_parts[0])
        d_a, d_mid, small, y_run, moved_gate, moved_up, beside_other = tie(
            d_a, d_mid, small, y_parts[1], moved_gate, moved_up, beside_other
        )

        moved = [across(d_a), pair(far[2]), ring(y_run), core(d_a), core(x_other)]
        y_sum = run_adds(take_all(beside_kept, beside_other, 0))
        (y_sum[0],) = run_adds([(y_sum[0], moved_gate)])
        x_other = moved.pop()
        x_sum = run_adds(take_all(x_kept, x_other, 0))
        (x_sum[1],) = run_adds([(x_sum[1], moved_up)])
        moved, y_sum, x_sum = tie(moved, y_sum, x_sum)
        x_gate, x_up, x_down = x_sum
        da = [d_a, moved[3], moved[0]]
        moved_down, y_run = moved[1], moved[2]
        own_other, y_run, da_3 = tie(
            own_other, run_adds([(y_run, y_parts[2])])[0], core(da[2])
        )
        da.append(da_3)

        moved = [across(y_sum[0]), pair(x_gate), ring(y_run), core(own_other)]
        d_one, keep_one, send_one = back(0, da)
        moved, d_one, keep_one, send_one, da = tie(moved, d_one, keep_one, send_one, da)
        arrived_y, arrived_x, own_other = [moved[0]], [moved[1]], moved[3]
        y_down, y_run = run_adds([(y_sum[2], moved_down), (moved[2], y_parts[3])])
        y_down, x_up, y_run = tie(y_down, x_up, y_run)

        moved = [across(y_down), pair(send_one), ring(y_run), across(y_sum[1]), pair(x_up)]
        d_two, keep_two, send_two = back(1, da)
        d_keep, d_send, grad_gain_first = first_gradients([d_one, d_two])
        moved, d_keep, d_send, keep_two, send_two, grad_gain_first = tie(
            moved, d_keep, d_send, keep_two, send_two, grad_gain_first
        )
        arrived_y += [moved[0], moved[3]]
        arrived_x.append(moved[4])
        summed, from_one = moved[2], moved[1]
        extra = jnp.concatenate([small, grad_gain_first])
        send_two = lax.dynamic_update_slice(send_two, low(extra), (keep_two.shape[0], 0))
        d_other = core(d_send)
        to_send = low(d_keep[rows:] + full(d_other[rows:]))
        d_first = d_keep[:rows] + full(d_other[:rows])
        n = keep_two.shape[0]
        place = expert_index // 2

        def quarters(half):
            cuts = half.reshape(ring_size, n // ring_size, width)
            goes = [low(pick(cuts, (place + k) % ring_size)) for k in range(1, ring_size)]
            return pick(cuts, place), goes

        stay_one, go_one = quarters(keep_one + full(from_one[:n]))
        to_send, d_first, send_two, stay_one, go_one = tie(
            to_send, d_first, send_two, stay_one, go_one
        )

        moved = tie(
            across(to_send), pair(send_two), [shift(v, k + 1) for k, v in enumerate(go_one)]
        )
        d_in = input_rows(d_first + full(moved[0]), d_mid)
        stay_two, go_two = quarters(keep_two + full(moved[1][:n]))
        count = extra.shape[0]
        extra = extra + full(moved[1][n : n + count])
        wider = jnp.pad(low(extra), ((0, EXTRA - count), (0, 0)))
        go_two = [jnp.concatenate([v, wider]) for v in go_two]
        from_one = moved[2]
        d_in, go_two, stay_two, extra = tie(d_in, go_two, stay_two, extra)

        moved = [across(d_in), pair(x_down), [shift(v, k + 1) for k, v in enumerate(go_two)]]
        out_own = low(residual_mid + full(summed) + full(y_parts[0]))
        own_sum = run_adds(take_all(own_kept, own_other, 0))
        quarter_one = low(total_of([stay_one] + from_one))
        moved, out_own, own_sum, quarter_one = tie(moved, out_own, own_sum, quarter_one)
        arrived_x.append(moved[1])
        q = stay_two.shape[0]
        quarter_two = low(total_of([stay_two] + [v[:q] for v in moved[2]]))
        extra = total_of([extra] + [v[q : q + count] for v in moved[2]])
        out_more = jnp.concatenate([out_own, jnp.pad(low(extra), ((0, EXTRA - count), (0, 0)))])
        input_blocks = [d_in, core(d_in), moved[0], core(moved[0])]
        input_blocks, quarter_one, quarter_two, extra, out_more, arrived_x = tie(
            input_blocks, quarter_one, quarter_two, extra, out_more, arrived_x
        )

        moved = [across(out_more), core(out_more)]
        from_one = [shift(quarter_one, k) for k in range(1, ring_size)]
        input_gradient = run_place(mine, input_blocks, FULL)
        moved, from_one, input_gradient = tie(moved, from_one, input_gradient)
        one = laid_z([quarter_one] + from_one)
        one, quarter_two, arrived_x, arrived_y = tie(one, quarter_two, arrived_x, arrived_y)

        from_two = [shift(quarter_two, k) for k in range(1, ring_size)]
        one_other, out_3 = pair(one), core(moved[0])
        grads = [
            total_of([own_sum[0], arrived_y[0], arrived_x[0]]),
            total_of([own_sum[1], arrived_y[2], arrived_x[1]]),
            total_of([own_sum[2], arrived_y[1], arrived_x[2]]),
        ]
        unturned = lambda v: v.reshape(local, hidden, width).transpose(0, 2, 1)
        grad_gate, grad_up, grad_down = unturned(grads[0]), unturned(grads[1]), grads[2]
        from_two, one_other, out_3, grad_gate, grad_up, grad_down = tie(
            from_two, one_other, out_3, grad_gate, grad_up, grad_down
        )
        two = laid_z([quarter_two] + from_two)

        output = run_place(mine, [out_own, moved[1], moved[0], out_3], LOW)
        sums = total_of(
            [extra] + [v[rows : rows + count] for v in (moved[1], moved[0], out_3)]
        )
        two_other, output, sums = tie(pair(two), output, sums)
        finished = run_finish(mine, None, size, [(one, one_other), (two, two_other)])
    else:
        g = spread(sent)
        h = ring_gather(hidden_second)
        near, far = gather_weights([gate, up, down])
        places = [0] * (2 * len(near)) + [1] * (2 * len(far))
        weights = with_cores(near + far)
        step = max(1, min(ring_size, 1024 // rows))
        y_parts, dh_parts, dgb_parts, hids, plan = [], [], [], [], [[] for _ in weights]
        for i in range(0, ring_size, step):
            at = slice(i, i + step)
            y, dh, dgb, hid = experts(h[at], g[at], weights, places)
            y_parts, dh_parts, dgb_parts = y_parts + y, dh_parts + dh, dgb_parts + dgb
            for s in range(len(weights)):
                base = len(weights) * first + s * wide
                plan[s].append((len(hids), s * first, base, i * rows, step * rows))
            hids.append(hid)
        grad_parts = []
        for i in range(0, len(weights), 4):
            chips = run_weights(
                h, g, hids, [plan[i], plan[i + 2], plan[i + 1], plan[i + 3]], wide
            )
            for kept, other in ((chips[0], core(chips[1])), (chips[2], core(chips[3]))):
                grad_parts.append(
                    run_adds([(piece, other, j * wide) for j, piece in enumerate(kept)])
                )
        grad_gate, grad_up, grad_down = scatter_weights(grad_parts)
        unturned = lambda v: v.reshape(local, hidden, width).transpose(0, 2, 1)
        grad_gate, grad_up = unturned(grad_gate), unturned(grad_up)
        running = low(full(ring_partial(dh_parts)))
        d_mid, d_a, small = token_gradients(running, dh_parts[0])
        da = tensor_blocks(d_a)
        backs = [back(i, da, False) for i in range(groups)]
        d_keep, d_send, grad_gain_first = first_gradients([d for d, _ in backs])
        d_parts = [
            (d_send if r % 2 else d_keep)[r // 2 * rows : (r // 2 + 1) * rows]
            for r in range(tensor_count)
        ]
        d_first = parts_sum(d_parts)
        input_blocks = tensor_blocks(input_rows(d_first, d_mid))
        input_gradient = run_place(mine, input_blocks, FULL)
        output = run_place(
            mine, tensor_blocks(low(residual_mid + ring_sum(y_parts))), LOW
        )
        finished = run_finish(
            mine, [lax.psum(square, "expert") for _, square in backs], size
        )
        sums = sum_everywhere(jnp.concatenate([small, grad_gain_first]))

    grad_query, grad_key, grad_value, grad_output = finished
    return (
        output,
        input_gradient,
        sums[-1],
        grad_query,
        grad_key,
        grad_value,
        grad_output,
        sums[0],
        sums[1:-1].T,
        grad_gate,
        grad_up,
        grad_down.reshape(local, hidden, width),
    )


def solution(mesh):
    in_specs = (
        P("expert", None),
        P("expert", None),
        P("expert", None),
        P("expert", None),
        P("expert", None),
        P(),
        P(None, "tensor"),
        P(None, "tensor"),
        P(None, "tensor"),
        P("tensor", None),
        P(),
        P(),
        P("expert", None, "tensor"),
        P("expert", None, "tensor"),
        P("expert", "tensor", None),
    )
    out_specs = (
        P("expert", None),
        P("expert", None),
        P(),
        P(None, "tensor"),
        P(None, "tensor"),
        P(None, "tensor"),
        P("tensor", None),
        P(),
        P(),
        P("expert", None, "tensor"),
        P("expert", None, "tensor"),
        P("expert", "tensor", None),
    )
    return jax.shard_map(shards, mesh=mesh, in_specs=in_specs, out_specs=out_specs, check_vma=False)
```

```python
import functools
import math

import jax
import jax.numpy as jnp
import numpy as np
from jax import lax
from jax.experimental import pallas as pl
from jax.experimental.pallas import tpu as pltpu
from jax.sharding import PartitionSpec as P

HEAD_WIDTH = 64
EPSILON = 1e-05
NEGATIVE = -1e30
LANES = 128
LOW = jnp.bfloat16
FULL = jnp.float32
NN = (((1,), (0,)), ((), ()))
NT = (((1,), (1,)), ((), ()))
TN = (((0,), (0,)), ((), ()))
BLOCK = 256
EXTRA = 32
AHEAD = 3
BUNCH = 2
TILE = 512
VMEM_GRANT = 58 * 1024 * 1024


def cost_of(flops, size):
    return pl.CostEstimate(flops=flops // 64, bytes_accessed=size // 64, transcendentals=0)


def tie(*values):
    return lax.optimization_barrier(values)


def mul(left, right, dims=NN):
    return lax.dot_general(left, right, dims, preferred_element_type=FULL)


def rope_tables(sequence_length):
    half_width = HEAD_WIDTH // 2
    frequency = np.exp(
        np.arange(half_width, dtype=np.float32) * np.float32(-2.0 * math.log(10000.0) / HEAD_WIDTH)
    )
    angles = np.arange(sequence_length, dtype=np.float32)[:, None] * frequency[None, :]
    cosine, sine = np.cos(angles), np.sin(angles)
    return (
        jnp.asarray(np.concatenate([cosine, cosine], axis=1)),
        jnp.asarray(np.concatenate([-sine, sine], axis=1)),
    )


def entire(shape):
    return pl.BlockSpec(shape, lambda i: (0,) * len(shape))


def normalized(values):
    inverse = lax.rsqrt(jnp.mean(values * values, axis=-1, keepdims=True) + EPSILON)
    return inverse


def swapped(values):
    half = values.shape[1] // 2
    return jnp.concatenate([values[:, half:], values[:, :half]], axis=1)


def tiles_of(length, tile):
    return [(start, min(length, start + tile + BLOCK)) for start in range(0, length, tile)]


def front_body(heads, groups, x_ref, gain_ref, wq_ref, wk_ref, wv_ref, cos_ref, sin_ref,
               h_ref, q_ref, k_ref, v_ref, inverse_ref):
    scale = HEAD_WIDTH ** (-0.5)
    x = x_ref[...].astype(FULL)
    inverse = normalized(x)
    inverse_ref[...] = inverse
    h = (x * inverse * gain_ref[...]).astype(LOW)
    h_ref[...] = h
    zq, zk, zv = mul(h, wq_ref[...]), mul(h, wk_ref[...]), mul(h, wv_ref[...])
    cosine, sine = cos_ref[...], sin_ref[...]
    for j in range(heads + groups):
        z, n = (zq, j) if j < heads else (zk, j - heads)
        part = z[:, n * HEAD_WIDTH : (n + 1) * HEAD_WIDTH]
        part = part * cosine + swapped(part) * sine
        if j < heads:
            q_ref[j] = (part.astype(LOW).astype(FULL) * scale).astype(LOW)
        else:
            k_ref[j - heads] = part.astype(LOW)
    for j in range(groups):
        v_ref[j] = zv[:, j * HEAD_WIDTH : (j + 1) * HEAD_WIDTH].astype(LOW)


def run_front(x, gain, weights, cosine, sine, heads, groups):
    length, width = x.shape
    tile = min(256, length)
    shape = jax.ShapeDtypeStruct
    fixed = lambda v: pl.BlockSpec(v.shape, lambda i: (0,) * v.ndim)
    strip = lambda columns: pl.BlockSpec((tile, columns), lambda i: (i, 0))
    of_heads = lambda n: pl.BlockSpec((n, tile, HEAD_WIDTH), lambda i: (0, i, 0))
    return pl.pallas_call(
        functools.partial(front_body, heads, groups),
        grid=(length // tile,),
        out_shape=[
            shape((length, width), LOW),
            shape((heads, length, HEAD_WIDTH), LOW),
            shape((groups, length, HEAD_WIDTH), LOW),
            shape((groups, length, HEAD_WIDTH), LOW),
            shape((length, 1), FULL),
        ],
        in_specs=[strip(width), fixed(gain)]
        + [fixed(w) for w in weights]
        + [strip(HEAD_WIDTH), strip(HEAD_WIDTH)],
        out_specs=[strip(width), of_heads(heads), of_heads(groups), of_heads(groups), strip(1)],
        compiler_params=pltpu.CompilerParams(vmem_limit_bytes=VMEM_GRANT),
        cost_estimate=cost_of(8 * length * width * width, 12 * length * width),
        name="front",
    )(x, gain, *weights, cosine, sine)


def add_body(count, *refs):
    for i in range(count):
        total = refs[2 * i][...].astype(FULL) + refs[2 * i + 1][...].astype(FULL)
        refs[2 * count + i][...] = total.astype(LOW)


def run_adds(pairs):
    rows, width = pairs[0][0].shape
    tile = rows // 2
    count = len(pairs)
    block = pl.BlockSpec((tile, width), lambda i: (i, 0))
    specs, values = [], []
    for one in pairs:
        offset = one[2] // tile if len(one) > 2 else 0
        specs += [block, pl.BlockSpec((tile, width), lambda i, offset=offset: (i + offset, 0))]
        values += one[:2]
    return list(
        pl.pallas_call(
            functools.partial(add_body, count),
            grid=(rows // tile,),
            out_shape=[jax.ShapeDtypeStruct((rows, width), LOW)] * count,
            in_specs=specs,
            out_specs=[block] * count,
            compiler_params=pltpu.CompilerParams(vmem_limit_bytes=20 * 1024 * 1024),
            cost_estimate=cost_of(1000, 6 * count * rows * width),
            name="adds",
        )(*values)
    )


def attention_body(heads, groups, rows, tile, mine_ref, q_ref, k_ref, v_ref, wo_ref, column_ref,
                   row_ref, mix_ref, lse_ref, *rest):
    part_refs, (turned_ref, out_ref) = rest[:-2], rest[-2:]
    length = row_ref.shape[1]
    size = heads // groups
    for j in range(groups):
        turned_ref[j] = v_ref[j].astype(FULL).T.astype(LOW)

    for group in range(groups):
        for start, keys in tiles_of(length, tile):
            visible = column_ref[0:keys, :] <= row_ref[:, start : start + tile]

            @pl.loop(group * size, (group + 1) * size)
            def _(head, group=group, start=start, keys=keys, visible=visible):
                s = mul(k_ref[group, 0:keys, :], q_ref[head, start : start + tile, :], NT)
                s = jnp.where(visible, s, NEGATIVE)
                peak = jnp.max(s, axis=0, keepdims=True)
                p = jnp.exp(s - peak)
                total = jnp.sum(p, axis=0, keepdims=True)
                lse_ref[head, :, start : start + tile] = peak + jnp.log(total)
                o = mul(turned_ref[group, :, 0:keys], p.astype(LOW)) / total
                out_ref[head, start : start + tile, :] = o.T.astype(LOW)

    for head in range(heads):
        mix_ref[:, head * HEAD_WIDTH : (head + 1) * HEAD_WIDTH] = out_ref[head]
    for r, part_ref in enumerate(part_refs):
        at = pl.ds(pl.multiple_of((mine_ref[0] ^ r) * rows, rows), rows)
        part_ref[...] = mul(mix_ref[at, :], wo_ref[...]).astype(part_ref.dtype)


def run_attention(mine, q, k, v, output_weight, column, row, count):
    heads, length, _ = q.shape
    groups = k.shape[0]
    width = output_weight.shape[1]
    rows = length // count
    shape = jax.ShapeDtypeStruct
    results = pl.pallas_call(
        functools.partial(attention_body, heads, groups, rows, min(2 * TILE, length)),
        grid=(1,),
        out_shape=[
            shape((length, heads * HEAD_WIDTH), LOW),
            shape((heads, 1, length), FULL),
        ]
        + [shape((rows, width), LOW if r % 2 else FULL) for r in range(count)],
        in_specs=[pl.BlockSpec(memory_space=pltpu.SMEM)]
        + [entire(v.shape) for v in (q, k, v, output_weight, column, row)],
        out_specs=[entire((length, heads * HEAD_WIDTH)), entire((heads, 1, length))]
        + [entire((rows, width))] * count,
        scratch_shapes=[
            pltpu.VMEM((groups, HEAD_WIDTH, length), LOW),
            pltpu.VMEM((heads, length, HEAD_WIDTH), LOW),
        ],
        compiler_params=pltpu.CompilerParams(vmem_limit_bytes=VMEM_GRANT),
        cost_estimate=cost_of(12 * length * width * width, 12 * length * width),
        name="attention",
    )(mine, q, k, v, output_weight, column, row)
    return results[0], results[1], list(results[2:])


def back_body(count, group, size, rows, tile, split, mine_ref, *rest):
    da_refs = rest[:count]
    (h_in, wo_ref, mix_ref, q_ref, k_ref, v_ref, lse_ref, column_ref, row_ref, cos_ref, sin_ref,
     d_ref, *outs, da_ref, h_ref, do_ref, turned_ref, dk_ref, dv_ref, dq_ref,
     square_ref, landed) = rest[count:]
    length = row_ref.shape[1]
    scale = HEAD_WIDTH ** (-0.5)
    first = group * size
    loads = []
    for r in range(count):
        at = pl.ds(pl.multiple_of((mine_ref[0] ^ r) * rows, rows), rows)
        load = pltpu.make_async_copy(da_refs[r], da_ref.at[at], landed.at[r])
        load.start()
        loads.append(load)
    late = pltpu.make_async_copy(h_in, h_ref, landed.at[count])
    late.start()
    turned_ref[...] = k_ref[group].astype(FULL).T.astype(LOW)
    dk_ref[...] = jnp.zeros(dk_ref.shape, FULL)
    dv_ref[...] = jnp.zeros(dv_ref.shape, FULL)
    for load in loads:
        load.wait()
    span = slice(first * HEAD_WIDTH, (first + size) * HEAD_WIDTH)

    @pl.loop(0, length // tile)
    def _(i):
        at = pl.ds(pl.multiple_of(i * tile, tile), tile)
        z = mul(da_ref[at, :], wo_ref[span, :], NT).astype(LOW)
        for j in range(size):
            do_ref[j, at, :] = z[:, j * HEAD_WIDTH : (j + 1) * HEAD_WIDTH]

    for start, keys in tiles_of(length, tile):
        visible = column_ref[0:keys, :] <= row_ref[:, start : start + tile]
        cosine, sine = cos_ref[start : start + tile, :], sin_ref[start : start + tile, :]

        @pl.loop(0, size)
        def _(head, start=start, keys=keys, visible=visible, cosine=cosine, sine=sine):
            q = q_ref[first + head, start : start + tile, :]
            do = do_ref[head, start : start + tile, :]
            s = mul(k_ref[group, 0:keys, :], q, NT)
            p = jnp.where(visible, jnp.exp(s - lse_ref[first + head, :, start : start + tile]), 0.0)
            dp = mul(v_ref[group, 0:keys, :], do, NT)
            delta = jnp.sum(p * dp, axis=0, keepdims=True)
            ds = (p * (dp - delta)).astype(LOW)
            dv_ref[0:keys, :] += mul(p.astype(LOW), do)
            dk_ref[0:keys, :] += mul(ds, q)
            dq = mul(turned_ref[:, 0:keys], ds).T * scale
            dq = dq * cosine - swapped(dq) * sine
            dq_ref[head, start : start + tile, :] = dq.astype(LOW)

    for head in range(size):
        d_ref[:, head * HEAD_WIDTH : (head + 1) * HEAD_WIDTH] = dq_ref[head]
    dk = dk_ref[...]
    dk = dk * cos_ref[...] - swapped(dk) * sin_ref[...]
    d_ref[:, size * HEAD_WIDTH : (size + 1) * HEAD_WIDTH] = dk.astype(LOW)
    d_ref[:, (size + 1) * HEAD_WIDTH :] = dv_ref[...].astype(LOW)
    late.wait()
    depth = (size + 2) * HEAD_WIDTH
    square_ref[0:depth, :] = mul(d_ref[...], h_ref[...], TN)
    square_ref[depth:, :] = mul(mix_ref[:, span], da_ref[...], TN)
    if not split:
        outs[0][...] = square_ref[...].astype(LOW)
        return
    keep_ref, send_ref = outs
    half = keep_ref.shape[0]
    for side in range(2):

        @pl.when(mine_ref[1] == side)
        def _(side=side):
            keep_ref[...] = square_ref[side * half : (side + 1) * half, :]
            send_ref[0:half, :] = square_ref[(1 - side) * half : (2 - side) * half, :].astype(LOW)

    send_ref[half:, :] = jnp.zeros((EXTRA, send_ref.shape[1]), LOW)


def run_back(group, split, mine, da, hidden, output_weight, mixture, q, k, v, lse, column, row, cosine, sine):
    heads, length, _ = q.shape
    groups = k.shape[0]
    size = heads // groups
    rows, width = da[0].shape
    count = len(da)
    half = (size + 1) * HEAD_WIDTH
    shape = jax.ShapeDtypeStruct
    return pl.pallas_call(
        functools.partial(back_body, count, group, size, rows, min(TILE, length), split),
        grid=(1,),
        out_shape=[
            shape((length, (size + 2) * HEAD_WIDTH), LOW),
        ]
        + (
            [shape((half, width), FULL), shape((half + EXTRA, width), LOW)]
            if split
            else [shape((2 * half, width), LOW)]
        ),
        in_specs=[pl.BlockSpec(memory_space=pltpu.SMEM)]
        + [pl.BlockSpec(memory_space=pltpu.HBM)] * (count + 1)
        + [
            entire(v.shape)
            for v in (output_weight, mixture, q, k, v, lse, column, row, cosine, sine)
        ],
        out_specs=[entire((length, (size + 2) * HEAD_WIDTH))]
        + (
            [entire((half, width)), entire((half + EXTRA, width))]
            if split
            else [entire((2 * half, width))]
        ),
        scratch_shapes=[
            pltpu.VMEM((length, width), LOW),
            pltpu.VMEM((length, width), LOW),
            pltpu.VMEM((size, length, HEAD_WIDTH), LOW),
            pltpu.VMEM((HEAD_WIDTH, length), LOW),
            pltpu.VMEM((length, HEAD_WIDTH), FULL),
            pltpu.VMEM((length, HEAD_WIDTH), FULL),
            pltpu.VMEM((size, length, HEAD_WIDTH), LOW),
            pltpu.VMEM((2 * half, width), FULL),
            pltpu.SemaphoreType.DMA((count + 1,)),
        ],
        compiler_params=pltpu.CompilerParams(vmem_limit_bytes=VMEM_GRANT),
        cost_estimate=cost_of(8 * length * width * width, 12 * length * width),
        name="back",
    )(mine, *da, hidden, output_weight, mixture, q, k, v, lse, column, row, cosine, sine)


def first_body(groups, count, mine_ref, x_ref, inverse_ref, *rest):
    d_refs, w_refs = rest[:groups], rest[groups : 2 * groups]
    keep_ref, send_ref, gain_ref, sum_ref = rest[2 * groups :]
    d_first = mul(d_refs[0][...], w_refs[0][...], NT)
    for d_ref, w_ref in zip(d_refs[1:], w_refs[1:]):
        d_first = d_first + mul(d_ref[...], w_ref[...], NT)
    sum_ref[...] = d_first
    normed = x_ref[...].astype(FULL) * inverse_ref[...]
    gain_ref[...] = jnp.sum(d_first * normed, axis=0, keepdims=True)
    rows = sum_ref.shape[0] // count
    for r in range(count):
        at = pl.ds(pl.multiple_of((mine_ref[0] ^ r) * rows, rows), rows)
        target = send_ref if r % 2 else keep_ref
        target[r // 2 * rows : (r // 2 + 1) * rows, :] = sum_ref[at, :].astype(target.dtype)


def run_first(mine, x, inverse, d_projected, weights, count):
    length, width = x.shape
    groups = len(weights)
    depth = weights[0].shape[1]
    tile = 256
    down = lambda n: pl.BlockSpec((n, tile), lambda i: (0, i))
    return pl.pallas_call(
        functools.partial(first_body, groups, count),
        grid=(width // tile,),
        in_specs=[pl.BlockSpec(memory_space=pltpu.SMEM), down(length), entire((length, 1))]
        + [entire((length, depth))] * groups
        + [pl.BlockSpec((tile, depth), lambda i: (i, 0))] * groups,
        out_specs=[down(length // 2), down(length // 2), down(1)],
        out_shape=[
            jax.ShapeDtypeStruct((length // 2, width), FULL),
            jax.ShapeDtypeStruct((length // 2, width), LOW),
            jax.ShapeDtypeStruct((1, width), FULL),
        ],
        scratch_shapes=[pltpu.VMEM((length, tile), FULL)],
        compiler_params=pltpu.CompilerParams(vmem_limit_bytes=VMEM_GRANT),
        cost_estimate=cost_of(1000, 1000),
        name="first_gradients",
    )(mine, x, inverse, *d_projected, *weights)


def token_body(num_experts, came_ref, own_ref, h_ref, router_ref, code_ref, mid_ref, gain_ref,
               g_ref, mid_out, low_out, gain_out, router_out):
    width = h_ref.shape[1]
    total = came_ref[...].astype(FULL) + own_ref[...].astype(FULL)
    d_gates = jnp.zeros(code_ref.shape, FULL)
    for n in range(3):
        tile, turn = divmod(n * num_experts, LANES)
        part = total[:, width + tile * LANES : width + (tile + 1) * LANES]
        d_gates = d_gates + (pltpu.roll(part, LANES - turn, 1) if turn else part)
    h = h_ref[...]
    code = code_ref[...]
    logits = mul(h, router_ref[...])
    picked = code > 0.5
    peak = jnp.max(jnp.where(picked, logits, NEGATIVE), axis=1, keepdims=True)
    exponent = jnp.where(picked, jnp.exp(logits - peak), 0.0)
    gates = exponent / jnp.sum(exponent, axis=1, keepdims=True)
    d_gates = jnp.where(code > 1.5, d_gates, 0.0)
    d_logits = gates * (d_gates - jnp.sum(gates * d_gates, axis=1, keepdims=True))
    d_logits = d_logits.astype(LOW)
    d_hidden = total[:, :width] + mul(d_logits, router_ref[...], NT)
    router_out[...] = mul(d_logits, h, TN)[:num_experts]
    mid = mid_ref[...]
    inverse = normalized(mid)
    normed = mid * inverse
    gain_out[...] = jnp.sum(d_hidden * normed, axis=0, keepdims=True)
    scaled = d_hidden * gain_ref[...]
    d_mid = g_ref[...].astype(FULL) + inverse * (
        scaled - normed * jnp.mean(scaled * normed, axis=1, keepdims=True)
    )
    mid_out[...] = d_mid
    low_out[...] = d_mid.astype(LOW)


def run_token(came, own, h, router, code, mid, gain, g, num_experts):
    rows, width = h.shape
    values = (came, own, h, router, code, mid, gain, g)
    shape = jax.ShapeDtypeStruct
    outs = ((rows, width), FULL), ((rows, width), LOW), ((1, width), FULL), ((num_experts, width), FULL)
    return pl.pallas_call(
        functools.partial(token_body, num_experts),
        grid=(1,),
        in_specs=[entire(v.shape) for v in values],
        out_specs=[entire(size) for size, _ in outs],
        out_shape=[shape(size, kind) for size, kind in outs],
        compiler_params=pltpu.CompilerParams(vmem_limit_bytes=28 * 1024 * 1024),
        cost_estimate=cost_of(1000, 1000),
        name="token_gradients",
    )(*values)


def finish_body(size, groups, split, mine_ref, *refs):
    count = 2 * groups if split else groups
    q_ref, k_ref, v_ref, o_ref = refs[count : count + 4]
    if split:
        half = refs[0].shape[0]
        wholes = refs[count + 4 :]
        for n in range(groups):
            for k in range(split):
                block = lax.rem(mine_ref[2] + split - k, split)
                for j, side in enumerate((mine_ref[1], 1 - mine_ref[1])):
                    start = pl.multiple_of(side * half + block * (half // split), half // split)
                    wholes[n][pl.ds(start, half // split), :] = refs[2 * n + j][
                        k * (half // split) : (k + 1) * (half // split), :
                    ]

    else:
        wholes = refs[:groups]
    cut = size * HEAD_WIDTH
    spans = ((q_ref, 0, cut), (k_ref, cut, cut + HEAD_WIDTH), (v_ref, cut + HEAD_WIDTH, cut + 2 * HEAD_WIDTH))
    for ref, start, end in spans:
        ref[...] = jnp.concatenate([w[start:end, :].astype(FULL) for w in wholes]).T
    end = cut + 2 * HEAD_WIDTH
    for i, w in enumerate(wholes):
        o_ref[i * cut : (i + 1) * cut, :] = w[end:, :].astype(FULL)


def run_finish(mine, wholes, size, halves=None, split=0):
    values = wholes if halves is None else [v for pair_of in halves for v in pair_of]
    groups = len(wholes if halves is None else halves)
    depth, width = values[0].shape
    tile = 256
    heads = size * groups * HEAD_WIDTH
    down = lambda n: pl.BlockSpec((tile, n), lambda i: (i, 0))
    along = lambda n: pl.BlockSpec((n, tile), lambda i: (0, i))
    shape = jax.ShapeDtypeStruct
    return pl.pallas_call(
        functools.partial(finish_body, size, groups, split),
        grid=(width // tile,),
        in_specs=[pl.BlockSpec(memory_space=pltpu.SMEM)] + [along(depth)] * len(values),
        out_specs=[down(heads), down(groups * HEAD_WIDTH), down(groups * HEAD_WIDTH), along(heads)],
        out_shape=[
            shape((width, heads), FULL),
            shape((width, groups * HEAD_WIDTH), FULL),
            shape((width, groups * HEAD_WIDTH), FULL),
            shape((heads, width), FULL),
        ],
        scratch_shapes=[]
        if halves is None
        else [pltpu.VMEM((2 * depth, tile), LOW)] * groups,
        compiler_params=pltpu.CompilerParams(vmem_limit_bytes=24 * 1024 * 1024),
        cost_estimate=cost_of(1000, 1000),
        name="finish",
    )(mine, *values)


def place_body(rows, mine_ref, *refs):
    for r, ref in enumerate(refs[:-1]):
        at = pl.ds(pl.multiple_of((mine_ref[0] ^ r) * rows, rows), rows)
        refs[-1][at, :] = ref[0:rows, :].astype(refs[-1].dtype)


def run_place(mine, blocks, kind):
    rows, width = blocks[0].shape
    whole = pl.BlockSpec(memory_space=pltpu.VMEM)
    return pl.pallas_call(
        functools.partial(place_body, rows),
        out_shape=jax.ShapeDtypeStruct((len(blocks) * rows, width), kind),
        in_specs=[pl.BlockSpec(memory_space=pltpu.SMEM)] + [whole] * len(blocks),
        out_specs=whole,
        compiler_params=pltpu.CompilerParams(vmem_limit_bytes=24 * 1024 * 1024),
        cost_estimate=cost_of(1000, 10 * len(blocks) * rows * width),
        name="place",
    )(mine, *blocks)


def gate_columns(num_experts):
    return -(-3 * num_experts // LANES) * LANES


def expert_body(places, block_count, local, hidden, row_tile, column_tile, num_experts, more,
                columns_ref, router_ref, *rest):
    rest = list(rest)
    take = lambda n: [rest.pop(0) for _ in range(n)]
    shard_count = len(places)
    h_refs, g_refs = take(block_count), take(block_count)
    w_refs = [take(3) for _ in range(shard_count)]
    before = take(3 * block_count) if more else None
    y_outs, dh_outs, sum_outs = take(block_count), take(block_count), take(block_count)
    (hid_out,) = take(1)
    (h_ref, g_ref, hid_ref, first_buffer, second_buffer, code_ref, kept_ref, y_ref, dh_ref,
     sum_ref) = take(10)
    arrived, landed, left = rest
    wide = local * hidden
    first = 2 * wide
    rows = h_refs[0].shape[0]
    total, width = h_ref.shape
    span = [pl.ds(i * rows, rows) for i in range(block_count)]

    def begin(source, target, flag):
        copy = pltpu.make_async_copy(source, target, flag)
        copy.start()
        return copy

    loads, olds = [], []
    for i in range(block_count):
        loads += [
            begin(h_refs[i], h_ref.at[span[i]], landed.at[i, 0]),
            begin(g_refs[i].at[:, pl.ds(0, width)], g_ref.at[span[i]], landed.at[i, 1]),
            begin(g_refs[i].at[:, pl.ds(width, LANES)], code_ref.at[span[i]], landed.at[i, 2]),
        ]
        if more:
            for j, target in enumerate((y_ref, dh_ref, sum_ref)):
                olds.append(
                    begin(before[j * block_count + i], target.at[span[i]], landed.at[i, 3 + j])
                )
    copies = []

    def fetch(s):
        targets = (
            first_buffer.at[pl.ds(s * first, wide)],
            first_buffer.at[pl.ds(s * first + wide, wide)],
            second_buffer.at[pl.ds(s * wide, wide)],
        )
        copies.append([begin(w_refs[s][j], targets[j], arrived.at[s, j]) for j in range(3)])

    for s in range(min(AHEAD, shard_count)):
        fetch(s)
    for load in loads:
        load.wait()

    def find_gates():
        code = code_ref[...].astype(FULL)
        logits = mul(h_ref[...], router_ref[...])
        picked = code > 0.5
        peak = jnp.max(jnp.where(picked, logits, NEGATIVE), axis=1, keepdims=True)
        exponent = jnp.where(picked, jnp.exp(logits - peak), 0.0)
        gates = exponent / jnp.sum(exponent, axis=1, keepdims=True)
        kept_ref[...] = jnp.where(code > 1.5, gates, 0.0).astype(LOW).astype(FULL)

    if more:
        for old in olds:
            old.wait()
    else:
        sum_ref[...] = jnp.zeros(sum_ref.shape, FULL)
    lane = lax.broadcasted_iota(jnp.int32, (row_tile, LANES), 1)
    owner = lax.broadcasted_iota(jnp.int32, (row_tile, wide), 1) // hidden
    for base in range(0, shard_count, BUNCH):
        bunch = range(base, min(base + BUNCH, shard_count))
        for s in bunch:
            for copy in copies[s]:
                copy.wait()
        for s in range(len(copies), min(base + len(bunch) + AHEAD, shard_count)):
            fetch(s)
        for i in range(total // row_tile):
            at = slice(i * row_tile, (i + 1) * row_tile)
            zs = mul(h_ref[at, :], first_buffer[base * first : (bunch[-1] + 1) * first, :], NT)
            qs = mul(g_ref[at, :], second_buffer[base * wide : (bunch[-1] + 1) * wide, :], NT)
            if base == 0 and i == 0:
                find_gates()
            kept = kept_ref[at, :]
            dgb = sum_ref[at, :]
            for n, s in enumerate(bunch):
                hits = [lane == columns_ref[local * places[s] + e] for e in range(local)]
                gate_of = jnp.zeros((row_tile, wide), FULL)
                for e in range(local):
                    own = jnp.sum(jnp.where(hits[e], kept, 0.0), axis=1, keepdims=True)
                    gate_of = jnp.where(owner == e, own, gate_of)
                gate = zs[:, n * first : n * first + wide]
                up = zs[:, n * first + wide : (n + 1) * first]
                q = qs[:, n * wide : (n + 1) * wide]
                sigmoid = jax.nn.sigmoid(gate)
                silu = gate * sigmoid
                act = silu * up
                d_act = q * gate_of
                start = s * first
                hid_ref[at, start : start + wide] = (
                    d_act * up * sigmoid * (1.0 + gate * (1.0 - sigmoid))
                ).astype(LOW)
                hid_ref[at, start + wide : start + first] = (d_act * silu).astype(LOW)
                start = shard_count * first + s * wide
                hid_ref[at, start : start + wide] = (act * gate_of).astype(LOW)
                product = act * q
                for e in range(local):
                    part = jnp.sum(jnp.where(owner == e, product, 0.0), axis=1, keepdims=True)
                    dgb = dgb + jnp.where(hits[e], part, 0.0)
            sum_ref[at, :] = dgb

    leaves = [begin(hid_ref, hid_out, left.at[0, 0])]
    rest_of = sum_ref[...]
    tiles = [jnp.zeros((total, LANES), FULL)] * (gate_columns(num_experts) // LANES)
    for n in range(3):
        piece = rest_of.astype(LOW).astype(FULL)
        rest_of = rest_of - piece
        tile, turn = divmod(n * num_experts, LANES)
        tiles[tile] = tiles[tile] + (pltpu.roll(piece, turn, 1) if turn else piece)
    for n, tile in enumerate(tiles):
        dh_ref[:, width + n * LANES : width + (n + 1) * LANES] = tile.astype(LOW)
    middle = shard_count * first
    for i in range(block_count):
        at = slice(i * rows, (i + 1) * rows)

        y = mul(hid_ref[at, middle:], second_buffer[...])
        if more:
            y = y + y_ref[at, :].astype(FULL)
        y_ref[at, :] = y.astype(LOW)
        leaves.append(begin(y_ref.at[span[i]], y_outs[i], left.at[1 + i, 0]))
        dh = mul(hid_ref[at, 0:middle], first_buffer[...])
        if more:
            dh = dh + dh_ref[at, 0:width].astype(FULL)
        dh_ref[at, 0:width] = dh.astype(LOW)
        leaves += [
            begin(dh_ref.at[span[i]], dh_outs[i], left.at[1 + i, 1]),
            begin(sum_ref.at[span[i]], sum_outs[i], left.at[1 + i, 2]),
        ]
    for leave in leaves:
        leave.wait()


def run_experts(columns, router, h, g, weights, places, local, hidden, num_experts, before=None):
    count, blocks = len(weights), len(h)
    rows, width = h[0].shape
    wide = local * hidden
    depth = 3 * wide
    total = blocks * rows
    wider = width + gate_columns(num_experts)
    whole = pl.BlockSpec(memory_space=pltpu.VMEM)
    away = pl.BlockSpec(memory_space=pltpu.HBM)
    shape = jax.ShapeDtypeStruct
    extra = [] if before is None else before[0] + before[1] + before[2]
    results = pl.pallas_call(
        functools.partial(
            expert_body, tuple(places), blocks, local, hidden, total // -(-total // 256), width,
            num_experts, bool(extra),
        ),
        out_shape=[shape((rows, width), LOW)] * blocks
        + [shape((rows, wider), LOW)] * blocks
        + [shape((rows, LANES), FULL)] * blocks
        + [shape((total, count * depth), LOW)],
        in_specs=[pl.BlockSpec(memory_space=pltpu.SMEM), whole]
        + [away] * (2 * blocks + 3 * count + len(extra)),
        out_specs=[away] * (3 * blocks + 1),
        scratch_shapes=[
            pltpu.VMEM((total, width), LOW),
            pltpu.VMEM((total, width), LOW),
            pltpu.VMEM((total, count * depth), LOW),
            pltpu.VMEM((count * 2 * wide, width), LOW),
            pltpu.VMEM((count * wide, width), LOW),
            pltpu.VMEM((total, LANES), LOW),
            pltpu.VMEM((total, LANES), FULL),
            pltpu.VMEM((total, width), LOW),
            pltpu.VMEM((total, wider), LOW),
            pltpu.VMEM((total, LANES), FULL),
            pltpu.SemaphoreType.DMA((count, 3)),
            pltpu.SemaphoreType.DMA((blocks, 6)),
            pltpu.SemaphoreType.DMA((blocks + 1, 3)),
        ],
        compiler_params=pltpu.CompilerParams(
            vmem_limit_bytes=VMEM_GRANT
        ),
        cost_estimate=cost_of(4 * total * width * depth * count, depth * width * count * 2),
        name="experts",
    )(columns, router, *h, *g, *[piece for shard in weights for piece in shard], *extra)
    return (
        list(results[:blocks]),
        list(results[blocks : 2 * blocks]),
        list(results[2 * blocks : 3 * blocks]),
        results[-1],
    )


def weight_body(plan, rows, wide, *rest):
    rest = list(rest)
    take = lambda n: [rest.pop(0) for _ in range(n)]
    blocks = plan[0][1]
    shards_plan = plan[1]
    h_refs, g_refs = take(blocks), take(blocks)
    hid_refs = take(plan[0][0])
    stay = len(shards_plan) // 2
    out_refs = [take(3) for _ in range(stay)]
    loose = plan[2]
    away_refs = take(3 * loose + stay - loose)
    h_ref, g_ref, first_ref, second_ref, out_buffer, landed, arrived, left = rest
    loads = []
    for i in range(blocks):
        at = pl.ds(i * rows, rows)
        sources = (h_refs[i], g_refs[i].at[:, pl.ds(0, h_ref.shape[1])])
        for j, (source, target) in enumerate(zip(sources, (h_ref, g_ref))):
            load = pltpu.make_async_copy(source, target.at[at], landed.at[i, j])
            load.start()
            loads.append(load)

    def fetch(s):
        slot = s % 2
        group = []
        for n, (hid, first, second, start, count) in enumerate(shards_plan[s]):
            at = pl.ds(start, count)
            group.append(
                pltpu.make_async_copy(
                    hid_refs[hid].at[:, pl.ds(first, 2 * wide)],
                    first_ref.at[slot, at],
                    arrived.at[slot, n, 0],
                )
            )
            group.append(
                pltpu.make_async_copy(
                    hid_refs[hid].at[:, pl.ds(second, wide)],
                    second_ref.at[slot, at],
                    arrived.at[slot, n, 1],
                )
            )
        for copy in group:
            copy.start()
        return group

    waiting = fetch(0)
    leaves = []
    for load in loads:
        load.wait()
    for s in range(len(shards_plan)):
        following = fetch(s + 1) if s + 1 < len(shards_plan) else None
        for copy in waiting:
            copy.wait()
        slot = s % 2
        sums = (
            lambda: mul(first_ref[slot, :, 0:wide], h_ref[...], TN),
            lambda: mul(first_ref[slot, :, wide:], h_ref[...], TN),
            lambda: mul(second_ref[slot], g_ref[...], TN),
        )
        for j in range(3):
            start = 3 * s + j
            out_buffer[start * wide : (start + 1) * wide, :] = sums[j]().astype(LOW)
            if s < stay:
                target = out_refs[s][j]
            elif s - stay < loose:
                target = away_refs[3 * (s - stay) + j]
            else:
                target = away_refs[s - stay + 2 * loose].at[pl.ds(j * wide, wide)]
            leave = pltpu.make_async_copy(
                out_buffer.at[pl.ds(start * wide, wide)], target, left.at[start]
            )
            leave.start()
            leaves.append(leave)
        waiting = following
    for leave in leaves:
        leave.wait()


def run_weights(h, g, hids, shards_plan, wide, loose=0):
    blocks = len(h)
    rows, width = h[0].shape
    total = blocks * rows
    stay = len(shards_plan) // 2
    pieces = max(len(p) for p in shards_plan)
    away = pl.BlockSpec(memory_space=pltpu.HBM)
    plan = ((len(hids), blocks), tuple(tuple(p) for p in shards_plan), loose)
    results = pl.pallas_call(
        functools.partial(weight_body, plan, rows, wide),
        out_shape=[jax.ShapeDtypeStruct((wide, width), LOW)] * (3 * stay)
        + [jax.ShapeDtypeStruct((wide, width), LOW)] * (3 * loose)
        + [jax.ShapeDtypeStruct((3 * wide, width), LOW)] * (stay - loose),
        in_specs=[away] * (2 * blocks + len(hids)),
        out_specs=[away] * (4 * stay + 2 * loose),
        scratch_shapes=[
            pltpu.VMEM((total, width), LOW),
            pltpu.VMEM((total, width), LOW),
            pltpu.VMEM((2, total, 2 * wide), LOW),
            pltpu.VMEM((2, total, wide), LOW),
            pltpu.VMEM((6 * stay * wide, width), LOW),
            pltpu.SemaphoreType.DMA((blocks, 2)),
            pltpu.SemaphoreType.DMA((2, pieces, 2)),
            pltpu.SemaphoreType.DMA((6 * stay,)),
        ],
        compiler_params=pltpu.CompilerParams(vmem_limit_bytes=VMEM_GRANT),
        cost_estimate=cost_of(12 * total * width * wide * stay, total * 6 * wide * stay * 2),
        name="weight_gradients",
    )(*h, *g, *hids)
    chips = []
    for i in range(stay):
        start = 3 * (stay + i)
        other = list(results[start : start + 3]) if i < loose else results[3 * stay + 2 * loose + i]
        chips += [list(results[3 * i : 3 * i + 3]), other]
    return chips


def swap(values, axis, bit):
    count = lax.axis_size(axis)
    return lax.ppermute(values, axis, [(i, i ^ bit) for i in range(count)])


def pair(values):
    return swap(values, "expert", 1)


def ring(values):
    count = lax.axis_size("expert")
    return lax.ppermute(values, "expert", [(i, (i + 2) % count) for i in range(count)])


def pick(values, index):
    return lax.dynamic_index_in_dim(values, index, 0, keepdims=False)


def ring_gather(block):
    blocks = [block]
    for _ in range(lax.axis_size("expert") // 2 - 1):
        blocks.append(ring(blocks[-1]))
    return blocks


def ring_partial(blocks):
    running = blocks[1]
    for k in range(2, len(blocks) + 1):
        running = ring(running.astype(LOW))
        if k < len(blocks):
            running = running.astype(FULL) + blocks[k].astype(FULL)
    return running


def ring_sum(blocks):
    return ring_partial(blocks).astype(FULL) + blocks[0].astype(FULL)


def bits_of(count):
    return [1 << i for i in range(count.bit_length() - 1)]


def parts_sum(parts):
    parts = list(parts)
    for bit in bits_of(len(parts)):
        for r in reversed(range(0, len(parts), 2 * bit)):
            other = swap(parts[r + bit].astype(LOW), "tensor", bit)
            parts[r] = parts[r].astype(FULL) + other.astype(FULL)
    return parts[0]


def tensor_blocks(own):
    count = lax.axis_size("tensor")
    blocks = [own] * count
    for bit in reversed(bits_of(count)):
        for r in range(0, count, 2 * bit):
            blocks[r + bit] = swap(blocks[r], "tensor", bit)
    return blocks


def total_of(parts):
    return sum(part.astype(FULL) for part in parts)


def laid_z(blocks):
    size = len(blocks)
    place = lax.axis_index("expert") // 2
    whole = jnp.zeros((size,) + blocks[0].shape, blocks[0].dtype)
    for k, block in enumerate(blocks):
        whole = lax.dynamic_update_index_in_dim(whole, block, (place - k) % size, 0)
    return whole.reshape((-1,) + blocks[0].shape[1:])


def joined(half, other):
    low = lax.axis_index("expert") % 2 == 0
    return jnp.concatenate([jnp.where(low, half, other), jnp.where(low, other, half)])


def sum_everywhere(values):
    for axis in ("tensor", "expert"):
        for bit in bits_of(lax.axis_size(axis)):
            values = values + swap(values, axis, bit)
    return values


def shift(block, steps):
    count = lax.axis_size("expert")
    return lax.ppermute(block, "expert", [(i, (i + 2 * steps) % count) for i in range(count)])


def spread(block):
    return [block] + [shift(block, k) for k in range(1, lax.axis_size("expert") // 2)]


def with_cores(chips):
    shards_of = []
    for chip in chips:
        shards_of += [chip, [swap(piece, "tensor", 1) for piece in chip]]
    return shards_of


def gather_weights(own):
    near, far = [own], [[pair(piece) for piece in own]]
    for bit in bits_of(lax.axis_size("tensor"))[1:]:
        for i in range(len(near)):
            near.append([swap(piece, "tensor", bit) for piece in near[i]])
            far.append(
                [
                    pair(near[-1][0]),
                    swap(far[i][1], "tensor", bit),
                    pair(near[-1][2]),
                ]
            )
    return near, far


def scatter_weights(parts):
    full = lambda v: v.astype(FULL)
    sums = [[full(piece) for piece in chip] for chip in parts]
    near, far = sums[: len(sums) // 2], sums[len(sums) // 2 :]
    for bit in reversed(bits_of(lax.axis_size("tensor"))[1:]):
        count = len(near) // 2
        across = lambda v: full(swap(v.astype(LOW), "tensor", bit))
        beside = lambda v: full(pair(v.astype(LOW)))
        for i in range(count):
            last_near, last_far = near[count + i], far[count + i]
            last_near = [
                last_near[0] + beside(last_far[0]),
                last_near[1],
                last_near[2] + beside(last_far[2]),
            ]
            far[i] = [far[i][0], far[i][1] + across(last_far[1]), far[i][2]]
            near[i] = [one + across(two) for one, two in zip(near[i], last_near)]
        near, far = near[:count], far[:count]
    return [own + full(pair(other.astype(LOW))) for own, other in zip(near[0], far[0])]


def shards(
    activations,
    cotangent,
    block_ids,
    expert_ids,
    route_ranks,
    attention_gain,
    query_weight,
    key_matrix,
    value_matrix,
    output_weight,
    mixture_gain,
    router_weight,
    expert_gate,
    expert_up,
    expert_down,
):
    sequence_length, width = activations.shape
    heads = query_weight.shape[1] // HEAD_WIDTH
    groups = key_matrix.shape[1] // HEAD_WIDTH
    tensor_count = lax.axis_size("tensor")
    expert_count = lax.axis_size("expert")
    tensor_index = lax.axis_index("tensor")
    expert_index = lax.axis_index("expert")
    num_experts = router_weight.shape[1]
    local, _, hidden = expert_gate.shape
    picks = expert_ids.shape[1]
    capacity = sequence_length * picks // num_experts
    rows = sequence_length // tensor_count
    ring_size = expert_count // 2
    row_offset = tensor_index * rows
    own_rows = lambda v: lax.dynamic_slice_in_dim(v, row_offset, rows, 0)
    wide = local * hidden

    down = expert_down.reshape(wide, width)
    gate = expert_gate.transpose(0, 2, 1).reshape(wide, width)
    up = expert_up.transpose(0, 2, 1).reshape(wide, width)
    cotangent_own = own_rows(cotangent)
    ids_own, ranks_own = own_rows(expert_ids), own_rows(route_ranks)
    expert_range = jnp.arange(LANES, dtype=jnp.int32)
    pair_code = jnp.where(ranks_own < capacity, 2.0, 1.0)
    code = jnp.zeros((rows, LANES), FULL)
    for j in range(picks):
        code = code + jnp.where(
            ids_own[:, j, None] == expert_range[None, :], pair_code[:, j, None], 0.0
        )
    cosine, sine = rope_tables(sequence_length)
    gain_first = attention_gain.astype(FULL)[None]
    mine = jnp.stack([tensor_index, expert_index % 2, expert_index // 2]).astype(jnp.int32)
    row = block_ids
    column = block_ids.reshape(sequence_length, 1)
    fine = tensor_count == 4 and ring_size == 4
    x_in = activations
    across = lambda v: swap(v, "tensor", 2)
    sent = jnp.concatenate([cotangent_own, code.astype(LOW)], axis=1)
    x_own = own_rows(activations)
    core = lambda v: swap(v, "tensor", 1)
    if fine:
        sent = tie(sent)[0]
        moved = [pair(down), across(down), ring(sent), core(down)]
    hidden_first, q, k, v, inverse_first = run_front(
        x_in, gain_first, (query_weight, key_matrix, value_matrix), cosine, sine, heads, groups
    )
    if fine:
        moved, hidden_first, q, k, v, gate, up, x_own, column = tie(
            moved, hidden_first, q, k, v, gate, up, x_own, column
        )
        down_x, down_y, g_1, down_c = moved
        moved = [pair(gate), across(gate), ring(g_1), core(down_x), core(up)]
    mixture, lse, parts = run_attention(mine, q, k, v, output_weight, column, row, tensor_count)
    if fine:
        moved, mixture, lse, parts, up = tie(moved, mixture, lse, parts, up)
        gate_x, gate_y, g_2, down_xc, up_c = moved
        parts = tie(parts[0], parts[2], core(parts[3]), core(parts[1]))
        to_send = (parts[1] + parts[2].astype(FULL)).astype(LOW)
        attention_out = parts[0] + parts[3].astype(FULL)
        to_send, attention_out, up, g_2, gate_x, down_y, gate = tie(
            to_send, attention_out, up, g_2, gate_x, down_y, gate
        )
        moved = [across(to_send), pair(up), ring(g_2), core(gate_x), core(gate)]
        moved, gate_y, down_y = tie(moved, gate_y, down_y)
        attention_out = attention_out + moved[0].astype(FULL)
        up_x, g_3, gate_xc, gate_c = moved[1:]
        g = [sent, g_1, g_2, g_3]
    else:
        attention_out = parts_sum(parts)

    gain_second = mixture_gain.astype(FULL)
    residual_mid = x_own.astype(FULL) + attention_out
    inverse_second = normalized(residual_mid)
    normed_second = residual_mid * inverse_second
    hidden_second = (normed_second * gain_second).astype(LOW)

    router_wide = jnp.pad(router_weight, ((0, 0), (0, LANES - num_experts)))
    columns = jnp.concatenate(
        [
            expert_index * local + jnp.arange(local, dtype=jnp.int32),
            (expert_index ^ 1) * local + jnp.arange(local, dtype=jnp.int32),
        ]
    ).astype(jnp.int32)
    experts = lambda h, g, weights, places, before=None: run_experts(
        columns, router_wide, h, g, weights, places, local, hidden, num_experts, before
    )
    first = 2 * wide
    low = lambda v: v.astype(LOW)
    full = lambda v: v.astype(FULL)

    def token_gradients(came, own):
        d_mid, d_a, grad_gain, grad_router = run_token(
            came, own, hidden_second, router_wide, code, residual_mid, gain_second[None],
            cotangent_own, num_experts,
        )
        return d_mid, d_a, jnp.concatenate([grad_gain, grad_router])

    back = lambda group, da, split=True: run_back(
        group, split, mine, da, hidden_first, output_weight, mixture, q, k, v, lse, column, row, cosine, sine
    )
    size = heads // groups
    cut = size * HEAD_WIDTH
    group_weights = [
        jnp.concatenate(
            [
                query_weight[:, i * cut : (i + 1) * cut],
                key_matrix[:, i * HEAD_WIDTH : (i + 1) * HEAD_WIDTH],
                value_matrix[:, i * HEAD_WIDTH : (i + 1) * HEAD_WIDTH],
            ],
            axis=1,
        )
        for i in range(groups)
    ]

    first_gradients = lambda d_projected: run_first(
        mine, activations, inverse_first, d_projected, group_weights, tensor_count
    )

    def input_rows(d_first, d_mid):
        values = full(x_own)
        inverse = normalized(values)
        normed = values * inverse
        scaled = d_first * gain_first
        return low(
            d_mid
            + inverse * (scaled - normed * jnp.mean(scaled * normed, axis=-1, keepdims=True))
        )

    if fine:
        h = [hidden_second]
        moved = [ring(h[0]), across(up), pair(down_y)]
        up_xc, gate_yc = core(up_x), core(gate_y)
        side = [
            [gate, up, down], [gate_c, up_c, down_c],
            [gate_x, up_x, down_x], [gate_xc, up_xc, down_xc],
        ]
        side_places = [0, 0, 1, 1]
        start = experts(h[:1], g[:1], side, side_places)
        moved, start, group_weights, gate_yc = tie(moved, start, group_weights, gate_yc)
        y_0, dh_0, dgb_0, hid_0 = start
        h.append(moved[0])
        up_y, down_far = moved[1:]

        moved = [ring(h[1]), across(gate_x), pair(up_y)]
        up_yc, down_yc = core(up_y), core(down_y)
        y_1, dh_1, dgb_1, hid_1 = experts(h[1:2], g[1:2], side, side_places)
        beside = [[gate_y, up_y, down_y], [gate_yc, up_yc, down_yc]]
        second = experts(
            h[:2], g[:2], beside, [0, 0], (y_0 + y_1, dh_0 + dh_1, dgb_0 + dgb_1)
        )
        moved, second, hid_1, down_far = tie(moved, second, hid_1, down_far)
        y_1, dh_1, dgb_1, hid_y = second
        h.append(moved[0])
        gate_far, up_far = moved[1:]

        moved = [ring(h[2])]
        gate_farc, up_farc, down_farc = core(gate_far), core(up_far), core(down_far)
        y_2, dh_2, dgb_2, hid_2 = experts(h[2:3], g[2:3], side + beside, side_places + [0, 0])
        distant = [[gate_far, up_far, down_far], [gate_farc, up_farc, down_farc]]
        third = experts(
            h[:3], g[:3], distant, [1, 1], (y_1 + y_2, dh_1 + dh_2, dgb_1 + dgb_2)
        )
        moved, third, hid_2, distant = tie(moved, third, hid_2, distant)
        y_parts, dh_parts, dgb_parts, hid_far = third
        h.append(moved[0])

        moved = ring(dh_parts[1])
        last = experts(h[3:], g[3:], side + beside + distant, side_places + [0, 0, 1, 1])
        moved, last = tie(moved, last)
        y, dh, _, hid_last = last
        y_parts, dh_parts = y_parts + y, dh_parts + dh

        (running,) = run_adds([(moved, dh_parts[2])])
        hids = [hid_0, hid_1, hid_y, hid_2, hid_far, hid_last]
        plan = []
        for s in range(8):
            place_of = lambda n, i: (i * first, n * first + i * wide)
            if s < 4:
                head = [(b, *place_of(4, s), b * rows, rows) for b in (0, 1)]
                head.append((3, *place_of(6, s), 2 * rows, rows))
            elif s < 6:
                head = [(2, *place_of(2, s - 4), 0, 2 * rows)]
                head.append((3, *place_of(6, s), 2 * rows, rows))
            else:
                head = [(4, *place_of(2, s - 6), 0, 3 * rows)]
            plan.append(head + [(5, *place_of(8, s), 3 * rows, rows)])
        weights_of = lambda which, loose=0: run_weights(
            h, g, hids, [plan[s] for s in which], wide, loose
        )
        take_all = lambda kept, other, start: [
            (piece, other, (start + i) * wide) for i, piece in enumerate(kept)
        ]
        running, hids = tie(running, hids)
        far, far_other, beside_kept, beside_other = weights_of([6, 4, 7, 5], 1)
        far_other = [core(v) for v in far_other]
        moved = ring(running)
        moved, far, far_other, beside_kept, beside_other = tie(
            moved, far, far_other, beside_kept, beside_other
        )

        (running,) = run_adds([(moved, dh_parts[3])])
        running, far, far_other, h = tie(running, far, far_other, h)
        far = run_adds(list(zip(far, far_other)))
        moved = [ring(running), pair(far[0]), across(far[1]), core(beside_other)]
        x_kept, x_other, own_kept, own_other = weights_of([2, 0, 3, 1])
        moved, x_kept, x_other, own_kept, own_other, beside_kept = tie(
            moved, x_kept, x_other, own_kept, own_other, beside_kept
        )
        running, moved_gate, moved_up, beside_other = moved
        d_mid, d_a, small = token_gradients(running, dh_parts[0])
        d_a, d_mid, small, y_run, moved_gate, moved_up, beside_other = tie(
            d_a, d_mid, small, y_parts[1], moved_gate, moved_up, beside_other
        )

        moved = [across(d_a), pair(far[2]), ring(y_run), core(d_a), core(x_other)]
        y_sum = run_adds(take_all(beside_kept, beside_other, 0))
        (y_sum[0],) = run_adds([(y_sum[0], moved_gate)])
        x_other = moved.pop()
        x_sum = run_adds(take_all(x_kept, x_other, 0))
        (x_sum[1],) = run_adds([(x_sum[1], moved_up)])
        moved, y_sum, x_sum = tie(moved, y_sum, x_sum)
        x_gate, x_up, x_down = x_sum
        da = [d_a, moved[3], moved[0]]
        moved_down, y_run = moved[1], moved[2]
        own_other, y_run, da_3 = tie(
            own_other, run_adds([(y_run, y_parts[2])])[0], core(da[2])
        )
        da.append(da_3)

        moved = [across(y_sum[0]), pair(x_gate), ring(y_run), core(own_other)]
        d_one, keep_one, send_one = back(0, da)
        moved, d_one, keep_one, send_one, da = tie(moved, d_one, keep_one, send_one, da)
        arrived_y, arrived_x, own_other = [moved[0]], [moved[1]], moved[3]
        y_down, y_run = run_adds([(y_sum[2], moved_down), (moved[2], y_parts[3])])
        y_down, x_up, y_run = tie(y_down, x_up, y_run)

        moved = [across(y_down), pair(send_one), ring(y_run), across(y_sum[1]), pair(x_up)]
        d_two, keep_two, send_two = back(1, da)
        d_keep, d_send, grad_gain_first = first_gradients([d_one, d_two])
        moved, d_keep, d_send, keep_two, send_two, grad_gain_first = tie(
            moved, d_keep, d_send, keep_two, send_two, grad_gain_first
        )
        arrived_y += [moved[0], moved[3]]
        arrived_x.append(moved[4])
        summed, from_one = moved[2], moved[1]
        extra = jnp.concatenate([small, grad_gain_first])
        send_two = lax.dynamic_update_slice(send_two, low(extra), (keep_two.shape[0], 0))
        d_other = core(d_send)
        to_send = low(d_keep[rows:] + full(d_other[rows:]))
        d_first = d_keep[:rows] + full(d_other[:rows])
        n = keep_two.shape[0]
        place = expert_index // 2

        def quarters(half):
            cuts = half.reshape(ring_size, n // ring_size, width)
            goes = [low(pick(cuts, (place + k) % ring_size)) for k in range(1, ring_size)]
            return pick(cuts, place), goes

        stay_one, go_one = quarters(keep_one + full(from_one[:n]))
        to_send, d_first, send_two, stay_one, go_one = tie(
            to_send, d_first, send_two, stay_one, go_one
        )

        moved = tie(
            across(to_send), pair(send_two), [shift(v, k + 1) for k, v in enumerate(go_one)]
        )
        d_in = input_rows(d_first + full(moved[0]), d_mid)
        stay_two, go_two = quarters(keep_two + full(moved[1][:n]))
        count = extra.shape[0]
        extra = extra + full(moved[1][n : n + count])
        wider = jnp.pad(low(extra), ((0, EXTRA - count), (0, 0)))
        go_two = [jnp.concatenate([v, wider]) for v in go_two]
        from_one = moved[2]
        d_in, go_two, stay_two, extra = tie(d_in, go_two, stay_two, extra)

        moved = [across(d_in), pair(x_down), [shift(v, k + 1) for k, v in enumerate(go_two)]]
        out_own = low(residual_mid + full(summed) + full(y_parts[0]))
        own_sum = run_adds(take_all(own_kept, own_other, 0))
        quarter_one = low(total_of([stay_one] + from_one))
        moved, out_own, own_sum, quarter_one = tie(moved, out_own, own_sum, quarter_one)
        arrived_x.append(moved[1])
        q = stay_two.shape[0]
        quarter_two = low(total_of([stay_two] + [v[:q] for v in moved[2]]))
        extra = total_of([extra] + [v[q : q + count] for v in moved[2]])
        out_more = jnp.concatenate([out_own, jnp.pad(low(extra), ((0, EXTRA - count), (0, 0)))])
        input_blocks = [d_in, core(d_in), moved[0], core(moved[0])]
        input_blocks, quarter_one, quarter_two, extra, out_more, arrived_x = tie(
            input_blocks, quarter_one, quarter_two, extra, out_more, arrived_x
        )

        moved = [across(out_more), core(out_more)]
        from_one = [shift(quarter_one, k) for k in range(1, ring_size)]
        input_gradient = run_place(mine, input_blocks, FULL)
        grads = [
            total_of([own_sum[0], arrived_y[0], arrived_x[0]]),
            total_of([own_sum[1], arrived_y[2], arrived_x[1]]),
            total_of([own_sum[2], arrived_y[1], arrived_x[2]]),
        ]
        unturned = lambda v: v.reshape(local, hidden, width).transpose(0, 2, 1)
        grad_gate, grad_up, grad_down = unturned(grads[0]), unturned(grads[1]), grads[2]
        moved, from_one, input_gradient, grad_gate, grad_up, grad_down = tie(
            moved, from_one, input_gradient, grad_gate, grad_up, grad_down
        )
        one = jnp.concatenate([quarter_one] + from_one)
        one, quarter_two = tie(one, quarter_two)

        from_two = [shift(quarter_two, k) for k in range(1, ring_size)]
        one_other, out_3 = pair(one), core(moved[0])
        from_two, one_other, out_3 = tie(from_two, one_other, out_3)
        two = jnp.concatenate([quarter_two] + from_two)

        output = run_place(mine, [out_own, moved[1], moved[0], out_3], LOW)
        sums = total_of(
            [extra] + [v[rows : rows + count] for v in (moved[1], moved[0], out_3)]
        )
        two_other, output, sums = tie(pair(two), output, sums)
        finished = run_finish(
            mine, None, size, [(one, one_other), (two, two_other)], ring_size
        )
    else:
        g = spread(sent)
        h = ring_gather(hidden_second)
        near, far = gather_weights([gate, up, down])
        places = [0] * (2 * len(near)) + [1] * (2 * len(far))
        weights = with_cores(near + far)
        step = max(1, min(ring_size, 1024 // rows))
        y_parts, dh_parts, dgb_parts, hids, plan = [], [], [], [], [[] for _ in weights]
        for i in range(0, ring_size, step):
            at = slice(i, i + step)
            y, dh, dgb, hid = experts(h[at], g[at], weights, places)
            y_parts, dh_parts, dgb_parts = y_parts + y, dh_parts + dh, dgb_parts + dgb
            for s in range(len(weights)):
                base = len(weights) * first + s * wide
                plan[s].append((len(hids), s * first, base, i * rows, step * rows))
            hids.append(hid)
        grad_parts = []
        for i in range(0, len(weights), 4):
            chips = run_weights(
                h, g, hids, [plan[i], plan[i + 2], plan[i + 1], plan[i + 3]], wide
            )
            for kept, other in ((chips[0], core(chips[1])), (chips[2], core(chips[3]))):
                grad_parts.append(
                    run_adds([(piece, other, j * wide) for j, piece in enumerate(kept)])
                )
        grad_gate, grad_up, grad_down = scatter_weights(grad_parts)
        unturned = lambda v: v.reshape(local, hidden, width).transpose(0, 2, 1)
        grad_gate, grad_up = unturned(grad_gate), unturned(grad_up)
        running = low(full(ring_partial(dh_parts)))
        d_mid, d_a, small = token_gradients(running, dh_parts[0])
        da = tensor_blocks(d_a)
        backs = [back(i, da, False) for i in range(groups)]
        d_keep, d_send, grad_gain_first = first_gradients([d for d, _ in backs])
        d_parts = [
            (d_send if r % 2 else d_keep)[r // 2 * rows : (r // 2 + 1) * rows]
            for r in range(tensor_count)
        ]
        d_first = parts_sum(d_parts)
        input_blocks = tensor_blocks(input_rows(d_first, d_mid))
        input_gradient = run_place(mine, input_blocks, FULL)
        output = run_place(
            mine, tensor_blocks(low(residual_mid + ring_sum(y_parts))), LOW
        )
        finished = run_finish(
            mine, [lax.psum(square, "expert") for _, square in backs], size
        )
        sums = sum_everywhere(jnp.concatenate([small, grad_gain_first]))

    grad_query, grad_key, grad_value, grad_output = finished
    return (
        output,
        input_gradient,
        sums[-1],
        grad_query,
        grad_key,
        grad_value,
        grad_output,
        sums[0],
        sums[1:-1].T,
        grad_gate,
        grad_up,
        grad_down.reshape(local, hidden, width),
    )


def solution(mesh):
    in_specs = (
        P("expert", None),
        P("expert", None),
        P("expert", None),
        P("expert", None),
        P("expert", None),
        P(),
        P(None, "tensor"),
        P(None, "tensor"),
        P(None, "tensor"),
        P("tensor", None),
        P(),
        P(),
        P("expert", None, "tensor"),
        P("expert", None, "tensor"),
        P("expert", "tensor", None),
    )
    out_specs = (
        P("expert", None),
        P("expert", None),
        P(),
        P(None, "tensor"),
        P(None, "tensor"),
        P(None, "tensor"),
        P("tensor", None),
        P(),
        P(),
        P("expert", None, "tensor"),
        P("expert", None, "tensor"),
        P("expert", "tensor", None),
    )
    return jax.shard_map(shards, mesh=mesh, in_specs=in_specs, out_specs=out_specs, check_vma=False)
```

```python
import functools
import math

import jax
import jax.numpy as jnp
import numpy as np
from jax import lax
from jax.experimental import pallas as pl
from jax.experimental.pallas import tpu as pltpu
from jax.sharding import PartitionSpec as P

HEAD_WIDTH = 64
EPSILON = 1e-05
NEGATIVE = -1e30
LANES = 128
LOW = jnp.bfloat16
FULL = jnp.float32
NN = (((1,), (0,)), ((), ()))
NT = (((1,), (1,)), ((), ()))
TN = (((0,), (0,)), ((), ()))
BLOCK = 256
EXTRA = 32
AHEAD = 3
BUNCH = 2
TILE = 512
VMEM_GRANT = 58 * 1024 * 1024


def cost_of(flops, size):
    return pl.CostEstimate(flops=flops // 64, bytes_accessed=size // 64, transcendentals=0)


def tie(*values):
    return lax.optimization_barrier(values)


def mul(left, right, dims=NN):
    return lax.dot_general(left, right, dims, preferred_element_type=FULL)


def rope_tables(sequence_length):
    half_width = HEAD_WIDTH // 2
    frequency = np.exp(
        np.arange(half_width, dtype=np.float32) * np.float32(-2.0 * math.log(10000.0) / HEAD_WIDTH)
    )
    angles = np.arange(sequence_length, dtype=np.float32)[:, None] * frequency[None, :]
    cosine, sine = np.cos(angles), np.sin(angles)
    return (
        jnp.asarray(np.concatenate([cosine, cosine], axis=1)),
        jnp.asarray(np.concatenate([-sine, sine], axis=1)),
    )


def entire(shape):
    return pl.BlockSpec(shape, lambda i: (0,) * len(shape))


def normalized(values):
    inverse = lax.rsqrt(jnp.mean(values * values, axis=-1, keepdims=True) + EPSILON)
    return inverse


def swapped(values):
    half = values.shape[1] // 2
    return jnp.concatenate([values[:, half:], values[:, :half]], axis=1)


def tiles_of(length, tile):
    return [(start, min(length, start + tile + BLOCK)) for start in range(0, length, tile)]


def front_body(heads, groups, x_ref, gain_ref, wq_ref, wk_ref, wv_ref, cos_ref, sin_ref,
               h_ref, q_ref, k_ref, v_ref, inverse_ref):
    scale = HEAD_WIDTH ** (-0.5)
    x = x_ref[...].astype(FULL)
    inverse = normalized(x)
    inverse_ref[...] = inverse
    h = (x * inverse * gain_ref[...]).astype(LOW)
    h_ref[...] = h
    zq, zk, zv = mul(h, wq_ref[...]), mul(h, wk_ref[...]), mul(h, wv_ref[...])
    cosine, sine = cos_ref[...], sin_ref[...]
    for j in range(heads + groups):
        z, n = (zq, j) if j < heads else (zk, j - heads)
        part = z[:, n * HEAD_WIDTH : (n + 1) * HEAD_WIDTH]
        part = part * cosine + swapped(part) * sine
        if j < heads:
            q_ref[j] = (part.astype(LOW).astype(FULL) * scale).astype(LOW)
        else:
            k_ref[j - heads] = part.astype(LOW)
    for j in range(groups):
        v_ref[j] = zv[:, j * HEAD_WIDTH : (j + 1) * HEAD_WIDTH].astype(LOW)


def run_front(x, gain, weights, cosine, sine, heads, groups):
    length, width = x.shape
    tile = min(256, length)
    shape = jax.ShapeDtypeStruct
    fixed = lambda v: pl.BlockSpec(v.shape, lambda i: (0,) * v.ndim)
    strip = lambda columns: pl.BlockSpec((tile, columns), lambda i: (i, 0))
    of_heads = lambda n: pl.BlockSpec((n, tile, HEAD_WIDTH), lambda i: (0, i, 0))
    return pl.pallas_call(
        functools.partial(front_body, heads, groups),
        grid=(length // tile,),
        out_shape=[
            shape((length, width), LOW),
            shape((heads, length, HEAD_WIDTH), LOW),
            shape((groups, length, HEAD_WIDTH), LOW),
            shape((groups, length, HEAD_WIDTH), LOW),
            shape((length, 1), FULL),
        ],
        in_specs=[strip(width), fixed(gain)]
        + [fixed(w) for w in weights]
        + [strip(HEAD_WIDTH), strip(HEAD_WIDTH)],
        out_specs=[strip(width), of_heads(heads), of_heads(groups), of_heads(groups), strip(1)],
        compiler_params=pltpu.CompilerParams(vmem_limit_bytes=VMEM_GRANT),
        cost_estimate=cost_of(8 * length * width * width, 12 * length * width),
        name="front",
    )(x, gain, *weights, cosine, sine)


def add_body(count, *refs):
    for i in range(count):
        total = refs[2 * i][...].astype(FULL) + refs[2 * i + 1][...].astype(FULL)
        refs[2 * count + i][...] = total.astype(LOW)


def run_adds(pairs):
    rows, width = pairs[0][0].shape
    tile = rows // 2
    count = len(pairs)
    block = pl.BlockSpec((tile, width), lambda i: (i, 0))
    specs, values = [], []
    for one in pairs:
        offset = one[2] // tile if len(one) > 2 else 0
        specs += [block, pl.BlockSpec((tile, width), lambda i, offset=offset: (i + offset, 0))]
        values += one[:2]
    return list(
        pl.pallas_call(
            functools.partial(add_body, count),
            grid=(rows // tile,),
            out_shape=[jax.ShapeDtypeStruct((rows, width), LOW)] * count,
            in_specs=specs,
            out_specs=[block] * count,
            compiler_params=pltpu.CompilerParams(vmem_limit_bytes=20 * 1024 * 1024),
            cost_estimate=cost_of(1000, 6 * count * rows * width),
            name="adds",
        )(*values)
    )


def attention_body(heads, groups, rows, tile, mine_ref, q_ref, k_ref, v_ref, wo_ref, column_ref,
                   row_ref, mix_ref, lse_ref, *rest):
    part_refs, (turned_ref, out_ref) = rest[:-2], rest[-2:]
    length = row_ref.shape[1]
    size = heads // groups
    for j in range(groups):
        turned_ref[j] = v_ref[j].astype(FULL).T.astype(LOW)

    for group in range(groups):
        for start, keys in tiles_of(length, tile):
            visible = column_ref[0:keys, :] <= row_ref[:, start : start + tile]

            @pl.loop(group * size, (group + 1) * size)
            def _(head, group=group, start=start, keys=keys, visible=visible):
                s = mul(k_ref[group, 0:keys, :], q_ref[head, start : start + tile, :], NT)
                s = jnp.where(visible, s, NEGATIVE)
                peak = jnp.max(s, axis=0, keepdims=True)
                p = jnp.exp(s - peak)
                total = jnp.sum(p, axis=0, keepdims=True)
                lse_ref[head, :, start : start + tile] = peak + jnp.log(total)
                o = mul(turned_ref[group, :, 0:keys], p.astype(LOW)) / total
                out_ref[head, start : start + tile, :] = o.T.astype(LOW)

    for head in range(heads):
        mix_ref[:, head * HEAD_WIDTH : (head + 1) * HEAD_WIDTH] = out_ref[head]
    for r, part_ref in enumerate(part_refs):
        at = pl.ds(pl.multiple_of((mine_ref[0] ^ r) * rows, rows), rows)
        part_ref[...] = mul(mix_ref[at, :], wo_ref[...]).astype(part_ref.dtype)


def run_attention(mine, q, k, v, output_weight, column, row, count):
    heads, length, _ = q.shape
    groups = k.shape[0]
    width = output_weight.shape[1]
    rows = length // count
    shape = jax.ShapeDtypeStruct
    results = pl.pallas_call(
        functools.partial(attention_body, heads, groups, rows, min(2 * TILE, length)),
        grid=(1,),
        out_shape=[
            shape((length, heads * HEAD_WIDTH), LOW),
            shape((heads, 1, length), FULL),
        ]
        + [shape((rows, width), LOW)] * count,
        in_specs=[pl.BlockSpec(memory_space=pltpu.SMEM)]
        + [entire(v.shape) for v in (q, k, v, output_weight, column, row)],
        out_specs=[entire((length, heads * HEAD_WIDTH)), entire((heads, 1, length))]
        + [entire((rows, width))] * count,
        scratch_shapes=[
            pltpu.VMEM((groups, HEAD_WIDTH, length), LOW),
            pltpu.VMEM((heads, length, HEAD_WIDTH), LOW),
        ],
        compiler_params=pltpu.CompilerParams(vmem_limit_bytes=VMEM_GRANT),
        cost_estimate=cost_of(12 * length * width * width, 12 * length * width),
        name="attention",
    )(mine, q, k, v, output_weight, column, row)
    return results[0], results[1], list(results[2:])


def back_body(count, group, size, rows, tile, split, mine_ref, *rest):
    da_refs = rest[:count]
    (h_in, wo_ref, mix_ref, q_ref, k_ref, v_ref, lse_ref, column_ref, row_ref, cos_ref, sin_ref,
     d_ref, *outs, da_ref, h_ref, do_ref, turned_ref, dk_ref, dv_ref, dq_ref,
     square_ref, landed) = rest[count:]
    length = row_ref.shape[1]
    scale = HEAD_WIDTH ** (-0.5)
    first = group * size
    loads = []
    for r in range(count):
        at = pl.ds(pl.multiple_of((mine_ref[0] ^ r) * rows, rows), rows)
        load = pltpu.make_async_copy(da_refs[r], da_ref.at[at], landed.at[r])
        load.start()
        loads.append(load)
    late = pltpu.make_async_copy(h_in, h_ref, landed.at[count])
    late.start()
    turned_ref[...] = k_ref[group].astype(FULL).T.astype(LOW)
    dk_ref[...] = jnp.zeros(dk_ref.shape, FULL)
    dv_ref[...] = jnp.zeros(dv_ref.shape, FULL)
    for load in loads:
        load.wait()
    span = slice(first * HEAD_WIDTH, (first + size) * HEAD_WIDTH)

    @pl.loop(0, length // tile)
    def _(i):
        at = pl.ds(pl.multiple_of(i * tile, tile), tile)
        z = mul(da_ref[at, :], wo_ref[span, :], NT).astype(LOW)
        for j in range(size):
            do_ref[j, at, :] = z[:, j * HEAD_WIDTH : (j + 1) * HEAD_WIDTH]

    for start, keys in tiles_of(length, tile):
        visible = column_ref[0:keys, :] <= row_ref[:, start : start + tile]
        cosine, sine = cos_ref[start : start + tile, :], sin_ref[start : start + tile, :]

        @pl.loop(0, size)
        def _(head, start=start, keys=keys, visible=visible, cosine=cosine, sine=sine):
            q = q_ref[first + head, start : start + tile, :]
            do = do_ref[head, start : start + tile, :]
            s = mul(k_ref[group, 0:keys, :], q, NT)
            p = jnp.where(visible, jnp.exp(s - lse_ref[first + head, :, start : start + tile]), 0.0)
            dp = mul(v_ref[group, 0:keys, :], do, NT)
            delta = jnp.sum(p * dp, axis=0, keepdims=True)
            ds = (p * (dp - delta)).astype(LOW)
            dv_ref[0:keys, :] += mul(p.astype(LOW), do)
            dk_ref[0:keys, :] += mul(ds, q)
            dq = mul(turned_ref[:, 0:keys], ds).T * scale
            dq = dq * cosine - swapped(dq) * sine
            dq_ref[head, start : start + tile, :] = dq.astype(LOW)

    for head in range(size):
        d_ref[:, head * HEAD_WIDTH : (head + 1) * HEAD_WIDTH] = dq_ref[head]
    dk = dk_ref[...]
    dk = dk * cos_ref[...] - swapped(dk) * sin_ref[...]
    d_ref[:, size * HEAD_WIDTH : (size + 1) * HEAD_WIDTH] = dk.astype(LOW)
    d_ref[:, (size + 1) * HEAD_WIDTH :] = dv_ref[...].astype(LOW)
    late.wait()
    depth = (size + 2) * HEAD_WIDTH
    square_ref[0:depth, :] = mul(d_ref[...], h_ref[...], TN)
    square_ref[depth:, :] = mul(mix_ref[:, span], da_ref[...], TN)
    if not split:
        outs[0][...] = square_ref[...].astype(LOW)
        return
    keep_ref, send_ref = outs
    half = keep_ref.shape[0]
    for side in range(2):

        @pl.when(mine_ref[1] == side)
        def _(side=side):
            keep_ref[...] = square_ref[side * half : (side + 1) * half, :]
            send_ref[0:half, :] = square_ref[(1 - side) * half : (2 - side) * half, :].astype(LOW)

    send_ref[half:, :] = jnp.zeros((EXTRA, send_ref.shape[1]), LOW)


def run_back(group, split, mine, da, hidden, output_weight, mixture, q, k, v, lse, column, row, cosine, sine):
    heads, length, _ = q.shape
    groups = k.shape[0]
    size = heads // groups
    rows, width = da[0].shape
    count = len(da)
    half = (size + 1) * HEAD_WIDTH
    shape = jax.ShapeDtypeStruct
    return pl.pallas_call(
        functools.partial(back_body, count, group, size, rows, min(TILE, length), split),
        grid=(1,),
        out_shape=[
            shape((length, (size + 2) * HEAD_WIDTH), LOW),
        ]
        + (
            [shape((half, width), FULL), shape((half + EXTRA, width), LOW)]
            if split
            else [shape((2 * half, width), LOW)]
        ),
        in_specs=[pl.BlockSpec(memory_space=pltpu.SMEM)]
        + [pl.BlockSpec(memory_space=pltpu.HBM)] * (count + 1)
        + [
            entire(v.shape)
            for v in (output_weight, mixture, q, k, v, lse, column, row, cosine, sine)
        ],
        out_specs=[entire((length, (size + 2) * HEAD_WIDTH))]
        + (
            [entire((half, width)), entire((half + EXTRA, width))]
            if split
            else [entire((2 * half, width))]
        ),
        scratch_shapes=[
            pltpu.VMEM((length, width), LOW),
            pltpu.VMEM((length, width), LOW),
            pltpu.VMEM((size, length, HEAD_WIDTH), LOW),
            pltpu.VMEM((HEAD_WIDTH, length), LOW),
            pltpu.VMEM((length, HEAD_WIDTH), FULL),
            pltpu.VMEM((length, HEAD_WIDTH), FULL),
            pltpu.VMEM((size, length, HEAD_WIDTH), LOW),
            pltpu.VMEM((2 * half, width), FULL),
            pltpu.SemaphoreType.DMA((count + 1,)),
        ],
        compiler_params=pltpu.CompilerParams(vmem_limit_bytes=VMEM_GRANT),
        cost_estimate=cost_of(8 * length * width * width, 12 * length * width),
        name="back",
    )(mine, *da, hidden, output_weight, mixture, q, k, v, lse, column, row, cosine, sine)


def first_body(groups, count, mine_ref, x_ref, inverse_ref, *rest):
    d_refs, w_refs = rest[:groups], rest[groups : 2 * groups]
    keep_ref, send_ref, gain_ref, sum_ref = rest[2 * groups :]
    d_first = mul(d_refs[0][...], w_refs[0][...], NT)
    for d_ref, w_ref in zip(d_refs[1:], w_refs[1:]):
        d_first = d_first + mul(d_ref[...], w_ref[...], NT)
    sum_ref[...] = d_first
    normed = x_ref[...].astype(FULL) * inverse_ref[...]
    gain_ref[...] = jnp.sum(d_first * normed, axis=0, keepdims=True)
    rows = sum_ref.shape[0] // count
    for r in range(count):
        at = pl.ds(pl.multiple_of((mine_ref[0] ^ r) * rows, rows), rows)
        target = send_ref if r % 2 else keep_ref
        target[r // 2 * rows : (r // 2 + 1) * rows, :] = sum_ref[at, :].astype(target.dtype)


def run_first(mine, x, inverse, d_projected, weights, count):
    length, width = x.shape
    groups = len(weights)
    depth = weights[0].shape[1]
    tile = 256
    down = lambda n: pl.BlockSpec((n, tile), lambda i: (0, i))
    return pl.pallas_call(
        functools.partial(first_body, groups, count),
        grid=(width // tile,),
        in_specs=[pl.BlockSpec(memory_space=pltpu.SMEM), down(length), entire((length, 1))]
        + [entire((length, depth))] * groups
        + [pl.BlockSpec((tile, depth), lambda i: (i, 0))] * groups,
        out_specs=[down(length // 2), down(length // 2), down(1)],
        out_shape=[
            jax.ShapeDtypeStruct((length // 2, width), FULL),
            jax.ShapeDtypeStruct((length // 2, width), LOW),
            jax.ShapeDtypeStruct((1, width), FULL),
        ],
        scratch_shapes=[pltpu.VMEM((length, tile), FULL)],
        compiler_params=pltpu.CompilerParams(vmem_limit_bytes=VMEM_GRANT),
        cost_estimate=cost_of(1000, 1000),
        name="first_gradients",
    )(mine, x, inverse, *d_projected, *weights)


def token_body(num_experts, came_ref, own_ref, h_ref, router_ref, code_ref, mid_ref, gain_ref,
               g_ref, mid_out, low_out, gain_out, router_out):
    width = h_ref.shape[1]
    total = came_ref[...].astype(FULL) + own_ref[...].astype(FULL)
    d_gates = jnp.zeros(code_ref.shape, FULL)
    for n in range(3):
        tile, turn = divmod(n * num_experts, LANES)
        part = total[:, width + tile * LANES : width + (tile + 1) * LANES]
        d_gates = d_gates + (pltpu.roll(part, LANES - turn, 1) if turn else part)
    h = h_ref[...]
    code = code_ref[...]
    logits = mul(h, router_ref[...])
    picked = code > 0.5
    peak = jnp.max(jnp.where(picked, logits, NEGATIVE), axis=1, keepdims=True)
    exponent = jnp.where(picked, jnp.exp(logits - peak), 0.0)
    gates = exponent / jnp.sum(exponent, axis=1, keepdims=True)
    d_gates = jnp.where(code > 1.5, d_gates, 0.0)
    d_logits = gates * (d_gates - jnp.sum(gates * d_gates, axis=1, keepdims=True))
    d_logits = d_logits.astype(LOW)
    d_hidden = total[:, :width] + mul(d_logits, router_ref[...], NT)
    router_out[...] = mul(d_logits, h, TN)[:num_experts]
    mid = mid_ref[...]
    inverse = normalized(mid)
    normed = mid * inverse
    gain_out[...] = jnp.sum(d_hidden * normed, axis=0, keepdims=True)
    scaled = d_hidden * gain_ref[...]
    d_mid = g_ref[...].astype(FULL) + inverse * (
        scaled - normed * jnp.mean(scaled * normed, axis=1, keepdims=True)
    )
    mid_out[...] = d_mid
    low_out[...] = d_mid.astype(LOW)


def run_token(came, own, h, router, code, mid, gain, g, num_experts):
    rows, width = h.shape
    values = (came, own, h, router, code, mid, gain, g)
    shape = jax.ShapeDtypeStruct
    outs = ((rows, width), FULL), ((rows, width), LOW), ((1, width), FULL), ((num_experts, width), FULL)
    return pl.pallas_call(
        functools.partial(token_body, num_experts),
        grid=(1,),
        in_specs=[entire(v.shape) for v in values],
        out_specs=[entire(size) for size, _ in outs],
        out_shape=[shape(size, kind) for size, kind in outs],
        compiler_params=pltpu.CompilerParams(vmem_limit_bytes=28 * 1024 * 1024),
        cost_estimate=cost_of(1000, 1000),
        name="token_gradients",
    )(*values)


def finish_body(size, groups, split, mine_ref, *refs):
    count = 2 * groups if split else groups
    q_ref, k_ref, v_ref, o_ref = refs[count : count + 4]
    if split:
        half = refs[0].shape[0]
        wholes = refs[count + 4 :]
        for n in range(groups):
            for k in range(split):
                block = lax.rem(mine_ref[2] + split - k, split)
                for j, side in enumerate((mine_ref[1], 1 - mine_ref[1])):
                    start = pl.multiple_of(side * half + block * (half // split), half // split)
                    wholes[n][pl.ds(start, half // split), :] = refs[2 * n + j][
                        k * (half // split) : (k + 1) * (half // split), :
                    ]

    else:
        wholes = refs[:groups]
    cut = size * HEAD_WIDTH
    spans = ((q_ref, 0, cut), (k_ref, cut, cut + HEAD_WIDTH), (v_ref, cut + HEAD_WIDTH, cut + 2 * HEAD_WIDTH))
    for ref, start, end in spans:
        ref[...] = jnp.concatenate([w[start:end, :].astype(FULL) for w in wholes]).T
    end = cut + 2 * HEAD_WIDTH
    for i, w in enumerate(wholes):
        o_ref[i * cut : (i + 1) * cut, :] = w[end:, :].astype(FULL)


def run_finish(mine, wholes, size, halves=None, split=0):
    values = wholes if halves is None else [v for pair_of in halves for v in pair_of]
    groups = len(wholes if halves is None else halves)
    depth, width = values[0].shape
    tile = 256
    heads = size * groups * HEAD_WIDTH
    down = lambda n: pl.BlockSpec((tile, n), lambda i: (i, 0))
    along = lambda n: pl.BlockSpec((n, tile), lambda i: (0, i))
    shape = jax.ShapeDtypeStruct
    return pl.pallas_call(
        functools.partial(finish_body, size, groups, split),
        grid=(width // tile,),
        in_specs=[pl.BlockSpec(memory_space=pltpu.SMEM)] + [along(depth)] * len(values),
        out_specs=[down(heads), down(groups * HEAD_WIDTH), down(groups * HEAD_WIDTH), along(heads)],
        out_shape=[
            shape((width, heads), FULL),
            shape((width, groups * HEAD_WIDTH), FULL),
            shape((width, groups * HEAD_WIDTH), FULL),
            shape((heads, width), FULL),
        ],
        scratch_shapes=[]
        if halves is None
        else [pltpu.VMEM((2 * depth, tile), LOW)] * groups,
        compiler_params=pltpu.CompilerParams(vmem_limit_bytes=24 * 1024 * 1024),
        cost_estimate=cost_of(1000, 1000),
        name="finish",
    )(mine, *values)


def place_body(rows, mine_ref, *refs):
    for r, ref in enumerate(refs[:-1]):
        at = pl.ds(pl.multiple_of((mine_ref[0] ^ r) * rows, rows), rows)
        refs[-1][at, :] = ref[0:rows, :].astype(refs[-1].dtype)


def run_place(mine, blocks, kind):
    rows, width = blocks[0].shape
    whole = pl.BlockSpec(memory_space=pltpu.VMEM)
    return pl.pallas_call(
        functools.partial(place_body, rows),
        out_shape=jax.ShapeDtypeStruct((len(blocks) * rows, width), kind),
        in_specs=[pl.BlockSpec(memory_space=pltpu.SMEM)] + [whole] * len(blocks),
        out_specs=whole,
        compiler_params=pltpu.CompilerParams(vmem_limit_bytes=24 * 1024 * 1024),
        cost_estimate=cost_of(1000, 10 * len(blocks) * rows * width),
        name="place",
    )(mine, *blocks)


def gate_columns(num_experts):
    return -(-3 * num_experts // LANES) * LANES


def expert_body(places, block_count, local, hidden, row_tile, column_tile, num_experts, more,
                columns_ref, router_ref, *rest):
    rest = list(rest)
    take = lambda n: [rest.pop(0) for _ in range(n)]
    shard_count = len(places)
    h_refs, g_refs = take(block_count), take(block_count)
    w_refs = [take(3) for _ in range(shard_count)]
    before = take(3 * block_count) if more else None
    y_outs, dh_outs, sum_outs = take(block_count), take(block_count), take(block_count)
    (hid_out,) = take(1)
    (h_ref, g_ref, hid_ref, first_buffer, second_buffer, code_ref, kept_ref, y_ref, dh_ref,
     sum_ref) = take(10)
    arrived, landed, left = rest
    wide = local * hidden
    first = 2 * wide
    rows = h_refs[0].shape[0]
    total, width = h_ref.shape
    span = [pl.ds(i * rows, rows) for i in range(block_count)]

    def begin(source, target, flag):
        copy = pltpu.make_async_copy(source, target, flag)
        copy.start()
        return copy

    loads, olds = [], []
    for i in range(block_count):
        loads += [
            begin(h_refs[i], h_ref.at[span[i]], landed.at[i, 0]),
            begin(g_refs[i].at[:, pl.ds(0, width)], g_ref.at[span[i]], landed.at[i, 1]),
            begin(g_refs[i].at[:, pl.ds(width, LANES)], code_ref.at[span[i]], landed.at[i, 2]),
        ]
        if more:
            for j, target in enumerate((y_ref, dh_ref, sum_ref)):
                olds.append(
                    begin(before[j * block_count + i], target.at[span[i]], landed.at[i, 3 + j])
                )
    copies = []

    def fetch(s):
        targets = (
            first_buffer.at[pl.ds(s * first, wide)],
            first_buffer.at[pl.ds(s * first + wide, wide)],
            second_buffer.at[pl.ds(s * wide, wide)],
        )
        copies.append([begin(w_refs[s][j], targets[j], arrived.at[s, j]) for j in range(3)])

    for s in range(min(AHEAD, shard_count)):
        fetch(s)
    for load in loads:
        load.wait()

    def find_gates():
        code = code_ref[...].astype(FULL)
        logits = mul(h_ref[...], router_ref[...])
        picked = code > 0.5
        peak = jnp.max(jnp.where(picked, logits, NEGATIVE), axis=1, keepdims=True)
        exponent = jnp.where(picked, jnp.exp(logits - peak), 0.0)
        gates = exponent / jnp.sum(exponent, axis=1, keepdims=True)
        kept_ref[...] = jnp.where(code > 1.5, gates, 0.0).astype(LOW).astype(FULL)

    if more:
        for old in olds:
            old.wait()
    else:
        sum_ref[...] = jnp.zeros(sum_ref.shape, FULL)
    lane = lax.broadcasted_iota(jnp.int32, (row_tile, LANES), 1)
    owner = lax.broadcasted_iota(jnp.int32, (row_tile, wide), 1) // hidden
    for base in range(0, shard_count, BUNCH):
        bunch = range(base, min(base + BUNCH, shard_count))
        for s in bunch:
            for copy in copies[s]:
                copy.wait()
        for s in range(len(copies), min(base + len(bunch) + AHEAD, shard_count)):
            fetch(s)
        for i in range(total // row_tile):
            at = slice(i * row_tile, (i + 1) * row_tile)
            zs = mul(h_ref[at, :], first_buffer[base * first : (bunch[-1] + 1) * first, :], NT)
            qs = mul(g_ref[at, :], second_buffer[base * wide : (bunch[-1] + 1) * wide, :], NT)
            if base == 0 and i == 0:
                find_gates()
            kept = kept_ref[at, :]
            dgb = sum_ref[at, :]
            for n, s in enumerate(bunch):
                hits = [lane == columns_ref[local * places[s] + e] for e in range(local)]
                gate_of = jnp.zeros((row_tile, wide), FULL)
                for e in range(local):
                    own = jnp.sum(jnp.where(hits[e], kept, 0.0), axis=1, keepdims=True)
                    gate_of = jnp.where(owner == e, own, gate_of)
                gate = zs[:, n * first : n * first + wide]
                up = zs[:, n * first + wide : (n + 1) * first]
                q = qs[:, n * wide : (n + 1) * wide]
                sigmoid = jax.nn.sigmoid(gate)
                silu = gate * sigmoid
                act = silu * up
                d_act = q * gate_of
                start = s * first
                hid_ref[at, start : start + wide] = (
                    d_act * up * sigmoid * (1.0 + gate * (1.0 - sigmoid))
                ).astype(LOW)
                hid_ref[at, start + wide : start + first] = (d_act * silu).astype(LOW)
                start = shard_count * first + s * wide
                hid_ref[at, start : start + wide] = (act * gate_of).astype(LOW)
                product = act * q
                for e in range(local):
                    part = jnp.sum(jnp.where(owner == e, product, 0.0), axis=1, keepdims=True)
                    dgb = dgb + jnp.where(hits[e], part, 0.0)
            sum_ref[at, :] = dgb

    leaves = [begin(hid_ref, hid_out, left.at[0, 0])]
    rest_of = sum_ref[...]
    tiles = [jnp.zeros((total, LANES), FULL)] * (gate_columns(num_experts) // LANES)
    for n in range(3):
        piece = rest_of.astype(LOW).astype(FULL)
        rest_of = rest_of - piece
        tile, turn = divmod(n * num_experts, LANES)
        tiles[tile] = tiles[tile] + (pltpu.roll(piece, turn, 1) if turn else piece)
    for n, tile in enumerate(tiles):
        dh_ref[:, width + n * LANES : width + (n + 1) * LANES] = tile.astype(LOW)
    middle = shard_count * first
    for i in range(block_count):
        at = slice(i * rows, (i + 1) * rows)

        y = mul(hid_ref[at, middle:], second_buffer[...])
        if more:
            y = y + y_ref[at, :].astype(FULL)
        y_ref[at, :] = y.astype(LOW)
        leaves.append(begin(y_ref.at[span[i]], y_outs[i], left.at[1 + i, 0]))
        dh = mul(hid_ref[at, 0:middle], first_buffer[...])
        if more:
            dh = dh + dh_ref[at, 0:width].astype(FULL)
        dh_ref[at, 0:width] = dh.astype(LOW)
        leaves += [
            begin(dh_ref.at[span[i]], dh_outs[i], left.at[1 + i, 1]),
            begin(sum_ref.at[span[i]], sum_outs[i], left.at[1 + i, 2]),
        ]
    for leave in leaves:
        leave.wait()


def run_experts(columns, router, h, g, weights, places, local, hidden, num_experts, before=None):
    count, blocks = len(weights), len(h)
    rows, width = h[0].shape
    wide = local * hidden
    depth = 3 * wide
    total = blocks * rows
    wider = width + gate_columns(num_experts)
    whole = pl.BlockSpec(memory_space=pltpu.VMEM)
    away = pl.BlockSpec(memory_space=pltpu.HBM)
    shape = jax.ShapeDtypeStruct
    extra = [] if before is None else before[0] + before[1] + before[2]
    results = pl.pallas_call(
        functools.partial(
            expert_body, tuple(places), blocks, local, hidden, total // -(-total // 256), width,
            num_experts, bool(extra),
        ),
        out_shape=[shape((rows, width), LOW)] * blocks
        + [shape((rows, wider), LOW)] * blocks
        + [shape((rows, LANES), FULL)] * blocks
        + [shape((total, count * depth), LOW)],
        in_specs=[pl.BlockSpec(memory_space=pltpu.SMEM), whole]
        + [away] * (2 * blocks + 3 * count + len(extra)),
        out_specs=[away] * (3 * blocks + 1),
        scratch_shapes=[
            pltpu.VMEM((total, width), LOW),
            pltpu.VMEM((total, width), LOW),
            pltpu.VMEM((total, count * depth), LOW),
            pltpu.VMEM((count * 2 * wide, width), LOW),
            pltpu.VMEM((count * wide, width), LOW),
            pltpu.VMEM((total, LANES), LOW),
            pltpu.VMEM((total, LANES), FULL),
            pltpu.VMEM((total, width), LOW),
            pltpu.VMEM((total, wider), LOW),
            pltpu.VMEM((total, LANES), FULL),
            pltpu.SemaphoreType.DMA((count, 3)),
            pltpu.SemaphoreType.DMA((blocks, 6)),
            pltpu.SemaphoreType.DMA((blocks + 1, 3)),
        ],
        compiler_params=pltpu.CompilerParams(
            vmem_limit_bytes=VMEM_GRANT
        ),
        cost_estimate=cost_of(4 * total * width * depth * count, depth * width * count * 2),
        name="experts",
    )(columns, router, *h, *g, *[piece for shard in weights for piece in shard], *extra)
    return (
        list(results[:blocks]),
        list(results[blocks : 2 * blocks]),
        list(results[2 * blocks : 3 * blocks]),
        results[-1],
    )


def weight_body(plan, rows, wide, *rest):
    rest = list(rest)
    take = lambda n: [rest.pop(0) for _ in range(n)]
    blocks = plan[0][1]
    shards_plan = plan[1]
    h_refs, g_refs = take(blocks), take(blocks)
    hid_refs = take(plan[0][0])
    stay = len(shards_plan) // 2
    out_refs = [take(3) for _ in range(stay)]
    loose = plan[2]
    away_refs = take(3 * loose + stay - loose)
    h_ref, g_ref, first_ref, second_ref, out_buffer, landed, arrived, left = rest
    loads = []
    for i in range(blocks):
        at = pl.ds(i * rows, rows)
        sources = (h_refs[i], g_refs[i].at[:, pl.ds(0, h_ref.shape[1])])
        for j, (source, target) in enumerate(zip(sources, (h_ref, g_ref))):
            load = pltpu.make_async_copy(source, target.at[at], landed.at[i, j])
            load.start()
            loads.append(load)

    def fetch(s):
        slot = s % 2
        group = []
        for n, (hid, first, second, start, count) in enumerate(shards_plan[s]):
            at = pl.ds(start, count)
            group.append(
                pltpu.make_async_copy(
                    hid_refs[hid].at[:, pl.ds(first, 2 * wide)],
                    first_ref.at[slot, at],
                    arrived.at[slot, n, 0],
                )
            )
            group.append(
                pltpu.make_async_copy(
                    hid_refs[hid].at[:, pl.ds(second, wide)],
                    second_ref.at[slot, at],
                    arrived.at[slot, n, 1],
                )
            )
        for copy in group:
            copy.start()
        return group

    waiting = fetch(0)
    leaves = []
    for load in loads:
        load.wait()
    for s in range(len(shards_plan)):
        following = fetch(s + 1) if s + 1 < len(shards_plan) else None
        for copy in waiting:
            copy.wait()
        slot = s % 2
        sums = (
            lambda: mul(first_ref[slot, :, 0:wide], h_ref[...], TN),
            lambda: mul(first_ref[slot, :, wide:], h_ref[...], TN),
            lambda: mul(second_ref[slot], g_ref[...], TN),
        )
        for j in range(3):
            start = 3 * s + j
            out_buffer[start * wide : (start + 1) * wide, :] = sums[j]().astype(LOW)
            if s < stay:
                target = out_refs[s][j]
            elif s - stay < loose:
                target = away_refs[3 * (s - stay) + j]
            else:
                target = away_refs[s - stay + 2 * loose].at[pl.ds(j * wide, wide)]
            leave = pltpu.make_async_copy(
                out_buffer.at[pl.ds(start * wide, wide)], target, left.at[start]
            )
            leave.start()
            leaves.append(leave)
        waiting = following
    for leave in leaves:
        leave.wait()


def run_weights(h, g, hids, shards_plan, wide, loose=0):
    blocks = len(h)
    rows, width = h[0].shape
    total = blocks * rows
    stay = len(shards_plan) // 2
    pieces = max(len(p) for p in shards_plan)
    away = pl.BlockSpec(memory_space=pltpu.HBM)
    plan = ((len(hids), blocks), tuple(tuple(p) for p in shards_plan), loose)
    results = pl.pallas_call(
        functools.partial(weight_body, plan, rows, wide),
        out_shape=[jax.ShapeDtypeStruct((wide, width), LOW)] * (3 * stay)
        + [jax.ShapeDtypeStruct((wide, width), LOW)] * (3 * loose)
        + [jax.ShapeDtypeStruct((3 * wide, width), LOW)] * (stay - loose),
        in_specs=[away] * (2 * blocks + len(hids)),
        out_specs=[away] * (4 * stay + 2 * loose),
        scratch_shapes=[
            pltpu.VMEM((total, width), LOW),
            pltpu.VMEM((total, width), LOW),
            pltpu.VMEM((2, total, 2 * wide), LOW),
            pltpu.VMEM((2, total, wide), LOW),
            pltpu.VMEM((6 * stay * wide, width), LOW),
            pltpu.SemaphoreType.DMA((blocks, 2)),
            pltpu.SemaphoreType.DMA((2, pieces, 2)),
            pltpu.SemaphoreType.DMA((6 * stay,)),
        ],
        compiler_params=pltpu.CompilerParams(vmem_limit_bytes=VMEM_GRANT),
        cost_estimate=cost_of(12 * total * width * wide * stay, total * 6 * wide * stay * 2),
        name="weight_gradients",
    )(*h, *g, *hids)
    chips = []
    for i in range(stay):
        start = 3 * (stay + i)
        other = list(results[start : start + 3]) if i < loose else results[3 * stay + 2 * loose + i]
        chips += [list(results[3 * i : 3 * i + 3]), other]
    return chips


def swap(values, axis, bit):
    count = lax.axis_size(axis)
    return lax.ppermute(values, axis, [(i, i ^ bit) for i in range(count)])


def pair(values):
    return swap(values, "expert", 1)


def ring(values):
    count = lax.axis_size("expert")
    return lax.ppermute(values, "expert", [(i, (i + 2) % count) for i in range(count)])


def pick(values, index):
    return lax.dynamic_index_in_dim(values, index, 0, keepdims=False)


def ring_gather(block):
    blocks = [block]
    for _ in range(lax.axis_size("expert") // 2 - 1):
        blocks.append(ring(blocks[-1]))
    return blocks


def ring_partial(blocks):
    running = blocks[1]
    for k in range(2, len(blocks) + 1):
        running = ring(running.astype(LOW))
        if k < len(blocks):
            running = running.astype(FULL) + blocks[k].astype(FULL)
    return running


def ring_sum(blocks):
    return ring_partial(blocks).astype(FULL) + blocks[0].astype(FULL)


def bits_of(count):
    return [1 << i for i in range(count.bit_length() - 1)]


def parts_sum(parts):
    parts = list(parts)
    for bit in bits_of(len(parts)):
        for r in reversed(range(0, len(parts), 2 * bit)):
            other = swap(parts[r + bit].astype(LOW), "tensor", bit)
            parts[r] = parts[r].astype(FULL) + other.astype(FULL)
    return parts[0]


def tensor_blocks(own):
    count = lax.axis_size("tensor")
    blocks = [own] * count
    for bit in reversed(bits_of(count)):
        for r in range(0, count, 2 * bit):
            blocks[r + bit] = swap(blocks[r], "tensor", bit)
    return blocks


def total_of(parts):
    return sum(part.astype(FULL) for part in parts)


def laid_z(blocks):
    size = len(blocks)
    place = lax.axis_index("expert") // 2
    whole = jnp.zeros((size,) + blocks[0].shape, blocks[0].dtype)
    for k, block in enumerate(blocks):
        whole = lax.dynamic_update_index_in_dim(whole, block, (place - k) % size, 0)
    return whole.reshape((-1,) + blocks[0].shape[1:])


def joined(half, other):
    low = lax.axis_index("expert") % 2 == 0
    return jnp.concatenate([jnp.where(low, half, other), jnp.where(low, other, half)])


def sum_everywhere(values):
    for axis in ("tensor", "expert"):
        for bit in bits_of(lax.axis_size(axis)):
            values = values + swap(values, axis, bit)
    return values


def shift(block, steps):
    count = lax.axis_size("expert")
    return lax.ppermute(block, "expert", [(i, (i + 2 * steps) % count) for i in range(count)])


def spread(block):
    return [block] + [shift(block, k) for k in range(1, lax.axis_size("expert") // 2)]


def with_cores(chips):
    shards_of = []
    for chip in chips:
        shards_of += [chip, [swap(piece, "tensor", 1) for piece in chip]]
    return shards_of


def gather_weights(own):
    near, far = [own], [[pair(piece) for piece in own]]
    for bit in bits_of(lax.axis_size("tensor"))[1:]:
        for i in range(len(near)):
            near.append([swap(piece, "tensor", bit) for piece in near[i]])
            far.append(
                [
                    pair(near[-1][0]),
                    swap(far[i][1], "tensor", bit),
                    pair(near[-1][2]),
                ]
            )
    return near, far


def scatter_weights(parts):
    full = lambda v: v.astype(FULL)
    sums = [[full(piece) for piece in chip] for chip in parts]
    near, far = sums[: len(sums) // 2], sums[len(sums) // 2 :]
    for bit in reversed(bits_of(lax.axis_size("tensor"))[1:]):
        count = len(near) // 2
        across = lambda v: full(swap(v.astype(LOW), "tensor", bit))
        beside = lambda v: full(pair(v.astype(LOW)))
        for i in range(count):
            last_near, last_far = near[count + i], far[count + i]
            last_near = [
                last_near[0] + beside(last_far[0]),
                last_near[1],
                last_near[2] + beside(last_far[2]),
            ]
            far[i] = [far[i][0], far[i][1] + across(last_far[1]), far[i][2]]
            near[i] = [one + across(two) for one, two in zip(near[i], last_near)]
        near, far = near[:count], far[:count]
    return [own + full(pair(other.astype(LOW))) for own, other in zip(near[0], far[0])]


def shards(
    activations,
    cotangent,
    block_ids,
    expert_ids,
    route_ranks,
    attention_gain,
    query_weight,
    key_matrix,
    value_matrix,
    output_weight,
    mixture_gain,
    router_weight,
    expert_gate,
    expert_up,
    expert_down,
):
    sequence_length, width = activations.shape
    heads = query_weight.shape[1] // HEAD_WIDTH
    groups = key_matrix.shape[1] // HEAD_WIDTH
    tensor_count = lax.axis_size("tensor")
    expert_count = lax.axis_size("expert")
    tensor_index = lax.axis_index("tensor")
    expert_index = lax.axis_index("expert")
    num_experts = router_weight.shape[1]
    local, _, hidden = expert_gate.shape
    picks = expert_ids.shape[1]
    capacity = sequence_length * picks // num_experts
    rows = sequence_length // tensor_count
    ring_size = expert_count // 2
    row_offset = tensor_index * rows
    own_rows = lambda v: lax.dynamic_slice_in_dim(v, row_offset, rows, 0)
    wide = local * hidden

    down = expert_down.reshape(wide, width)
    gate = expert_gate.transpose(0, 2, 1).reshape(wide, width)
    up = expert_up.transpose(0, 2, 1).reshape(wide, width)
    cotangent_own = own_rows(cotangent)
    ids_own, ranks_own = own_rows(expert_ids), own_rows(route_ranks)
    expert_range = jnp.arange(LANES, dtype=jnp.int32)
    pair_code = jnp.where(ranks_own < capacity, 2.0, 1.0)
    code = jnp.zeros((rows, LANES), FULL)
    for j in range(picks):
        code = code + jnp.where(
            ids_own[:, j, None] == expert_range[None, :], pair_code[:, j, None], 0.0
        )
    cosine, sine = rope_tables(sequence_length)
    gain_first = attention_gain.astype(FULL)[None]
    mine = jnp.stack([tensor_index, expert_index % 2, expert_index // 2]).astype(jnp.int32)
    row = block_ids
    column = block_ids.reshape(sequence_length, 1)
    fine = tensor_count == 4 and ring_size == 4
    x_in = activations
    across = lambda v: swap(v, "tensor", 2)
    sent = jnp.concatenate([cotangent_own, code.astype(LOW)], axis=1)
    x_own = own_rows(activations)
    core = lambda v: swap(v, "tensor", 1)
    if fine:
        sent = tie(sent)[0]
        moved = [pair(down), across(down), ring(sent), core(down)]
    hidden_first, q, k, v, inverse_first = run_front(
        x_in, gain_first, (query_weight, key_matrix, value_matrix), cosine, sine, heads, groups
    )
    if fine:
        moved, hidden_first, q, k, v, gate, up, x_own, column = tie(
            moved, hidden_first, q, k, v, gate, up, x_own, column
        )
        down_x, down_y, g_1, down_c = moved
        moved = [pair(gate), across(gate), ring(g_1), core(down_x), core(up)]
    mixture, lse, parts = run_attention(mine, q, k, v, output_weight, column, row, tensor_count)
    if fine:
        moved, mixture, lse, parts, up = tie(moved, mixture, lse, parts, up)
        gate_x, gate_y, g_2, down_xc, up_c = moved
        parts = tie(parts[0], parts[2], core(parts[3]), core(parts[1]))
        to_send = (parts[1].astype(FULL) + parts[2].astype(FULL)).astype(LOW)
        attention_out = parts[0].astype(FULL) + parts[3].astype(FULL)
        to_send, attention_out, up, g_2, gate_x, down_y, gate = tie(
            to_send, attention_out, up, g_2, gate_x, down_y, gate
        )
        moved = [across(to_send), pair(up), ring(g_2), core(gate_x), core(gate)]
        moved, gate_y, down_y = tie(moved, gate_y, down_y)
        attention_out = attention_out + moved[0].astype(FULL)
        up_x, g_3, gate_xc, gate_c = moved[1:]
        g = [sent, g_1, g_2, g_3]
    else:
        attention_out = parts_sum(parts)

    gain_second = mixture_gain.astype(FULL)
    residual_mid = x_own.astype(FULL) + attention_out
    inverse_second = normalized(residual_mid)
    normed_second = residual_mid * inverse_second
    hidden_second = (normed_second * gain_second).astype(LOW)

    router_wide = jnp.pad(router_weight, ((0, 0), (0, LANES - num_experts)))
    columns = jnp.concatenate(
        [
            expert_index * local + jnp.arange(local, dtype=jnp.int32),
            (expert_index ^ 1) * local + jnp.arange(local, dtype=jnp.int32),
        ]
    ).astype(jnp.int32)
    experts = lambda h, g, weights, places, before=None: run_experts(
        columns, router_wide, h, g, weights, places, local, hidden, num_experts, before
    )
    first = 2 * wide
    low = lambda v: v.astype(LOW)
    full = lambda v: v.astype(FULL)

    def token_gradients(came, own):
        d_mid, d_a, grad_gain, grad_router = run_token(
            came, own, hidden_second, router_wide, code, residual_mid, gain_second[None],
            cotangent_own, num_experts,
        )
        return d_mid, d_a, jnp.concatenate([grad_gain, grad_router])

    back = lambda group, da, split=True: run_back(
        group, split, mine, da, hidden_first, output_weight, mixture, q, k, v, lse, column, row, cosine, sine
    )
    size = heads // groups
    cut = size * HEAD_WIDTH
    group_weights = [
        jnp.concatenate(
            [
                query_weight[:, i * cut : (i + 1) * cut],
                key_matrix[:, i * HEAD_WIDTH : (i + 1) * HEAD_WIDTH],
                value_matrix[:, i * HEAD_WIDTH : (i + 1) * HEAD_WIDTH],
            ],
            axis=1,
        )
        for i in range(groups)
    ]

    first_gradients = lambda d_projected: run_first(
        mine, activations, inverse_first, d_projected, group_weights, tensor_count
    )

    def input_rows(d_first, d_mid):
        values = full(x_own)
        inverse = normalized(values)
        normed = values * inverse
        scaled = d_first * gain_first
        return low(
            d_mid
            + inverse * (scaled - normed * jnp.mean(scaled * normed, axis=-1, keepdims=True))
        )

    if fine:
        h = [hidden_second]
        moved = [ring(h[0]), across(up), pair(down_y)]
        up_xc, gate_yc = core(up_x), core(gate_y)
        side = [
            [gate, up, down], [gate_c, up_c, down_c],
            [gate_x, up_x, down_x], [gate_xc, up_xc, down_xc],
        ]
        side_places = [0, 0, 1, 1]
        start = experts(h[:1], g[:1], side, side_places)
        moved, start, group_weights, gate_yc = tie(moved, start, group_weights, gate_yc)
        y_0, dh_0, dgb_0, hid_0 = start
        h.append(moved[0])
        up_y, down_far = moved[1:]

        moved = [ring(h[1]), across(gate_x), pair(up_y)]
        up_yc, down_yc = core(up_y), core(down_y)
        y_1, dh_1, dgb_1, hid_1 = experts(h[1:2], g[1:2], side, side_places)
        beside = [[gate_y, up_y, down_y], [gate_yc, up_yc, down_yc]]
        second = experts(
            h[:2], g[:2], beside, [0, 0], (y_0 + y_1, dh_0 + dh_1, dgb_0 + dgb_1)
        )
        moved, second, hid_1, down_far = tie(moved, second, hid_1, down_far)
        y_1, dh_1, dgb_1, hid_y = second
        h.append(moved[0])
        gate_far, up_far = moved[1:]

        moved = [ring(h[2])]
        gate_farc, up_farc, down_farc = core(gate_far), core(up_far), core(down_far)
        y_2, dh_2, dgb_2, hid_2 = experts(h[2:3], g[2:3], side + beside, side_places + [0, 0])
        distant = [[gate_far, up_far, down_far], [gate_farc, up_farc, down_farc]]
        third = experts(
            h[:3], g[:3], distant, [1, 1], (y_1 + y_2, dh_1 + dh_2, dgb_1 + dgb_2)
        )
        moved, third, hid_2, distant = tie(moved, third, hid_2, distant)
        y_parts, dh_parts, dgb_parts, hid_far = third
        h.append(moved[0])

        moved = ring(dh_parts[1])
        last = experts(h[3:], g[3:], side + beside + distant, side_places + [0, 0, 1, 1])
        moved, last = tie(moved, last)
        y, dh, _, hid_last = last
        y_parts, dh_parts = y_parts + y, dh_parts + dh

        (running,) = run_adds([(moved, dh_parts[2])])
        hids = [hid_0, hid_1, hid_y, hid_2, hid_far, hid_last]
        plan = []
        for s in range(8):
            place_of = lambda n, i: (i * first, n * first + i * wide)
            if s < 4:
                head = [(b, *place_of(4, s), b * rows, rows) for b in (0, 1)]
                head.append((3, *place_of(6, s), 2 * rows, rows))
            elif s < 6:
                head = [(2, *place_of(2, s - 4), 0, 2 * rows)]
                head.append((3, *place_of(6, s), 2 * rows, rows))
            else:
                head = [(4, *place_of(2, s - 6), 0, 3 * rows)]
            plan.append(head + [(5, *place_of(8, s), 3 * rows, rows)])
        weights_of = lambda which, loose=0: run_weights(
            h, g, hids, [plan[s] for s in which], wide, loose
        )
        take_all = lambda kept, other, start: [
            (piece, other, (start + i) * wide) for i, piece in enumerate(kept)
        ]
        running, hids = tie(running, hids)
        far, far_other, beside_kept, beside_other = weights_of([6, 4, 7, 5], 1)
        far_other = [core(v) for v in far_other]
        moved = ring(running)
        moved, far, far_other, beside_kept, beside_other = tie(
            moved, far, far_other, beside_kept, beside_other
        )

        (running,) = run_adds([(moved, dh_parts[3])])
        running, far, far_other, h = tie(running, far, far_other, h)
        far = run_adds(list(zip(far, far_other)))
        moved = [ring(running), pair(far[0]), across(far[1]), core(beside_other)]
        x_kept, x_other, own_kept, own_other = weights_of([2, 0, 3, 1])
        moved, x_kept, x_other, own_kept, own_other, beside_kept = tie(
            moved, x_kept, x_other, own_kept, own_other, beside_kept
        )
        running, moved_gate, moved_up, beside_other = moved
        d_mid, d_a, small = token_gradients(running, dh_parts[0])
        d_a, d_mid, small, y_run, moved_gate, moved_up, beside_other = tie(
            d_a, d_mid, small, y_parts[1], moved_gate, moved_up, beside_other
        )

        moved = [across(d_a), pair(far[2]), ring(y_run), core(d_a), core(x_other)]
        y_sum = run_adds(take_all(beside_kept, beside_other, 0))
        (y_sum[0],) = run_adds([(y_sum[0], moved_gate)])
        x_other = moved.pop()
        x_sum = run_adds(take_all(x_kept, x_other, 0))
        (x_sum[1],) = run_adds([(x_sum[1], moved_up)])
        moved, y_sum, x_sum = tie(moved, y_sum, x_sum)
        x_gate, x_up, x_down = x_sum
        da = [d_a, moved[3], moved[0]]
        moved_down, y_run = moved[1], moved[2]
        own_other, y_run, da_3 = tie(
            own_other, run_adds([(y_run, y_parts[2])])[0], core(da[2])
        )
        da.append(da_3)

        moved = [across(y_sum[0]), pair(x_gate), ring(y_run), core(own_other)]
        d_one, keep_one, send_one = back(0, da)
        moved, d_one, keep_one, send_one, da = tie(moved, d_one, keep_one, send_one, da)
        arrived_y, arrived_x, own_other = [moved[0]], [moved[1]], moved[3]
        y_down, y_run = run_adds([(y_sum[2], moved_down), (moved[2], y_parts[3])])
        y_down, x_up, y_run = tie(y_down, x_up, y_run)

        moved = [across(y_down), pair(send_one), ring(y_run), across(y_sum[1]), pair(x_up)]
        d_two, keep_two, send_two = back(1, da)
        d_keep, d_send, grad_gain_first = first_gradients([d_one, d_two])
        moved, d_keep, d_send, keep_two, send_two, grad_gain_first = tie(
            moved, d_keep, d_send, keep_two, send_two, grad_gain_first
        )
        arrived_y += [moved[0], moved[3]]
        arrived_x.append(moved[4])
        summed, from_one = moved[2], moved[1]
        extra = jnp.concatenate([small, grad_gain_first])
        send_two = lax.dynamic_update_slice(send_two, low(extra), (keep_two.shape[0], 0))
        d_other = core(d_send)
        to_send = low(d_keep[rows:] + full(d_other[rows:]))
        d_first = d_keep[:rows] + full(d_other[:rows])
        n = keep_two.shape[0]
        place = expert_index // 2

        def quarters(half):
            cuts = half.reshape(ring_size, n // ring_size, width)
            goes = [low(pick(cuts, (place + k) % ring_size)) for k in range(1, ring_size)]
            return pick(cuts, place), goes

        stay_one, go_one = quarters(keep_one + full(from_one[:n]))
        to_send, d_first, send_two, stay_one, go_one = tie(
            to_send, d_first, send_two, stay_one, go_one
        )

        moved = tie(
            across(to_send), pair(send_two), [shift(v, k + 1) for k, v in enumerate(go_one)]
        )
        d_in = input_rows(d_first + full(moved[0]), d_mid)
        stay_two, go_two = quarters(keep_two + full(moved[1][:n]))
        count = extra.shape[0]
        extra = extra + full(moved[1][n : n + count])
        wider = jnp.pad(low(extra), ((0, EXTRA - count), (0, 0)))
        go_two = [jnp.concatenate([v, wider]) for v in go_two]
        from_one = moved[2]
        d_in, go_two, stay_two, extra = tie(d_in, go_two, stay_two, extra)

        moved = [across(d_in), pair(x_down), [shift(v, k + 1) for k, v in enumerate(go_two)]]
        out_own = low(residual_mid + full(summed) + full(y_parts[0]))
        own_sum = run_adds(take_all(own_kept, own_other, 0))
        quarter_one = low(total_of([stay_one] + from_one))
        moved, out_own, own_sum, quarter_one = tie(moved, out_own, own_sum, quarter_one)
        arrived_x.append(moved[1])
        q = stay_two.shape[0]
        quarter_two = low(total_of([stay_two] + [v[:q] for v in moved[2]]))
        extra = total_of([extra] + [v[q : q + count] for v in moved[2]])
        out_more = jnp.concatenate([out_own, jnp.pad(low(extra), ((0, EXTRA - count), (0, 0)))])
        input_blocks = [d_in, core(d_in), moved[0], core(moved[0])]
        input_blocks, quarter_one, quarter_two, extra, out_more, arrived_x = tie(
            input_blocks, quarter_one, quarter_two, extra, out_more, arrived_x
        )

        moved = [across(out_more), core(out_more)]
        from_one = [shift(quarter_one, k) for k in range(1, ring_size)]
        input_gradient = run_place(mine, input_blocks, FULL)
        grads = [
            total_of([own_sum[0], arrived_y[0], arrived_x[0]]),
            total_of([own_sum[1], arrived_y[2], arrived_x[1]]),
            total_of([own_sum[2], arrived_y[1], arrived_x[2]]),
        ]
        unturned = lambda v: v.reshape(local, hidden, width).transpose(0, 2, 1)
        grad_gate, grad_up, grad_down = unturned(grads[0]), unturned(grads[1]), grads[2]
        moved, from_one, input_gradient, grad_gate, grad_up, grad_down = tie(
            moved, from_one, input_gradient, grad_gate, grad_up, grad_down
        )
        one = jnp.concatenate([quarter_one] + from_one)
        one, quarter_two = tie(one, quarter_two)

        from_two = [shift(quarter_two, k) for k in range(1, ring_size)]
        one_other, out_3 = pair(one), core(moved[0])
        from_two, one_other, out_3 = tie(from_two, one_other, out_3)
        two = jnp.concatenate([quarter_two] + from_two)

        output = run_place(mine, [out_own, moved[1], moved[0], out_3], LOW)
        sums = total_of(
            [extra] + [v[rows : rows + count] for v in (moved[1], moved[0], out_3)]
        )
        two_other, output, sums = tie(pair(two), output, sums)
        finished = run_finish(
            mine, None, size, [(one, one_other), (two, two_other)], ring_size
        )
    else:
        g = spread(sent)
        h = ring_gather(hidden_second)
        near, far = gather_weights([gate, up, down])
        places = [0] * (2 * len(near)) + [1] * (2 * len(far))
        weights = with_cores(near + far)
        step = max(1, min(ring_size, 1024 // rows))
        y_parts, dh_parts, dgb_parts, hids, plan = [], [], [], [], [[] for _ in weights]
        for i in range(0, ring_size, step):
            at = slice(i, i + step)
            y, dh, dgb, hid = experts(h[at], g[at], weights, places)
            y_parts, dh_parts, dgb_parts = y_parts + y, dh_parts + dh, dgb_parts + dgb
            for s in range(len(weights)):
                base = len(weights) * first + s * wide
                plan[s].append((len(hids), s * first, base, i * rows, step * rows))
            hids.append(hid)
        grad_parts = []
        for i in range(0, len(weights), 4):
            chips = run_weights(
                h, g, hids, [plan[i], plan[i + 2], plan[i + 1], plan[i + 3]], wide
            )
            for kept, other in ((chips[0], core(chips[1])), (chips[2], core(chips[3]))):
                grad_parts.append(
                    run_adds([(piece, other, j * wide) for j, piece in enumerate(kept)])
                )
        grad_gate, grad_up, grad_down = scatter_weights(grad_parts)
        unturned = lambda v: v.reshape(local, hidden, width).transpose(0, 2, 1)
        grad_gate, grad_up = unturned(grad_gate), unturned(grad_up)
        running = low(full(ring_partial(dh_parts)))
        d_mid, d_a, small = token_gradients(running, dh_parts[0])
        da = tensor_blocks(d_a)
        backs = [back(i, da, False) for i in range(groups)]
        d_keep, d_send, grad_gain_first = first_gradients([d for d, _ in backs])
        d_parts = [
            (d_send if r % 2 else d_keep)[r // 2 * rows : (r // 2 + 1) * rows]
            for r in range(tensor_count)
        ]
        d_first = parts_sum(d_parts)
        input_blocks = tensor_blocks(input_rows(d_first, d_mid))
        input_gradient = run_place(mine, input_blocks, FULL)
        output = run_place(
            mine, tensor_blocks(low(residual_mid + ring_sum(y_parts))), LOW
        )
        finished = run_finish(
            mine, [lax.psum(square, "expert") for _, square in backs], size
        )
        sums = sum_everywhere(jnp.concatenate([small, grad_gain_first]))

    grad_query, grad_key, grad_value, grad_output = finished
    return (
        output,
        input_gradient,
        sums[-1],
        grad_query,
        grad_key,
        grad_value,
        grad_output,
        sums[0],
        sums[1:-1].T,
        grad_gate,
        grad_up,
        grad_down.reshape(local, hidden, width),
    )


def solution(mesh):
    in_specs = (
        P("expert", None),
        P("expert", None),
        P("expert", None),
        P("expert", None),
        P("expert", None),
        P(),
        P(None, "tensor"),
        P(None, "tensor"),
        P(None, "tensor"),
        P("tensor", None),
        P(),
        P(),
        P("expert", None, "tensor"),
        P("expert", None, "tensor"),
        P("expert", "tensor", None),
    )
    out_specs = (
        P("expert", None),
        P("expert", None),
        P(),
        P(None, "tensor"),
        P(None, "tensor"),
        P(None, "tensor"),
        P("tensor", None),
        P(),
        P(),
        P("expert", None, "tensor"),
        P("expert", None, "tensor"),
        P("expert", "tensor", None),
    )
    return jax.shard_map(shards, mesh=mesh, in_specs=in_specs, out_specs=out_specs, check_vma=False)
```
